128 devices in a mesh: shard: 16 (over y_lo, x, core), ctx: 4 (over z), tp: 2 (over y_hi).
Axes of the slice: x: 4, y: 4 (y_hi: 2, y_lo: 2; y = y_hi * 2 + y_lo), z: 4, core: 2. Of those that a mesh axis runs over, the one named last changes fastest.
Arguments:
- tokens: bfloat16 [12288, 2048], P(('shard', 'ctx')), may hold values from -6 to 6
- parents: int32 [16, 16], P('shard'), may hold values from -1 to 14, as said below
- gain_attn: bfloat16 [2048], P('shard'), may hold values from 0.5 to 1.5
- w_query: bfloat16 [2048, 2048], P('shard', 'tp'), may hold values from -0.125 to 0.125
- key_weight: bfloat16 [2048, 1024], P('shard', 'tp'), may hold values from -0.125 to 0.125
- value_weight: bfloat16 [2048, 1024], P('shard', 'tp'), may hold values from -0.125 to 0.125
- w_out: bfloat16 [2048, 2048], P('tp', 'shard'), may hold values from -0.5 to 0.5
- gain_ffn: bfloat16 [2048], P('shard'), may hold values from 0.5 to 1.5
- w_gate: bfloat16 [2048, 8192], P('shard', 'tp'), may hold values from -0.125 to 0.125
- w_up: bfloat16 [2048, 8192], P('shard', 'tp'), may hold values from -0.125 to 0.125
- w_down: bfloat16 [8192, 2048], P('tp', 'shard'), may hold values from -0.0625 to 0.0625
- cotangent: bfloat16 [12288, 2048], P(('shard', 'ctx')), may hold values from -6 to 6
Outputs:
- output: bfloat16 [12288, 2048], P(('shard', 'ctx'))
- grad_tokens: bfloat16 [12288, 2048], P(('shard', 'ctx'))
- grad_gain_attn: float32 [2048], P('shard')
- grad_query: float32 [2048, 2048], P('shard', 'tp')
- grad_key: float32 [2048, 1024], P('shard', 'tp')
- grad_value: float32 [2048, 1024], P('shard', 'tp')
- grad_out: float32 [2048, 2048], P('tp', 'shard')
- grad_gain_ffn: float32 [2048], P('shard')
- grad_gate: float32 [2048, 8192], P('shard', 'tp')
- grad_up: float32 [2048, 8192], P('shard', 'tp')
- grad_down: float32 [8192, 2048], P('tp', 'shard')
The draws below stay inside these ranges and needn't reach their ends.
Inputs may be any that keep to these rules, and one draw needn't show every extreme that they name: parents[t, 0] = -1. For s >= 1, parents[t, s] lies in [b, s - 1], where b = -1 if s < 4, else 4 * (s // 4 - 1); -1 marks a root. parents[t, 15] = 14 in every tree.
All inputs are finite; a program needn't handle non-finite values.
Results may differ from the reference program's by a relative error of at most 0.025.
Values may be sent and summed in bfloat16 or wider, within the bound.
A program may use at most 256 MiB of HBM per device.

```python
import math
import jax
import jax.numpy as jnp
from jax import lax

MODEL_WIDTH = 2048
QUERY_HEADS = 8
KEY_VALUE_HEADS = 4
HEAD_SIZE = 256
FF = 8192
SEG = 48
SEGS_DEV = 4
NSEG = 16
TREE_COUNT = 16
TOKENS = 12288


def draw_parents(key, part):
    key = jax.random.fold_in(key, 7)
    index = jnp.arange(NSEG)
    block = index // SEGS_DEV
    lowest = jnp.where(block == 0, -1, (block - 1) * SEGS_DEV)
    drawn = jax.random.randint(key, (TREE_COUNT, NSEG), lowest[None, :], index[None, :])
    drawn = jnp.where(index[None, :] == NSEG - 1, NSEG - 2, drawn)
    return drawn.astype(jnp.int32)


def steps_of(own_key, extent, shards, low, top_value):
    def one(dim, shards_of):
        heights = jax.random.uniform(jax.random.fold_in(jax.random.fold_in(own_key, 6), dim), (shards_of,), jnp.float32, low / len(shards), top_value / len(shards))
        return jnp.repeat(jnp.exp(heights), extent[dim] // shards_of).reshape((-1,) + (1,) * (len(extent) - dim - 1))

    factor_of = one(*shards[0])
    for cut in shards[1:]:
        factor_of = factor_of * one(*cut)
    return factor_of


def scatter_about(key, shape, deviation, most, cuts=(), kind=jnp.bfloat16):
    factor_of = steps_of(key, shape, cuts, -0.22, 0.18) if cuts else 1.0
    values = jax.random.normal(key, shape, jnp.float32) * deviation * factor_of
    return jnp.minimum(jnp.maximum(values, -most), most).astype(kind)


def setup_inputs(seed: int = 0) -> dict:
    seeds = jax.random.split(jax.random.key(seed), 13)
    tokens = scatter_about(seeds[0], (TOKENS, MODEL_WIDTH), 1.0, 6.0, ((0, 64),))
    parents = draw_parents(jax.random.fold_in(seeds[12], 71), 0)
    gain_attn = jnp.clip(1.0 + 0.1 * jax.random.normal(seeds[2], (MODEL_WIDTH,), jnp.float32), 0.5, 1.5).astype(jnp.bfloat16)
    w_query = scatter_about(seeds[3], (MODEL_WIDTH, QUERY_HEADS * HEAD_SIZE), MODEL_WIDTH ** -0.5, 0.125, ((0, 16), (1, 2)))
    key_weight = scatter_about(seeds[4], (MODEL_WIDTH, KEY_VALUE_HEADS * HEAD_SIZE), MODEL_WIDTH ** -0.5, 0.125, ((0, 16), (1, 2)))
    value_weight = scatter_about(seeds[5], (MODEL_WIDTH, KEY_VALUE_HEADS * HEAD_SIZE), MODEL_WIDTH ** -0.5, 0.125, ((0, 16), (1, 2)))
    w_out = scatter_about(seeds[6], (QUERY_HEADS * HEAD_SIZE, MODEL_WIDTH), (QUERY_HEADS * HEAD_SIZE // 16) ** -0.5, 0.5, ((0, 2), (1, 16)))
    gain_ffn = jnp.clip(1.0 + 0.1 * jax.random.normal(seeds[7], (MODEL_WIDTH,), jnp.float32), 0.5, 1.5).astype(jnp.bfloat16)
    w_gate = scatter_about(seeds[8], (MODEL_WIDTH, FF), MODEL_WIDTH ** -0.5, 0.125, ((0, 16), (1, 2)))
    w_up = scatter_about(seeds[9], (MODEL_WIDTH, FF), MODEL_WIDTH ** -0.5, 0.125, ((0, 16), (1, 2)))
    w_down = scatter_about(seeds[10], (FF, MODEL_WIDTH), FF ** -0.5, 0.0625, ((0, 2), (1, 16)))
    cotangent = scatter_about(seeds[11], (TOKENS, MODEL_WIDTH), 1.0, 6.0, ((0, 64),))
    return dict(tokens=tokens, parents=parents, gain_attn=gain_attn, w_query=w_query, key_weight=key_weight, value_weight=value_weight, w_out=w_out, gain_ffn=gain_ffn, w_gate=w_gate, w_up=w_up, w_down=w_down, cotangent=cotangent)


EPSILON = 1e-06
THETA = 1000042.0
NEGATIVE = -1e+30
HIGHEST = lax.Precision.HIGHEST

@jax.custom_vjp
def lower_precision(v):
    return lax.optimization_barrier(v.astype(jnp.bfloat16)).astype(jnp.float32)

@jax.custom_vjp
def lower_backward(v):
    return v

def low_keep(v):
    return (lower_precision(v), None)

def low_pass(kept, grad):
    return (grad,)

def back_keep(v):
    return (v, None)

def back_low(kept, grad):
    return (lower_precision(grad),)
lower_precision.defvjp(low_keep, low_pass)
lower_backward.defvjp(back_keep, back_low)

def matrix_product(left, right):
    return jnp.dot(left, right, precision=HIGHEST, preferred_element_type=jnp.float32)

def rms_norm(value_rows, weights):
    return value_rows * lax.rsqrt(lax.optimization_barrier(jnp.mean(value_rows * value_rows, -1, keepdims=True)) + EPSILON) * weights

def rotate(value_rows, cosine, sine):
    middle = value_rows.shape[-1] // 2
    first = value_rows[..., :middle]
    second = value_rows[..., middle:]
    return jnp.concatenate([first * cosine - second * sine, second * cosine + first * sine], -1)

def ancestry(parents):
    index = jnp.arange(NSEG)
    links = (parents[:, :, None] == index[None, None, :]).astype(jnp.float32)
    identity = jnp.broadcast_to(jnp.eye(NSEG, dtype=jnp.float32), links.shape)
    reached = identity
    for sweep in range(NSEG):
        reached = jnp.maximum(identity, jnp.einsum('tsu,tuv->tsv', links, reached, precision=HIGHEST))
    return reached

def attend_heads(pieces):
    query_rows, key_rows, value_rows, allowed_mask = pieces
    key_rows = jnp.repeat(key_rows, QUERY_HEADS // KEY_VALUE_HEADS, axis=1)
    value_rows = jnp.repeat(value_rows, QUERY_HEADS // KEY_VALUE_HEADS, axis=1)
    raw = lower_backward(jnp.einsum('qhd,khd->hqk', query_rows, key_rows, precision=HIGHEST))
    scores = jnp.where(allowed_mask[None], raw * (1.0 / math.sqrt(HEAD_SIZE)), NEGATIVE)
    probs = lower_precision(jax.nn.softmax(scores, axis=-1))
    return jnp.einsum('hqk,khd->qhd', probs, value_rows, precision=HIGHEST)

def reference(tokens, parents, gain_attn, w_query, key_weight, value_weight, w_out, gain_ffn, w_gate, w_up, w_down, cotangent):
    reached = ancestry(parents)
    depth = lax.optimization_barrier(jnp.sum(reached, -1)) - 1.0
    length_total = NSEG * SEG
    within = jnp.arange(length_total)
    segment = within // SEG
    offset = within % SEG
    position = depth[:, segment] * SEG + offset.astype(jnp.float32)[None, :]
    half_width = HEAD_SIZE // 2
    frequency = jnp.power(THETA, -(jnp.arange(half_width, dtype=jnp.float32) * 2.0) / HEAD_SIZE)
    angles = position.reshape(-1)[:, None] * frequency[None, :]
    cosine = jnp.cos(angles)[:, None, :]
    sine = jnp.sin(angles)[:, None, :]
    linked = reached[:, segment][:, :, segment] > 0.5
    causal = (segment[:, None] != segment[None, :]) | (offset[None, :] <= offset[:, None])
    allowed_mask = linked & causal[None]
    total_sum = tokens.shape[0]

    def forward(inputs, gain_one, query_w, key_matrix, value_matrix, out_w, gain_two, gate_w, up_w, down_w):
        normed_input = lower_precision(rms_norm(inputs, gain_one))
        query_rows = lower_backward(matrix_product(normed_input, query_w)).reshape(total_sum, QUERY_HEADS, HEAD_SIZE)
        query_rows = lower_precision(rotate(query_rows, cosine, sine))
        key_rows = lower_backward(matrix_product(normed_input, key_matrix)).reshape(total_sum, KEY_VALUE_HEADS, HEAD_SIZE)
        key_rows = lower_precision(rotate(key_rows, cosine, sine))
        value_rows = lower_precision(lower_backward(matrix_product(normed_input, value_matrix))).reshape(total_sum, KEY_VALUE_HEADS, HEAD_SIZE)
        mixed_output = lax.map(jax.checkpoint(attend_heads), (query_rows.reshape(TREE_COUNT, length_total, QUERY_HEADS, HEAD_SIZE), key_rows.reshape(TREE_COUNT, length_total, KEY_VALUE_HEADS, HEAD_SIZE), value_rows.reshape(TREE_COUNT, length_total, KEY_VALUE_HEADS, HEAD_SIZE), allowed_mask))
        attended = lower_precision(lower_backward(mixed_output.reshape(total_sum, QUERY_HEADS * HEAD_SIZE)))
        hidden_state = inputs + lower_backward(matrix_product(attended, out_w))
        second = lower_precision(rms_norm(hidden_state, gain_two))
        gating = lower_backward(matrix_product(second, gate_w))
        upward = lower_backward(matrix_product(second, up_w))
        inner = lower_precision(jax.nn.silu(gating) * upward)
        return hidden_state + lower_backward(matrix_product(inner, down_w))
    floats = tuple((argument.astype(jnp.float32) for argument in (tokens, gain_attn, w_query, key_weight, value_weight, w_out, gain_ffn, w_gate, w_up, w_down)))
    result, pullback = jax.vjp(forward, *floats)
    grads = pullback(cotangent.astype(jnp.float32))
    return (result.astype(jnp.bfloat16), grads[0].astype(jnp.bfloat16), grads[1], grads[2], grads[3], grads[4], grads[5], grads[6], grads[7], grads[8], grads[9])
```

```python
import math

import jax
import jax.numpy as jnp
from jax import lax
from jax.sharding import PartitionSpec as P

HEAD = 256
SEG = 48
SEGS_DEV = 4
NSEG = 16
ROWS = 192
TREE = 768
WIDTH = 2048
FFD = 1024

EPSILON = 1e-06
THETA = 1000042.0
NEGATIVE = -1e30
HIGHEST = lax.Precision.HIGHEST
F32 = jnp.float32
BF16 = jnp.bfloat16


def contract(left, right, left_axis, right_axis):
    return lax.dot_general(
        left, right, (((left_axis,), (right_axis,)), ((), ())), preferred_element_type=F32
    )


def norm_factor(rows):
    return lax.rsqrt(jnp.mean(rows * rows, -1, keepdims=True) + EPSILON)


def norm_backward(rows, factor, weights, upstream):
    weighted = upstream * weights
    inner = jnp.mean(weighted * rows, -1, keepdims=True)
    return (
        factor * weighted - rows * (factor * factor * factor) * inner,
        jnp.sum(upstream * rows * factor, 0),
    )


def rotate(rows, cosine, sine):
    first = rows[:, : HEAD // 2]
    second = rows[:, HEAD // 2 :]
    return jnp.concatenate([first * cosine - second * sine, second * cosine + first * sine], -1)


def tables(parent_row):
    index = jnp.arange(NSEG)
    links = (parent_row[:, None] == index[None, :]).astype(F32)
    reached = links + jnp.eye(NSEG, dtype=F32)
    for _ in range(4):
        reached = jnp.minimum(jnp.dot(reached, reached, precision=HIGHEST), 1.0)
    depth = jnp.sum(reached, 1) - 1.0
    token = jnp.arange(TREE)
    segment = token // SEG
    offset = token % SEG
    onehot = (segment[:, None] == index[None, :]).astype(F32)
    position = jnp.dot(onehot, depth, precision=HIGHEST) * SEG + offset.astype(F32)
    half = HEAD // 2
    frequency = jnp.power(THETA, -(jnp.arange(half, dtype=F32) * 2.0) / HEAD)
    angles = position[:, None] * frequency[None, :]
    linked = contract(jnp.dot(onehot, reached, precision=HIGHEST), onehot, 1, 1) > 0.5
    allowed = linked & (
        (segment[:, None] != segment[None, :]) | (offset[None, :] <= offset[:, None])
    )
    return jnp.cos(angles), jnp.sin(angles), allowed


def local(
    tokens,
    parents,
    gain_attn,
    w_query,
    key_weight,
    value_weight,
    w_out,
    gain_ffn,
    w_gate,
    w_up,
    w_down,
    cotangent,
):
    z = lax.axis_index("ctx")
    t = lax.axis_index("tp")

    def cols(w, at, size):
        return lax.dynamic_slice_in_dim(w, at, size, 1)

    def rows(w, at, size):
        return lax.dynamic_slice_in_dim(w, at, size, 0)

    gains = jnp.pad(jnp.stack([gain_attn, gain_ffn], 1), ((0, 0), (0, 126)))
    attn_mine = jnp.concatenate(
        [
            cols(w_query, z * HEAD, HEAD),
            cols(key_weight, (z // 2) * HEAD, HEAD),
            cols(value_weight, (z // 2) * HEAD, HEAD),
            rows(w_out, z * HEAD, HEAD).T,
            gains,
        ],
        1,
    )
    ffn_mine = jnp.concatenate(
        [cols(w_gate, z * FFD, FFD), cols(w_up, z * FFD, FFD), rows(w_down, z * FFD, FFD).T], 1
    )
    attn_w = lax.all_gather(attn_mine, "shard", axis=0, tiled=True)
    ffn_w = lax.all_gather(ffn_mine, "shard", axis=0, tiled=True)
    x_full = lax.all_gather(tokens, "ctx", axis=0, tiled=True)
    c_full = lax.all_gather(cotangent, "ctx", axis=0, tiled=True)
    gain_one = attn_w[:, 4 * HEAD].astype(F32)
    gain_two = attn_w[:, 4 * HEAD + 1].astype(F32)
    cosine, sine, allowed = tables(parents[0])

    x_f = x_full.astype(F32)
    n1 = (x_f * norm_factor(x_f) * gain_one).astype(BF16)
    wq, wk, wv, wo = (attn_w[:, i * HEAD : (i + 1) * HEAD] for i in range(4))
    q = rotate(contract(n1, wq, 1, 0), cosine, sine).astype(BF16)
    k = rotate(contract(n1, wk, 1, 0), cosine, sine).astype(BF16)
    v = contract(n1, wv, 1, 0).astype(BF16)
    scores = jnp.where(allowed, contract(q, k, 1, 1) * (1.0 / math.sqrt(HEAD)), NEGATIVE)
    highest = jnp.max(scores, -1, keepdims=True)
    weight = jnp.exp(scores - highest)
    p = weight / jnp.sum(weight, -1, keepdims=True)
    pl_low = p.astype(BF16)
    a = contract(pl_low, v, 1, 0).astype(BF16)
    half_rows = ROWS // 2

    def own_half(rows_):
        return lax.dynamic_slice_in_dim(rows_, t * half_rows, half_rows, 0)

    def scatter(part):
        return lax.psum_scatter(
            part.astype(BF16), ("ctx", "tp"), scatter_dimension=0, tiled=True
        ).astype(F32)

    x_own = own_half(tokens).astype(F32)
    h = x_own + scatter(contract(a, wo, 1, 1))
    r2 = norm_factor(h)
    n2_own = (h * r2 * gain_two).astype(BF16)
    n2 = lax.all_gather(n2_own, ("ctx", "tp"), axis=0, tiled=True)
    wg, wu, wd = (ffn_w[:, i * FFD : (i + 1) * FFD] for i in range(3))
    g = contract(n2, wg, 1, 0)
    u = contract(n2, wu, 1, 0)
    sg = jax.nn.sigmoid(g)
    swish = g * sg
    hid = (swish * u).astype(BF16)
    d_hid = contract(c_full, wd, 1, 0)
    dg = (d_hid * u * sg * (1.0 + g * (1.0 - sg))).astype(BF16)
    du = (d_hid * swish).astype(BF16)
    dn2 = scatter(contract(dg, wg, 1, 1) + contract(du, wu, 1, 1))
    out_own = (h + scatter(contract(hid, wd, 1, 1))).astype(BF16)
    grad_ffn = jnp.concatenate(
        [
            contract(n2, dg, 0, 0).astype(BF16),
            contract(n2, du, 0, 0).astype(BF16),
            contract(c_full, hid, 0, 0).astype(BF16),
        ],
        1,
    )
    grad_ffn = lax.psum_scatter(grad_ffn, "shard", scatter_dimension=0, tiled=True)
    back_two, term_gain_two = norm_backward(h, r2, gain_two, dn2)
    dh = own_half(cotangent).astype(F32) + back_two
    dhl = lax.all_gather(dh.astype(BF16), ("ctx", "tp"), axis=0, tiled=True)
    da = contract(dhl, wo, 1, 0).astype(BF16)
    dp = contract(da, v, 1, 1)
    ds = p * (dp - jnp.sum(p * dp, -1, keepdims=True))
    draw = (ds * (1.0 / math.sqrt(HEAD))).astype(BF16)
    dq = rotate(contract(draw, k, 1, 0), cosine, -sine).astype(BF16)
    dk = rotate(contract(draw, q, 0, 0), cosine, -sine).astype(BF16)
    dv = contract(pl_low, da, 0, 0).astype(BF16)
    dn1 = scatter(contract(dq, wq, 1, 1) + contract(dk, wk, 1, 1) + contract(dv, wv, 1, 1))
    r1_own = norm_factor(x_own)
    back_one, term_gain_one = norm_backward(x_own, r1_own, gain_one, dn1)
    dtok_own = (dh + back_one).astype(BF16)
    both = lax.all_gather(jnp.concatenate([out_own, dtok_own], 1), "tp", axis=0, tiled=True)
    gain_terms = lax.psum(
        jnp.stack([term_gain_one, term_gain_two], 1), "tp"
    )
    grad_attn = jnp.concatenate(
        [
            contract(n1, dq, 0, 0).astype(BF16),
            contract(n1, dk, 0, 0).astype(BF16),
            contract(n1, dv, 0, 0).astype(BF16),
            contract(dhl, a, 0, 0).astype(BF16),
            jnp.pad(gain_terms, ((0, 0), (0, 126))).astype(BF16),
        ],
        1,
    )
    grad_attn = lax.psum_scatter(grad_attn, "shard", scatter_dimension=0, tiled=True)
    ffn_all = lax.all_gather(grad_ffn, "ctx", axis=0)
    attn_all = lax.all_gather(grad_attn, "ctx", axis=0).astype(F32)

    def wide(parts):
        return jnp.concatenate([parts[i] for i in range(parts.shape[0])], 1).astype(F32)

    grad_query = wide(attn_all[:, :, :HEAD])
    kv = attn_all[0::2, :, HEAD : 3 * HEAD] + attn_all[1::2, :, HEAD : 3 * HEAD]
    grad_key = wide(kv[:, :, :HEAD])
    grad_value = wide(kv[:, :, HEAD:])
    grad_out = wide(attn_all[:, :, 3 * HEAD : 4 * HEAD]).T
    gain_sums = jnp.sum(attn_all[:, :, 4 * HEAD :], 0)
    grad_gate = wide(ffn_all[:, :, :FFD])
    grad_up = wide(ffn_all[:, :, FFD : 2 * FFD])
    grad_down = wide(ffn_all[:, :, 2 * FFD :]).T
    return (
        both[:, :WIDTH],
        both[:, WIDTH:],
        gain_sums[:, 0],
        grad_query,
        grad_key,
        grad_value,
        grad_out,
        gain_sums[:, 1],
        grad_gate,
        grad_up,
        grad_down,
    )


def solution(mesh):
    rows = P(("shard", "ctx"), None)
    weight = P("shard", "tp")
    turned = P("tp", "shard")
    vector = P("shard")
    return jax.shard_map(
        local,
        mesh=mesh,
        in_specs=(
            rows, P("shard", None), vector, weight, weight, weight, turned, vector,
            weight, weight, turned, rows,
        ),
        out_specs=(
            rows, rows, vector, weight, weight, weight, turned, vector, weight, weight, turned,
        ),
        check_vma=False,
    )
```

```python
import functools
import math

import jax
import jax.numpy as jnp
from jax import lax
from jax.experimental import pallas as pl
from jax.experimental.pallas import tpu as pltpu
from jax.sharding import PartitionSpec as P

HEAD = 256
HALF = HEAD // 2
SEG = 48
NSEG = 16
ROWS = 192
TREE = 768
WIDTH = 2048
FFD = 1024
BLOCK = 128
GROWS = 32

EPSILON = 1e-06
THETA = 1000042.0
NEGATIVE = -1e30
HIGHEST = lax.Precision.HIGHEST
F32 = jnp.float32
BF16 = jnp.bfloat16
MESH = pl.DeviceIdType.MESH
ANY = pl.BlockSpec(memory_space=pl.ANY)
VM = pl.BlockSpec(memory_space=pltpu.VMEM)


def nn(left, right):
    return jnp.dot(left, right, preferred_element_type=F32)


def nt(left, right):
    return lax.dot_general(left, right, (((1,), (1,)), ((), ())), preferred_element_type=F32)


def tn(left, right):
    return lax.dot_general(left, right, (((0,), (0,)), ((), ())), preferred_element_type=F32)


def ring(value, step):
    return lax.rem(value + step, 4)


class Place:
    def __init__(self):
        shard = lax.axis_index("shard")
        self.shard = shard
        self.y = shard // 8
        self.x = lax.rem(shard // 2, 4)
        self.c = lax.rem(shard, 2)
        self.z = lax.axis_index("ctx")
        self.t = lax.axis_index("tp")

    def block(self, dy=0, dx=0, dc=0):
        y = 1 - self.y if dy else self.y
        c = 1 - self.c if dc else self.c
        return y * 8 + ring(self.x, dx) * 2 + c

    def to(self, dy=0, dx=0, dc=0, dz=0, dt=0):
        t = 1 - self.t if dt else self.t
        return (self.block(dy, dx, dc), ring(self.z, dz), t)


ALL_NEAR = ("y", "x+", "x-", "c", "z+", "z-", "t")
NEAR = {
    "y": dict(dy=1), "x+": dict(dx=1), "x-": dict(dx=3), "c": dict(dc=1),
    "z+": dict(dz=1), "z-": dict(dz=3), "t": dict(dt=1),
}


class Net:
    def __init__(self, here, send, recv, local):
        self.here, self.send, self.recv, self.local = here, send, recv, local
        self.sent, self.count, self.copies = [], 0, 0

    def greet(self, names):
        barrier = pltpu.get_barrier_semaphore()
        for name in names:
            pl.semaphore_signal(
                barrier, inc=1, device_id=self.here.to(**NEAR[name]), device_id_type=MESH
            )
        pl.semaphore_wait(barrier, len(names))

    def push(self, src, dst, name):
        index = self.count
        self.count += 1
        copy = pltpu.make_async_remote_copy(
            src_ref=src,
            dst_ref=dst,
            send_sem=self.send.at[index],
            recv_sem=self.recv.at[index],
            device_id=self.here.to(**NEAR[name]),
            device_id_type=MESH,
        )
        copy.start()
        self.sent.append(copy)
        return copy

    def copy(self, src, dst):
        index = self.copies
        self.copies += 1
        copy = pltpu.make_async_copy(src, dst, self.local.at[index])
        copy.start()
        return copy

    def drain(self):
        for copy in self.sent:
            copy.wait_send()


def near_sems(remote, local):
    return [
        pltpu.SemaphoreType.DMA((remote,)),
        pltpu.SemaphoreType.DMA((remote,)),
        pltpu.SemaphoreType.DMA((local,)),
    ]


def chunk(index):
    return pl.ds(pl.multiple_of(index * ROWS, ROWS), ROWS)


class RingGather:
    def __init__(self, net, own, full):
        self.net, self.full, self.rows = net, full, own.shape[0]
        half = self.rows // 2
        one, two = own.at[pl.ds(0, half)], own.at[pl.ds(half, half)]
        self.a1 = net.push(one, self.half(0, 0), "z+")
        self.b2 = net.push(two, self.half(0, 1), "z-")
        self.a2 = net.push(two, self.half(0, 1), "z+")
        self.b1 = net.push(one, self.half(0, 0), "z-")

    def half(self, step, part):
        half = self.rows // 2
        start = ring(self.net.here.z, step) * self.rows + part * half
        return self.full.at[pl.ds(pl.multiple_of(start, half), half)]

    def at(self, step):
        return span(ring(self.net.here.z, step), self.rows)

    def forward(self):
        self.a1.wait_recv()
        self.f1 = self.net.push(self.half(3, 0), self.half(3, 0), "z+")
        self.b2.wait_recv()
        self.f2 = self.net.push(self.half(1, 1), self.half(1, 1), "z-")

    def left(self):
        self.a2.wait_recv()

    def right(self):
        self.b1.wait_recv()

    def far(self):
        self.f1.wait_recv()
        self.f2.wait_recv()


class RingSum:
    def __init__(self, net, part, passed, plus, minus, mine, other, subs):
        self.net, self.part, self.passed = net, part, passed
        self.plus, self.minus, self.mine, self.other = plus, minus, mine, other
        width = part.shape[1] // subs
        self.cols = [
            (pl.ds(i * width, width // 2), pl.ds(i * width + width // 2, width // 2))
            for i in range(subs)
        ]
        self.subs = subs
        self.width = width
        self.e1, self.e2, self.r1, self.r2 = {}, {}, {}, {}
        self.s1, self.s2, self.t = {}, {}, {}

    def at(self, step):
        return chunk(ring(self.net.here.z, step))

    def far(self, i):
        one, two = self.cols[i]
        self.e1[i] = self.net.push(self.part.at[self.at(2), one], self.passed.at[:, one], "z+")
        self.e2[i] = self.net.push(self.part.at[self.at(2), two], self.passed.at[:, two], "z-")

    def raw(self, i):
        one, two = self.cols[i]
        self.r1[i] = self.net.push(self.part.at[self.at(1), two], self.plus.at[:, two], "z+")
        self.r2[i] = self.net.push(self.part.at[self.at(3), one], self.minus.at[:, one], "z-")

    def add(self, i):
        one, two = self.cols[i]
        part, passed = self.part, self.passed
        self.e1[i].wait_recv()
        part[self.at(1), one] = (
            part[self.at(1), one].astype(F32) + passed[:, one].astype(F32)
        ).astype(BF16)
        self.s1[i] = self.net.push(part.at[self.at(1), one], self.plus.at[:, one], "z+")
        self.e2[i].wait_recv()
        part[self.at(3), two] = (
            part[self.at(3), two].astype(F32) + passed[:, two].astype(F32)
        ).astype(BF16)
        self.s2[i] = self.net.push(part.at[self.at(3), two], self.minus.at[:, two], "z-")

    def cross(self, i):
        for copy in (self.r1[i], self.r2[i], self.s1[i], self.s2[i]):
            copy.wait_recv()
        both = pl.ds(i * self.width, self.width)
        self.mine[:, both] = (
            self.part[self.at(0), both].astype(F32)
            + self.plus[:, both].astype(F32)
            + self.minus[:, both].astype(F32)
        ).astype(BF16)
        self.t[i] = self.net.push(self.mine.at[:, both], self.other.at[:, both], "t")

    def arrive(self, i):
        self.t[i].wait_recv()


def ring_sum_scratch():
    return [pltpu.VMEM((ROWS, WIDTH), BF16) for _ in range(5)]


class ShardGather:
    def __init__(self, net, own, full, rows):
        self.net, self.own, self.full, self.rows = net, own, full, rows
        self.to_sibling = []

    def at(self, part=None, **step):
        block = self.net.here.block(**step)
        if part is None:
            return self.full.at[pl.ds(pl.multiple_of(block * self.rows, self.rows), self.rows)]
        half = self.rows // 2
        start = block * self.rows + part * half
        return self.full.at[pl.ds(pl.multiple_of(start, half), half)]

    def relay(self, name, part=None, **step):
        ref = self.at(part, **step)
        return self.net.push(ref, ref, name)

    def sibling(self, part=None, **step):
        self.to_sibling.append(self.relay("c", part, **step))

    def begin(self):
        self.y0, self.p0, self.m0, c0 = (
            self.net.push(self.own, self.at(), name) for name in ("y", "x+", "x-", "c")
        )
        self.to_sibling.append(c0)

    def across(self):
        self.y0.wait_recv()
        self.p1 = self.relay("x+", dy=1)
        self.m1 = self.relay("x-", dy=1)
        self.sibling(dy=1)

    def near(self, dy):
        plus, minus = (self.p1, self.m1) if dy else (self.p0, self.m0)
        plus.wait_recv()
        fp = self.relay("x+", 0, dy=dy, dx=3)
        self.sibling(dy=dy, dx=3)
        minus.wait_recv()
        fm = self.relay("x-", 1, dy=dy, dx=1)
        self.sibling(dy=dy, dx=1)
        if dy:
            self.fp1, self.fm1 = fp, fm
        else:
            self.fp0, self.fm0 = fp, fm

    def far(self, dy):
        plus, minus = (self.fp1, self.fm1) if dy else (self.fp0, self.fm0)
        plus.wait_recv()
        self.sibling(0, dy=dy, dx=2)
        minus.wait_recv()
        self.sibling(1, dy=dy, dx=2)

    def finish(self):
        for copy in self.to_sibling:
            copy.wait_recv()


class ShardSum:
    def __init__(self, net, source, rows, held, gift, passed, plus, minus, last):
        self.net, self.source, self.rows = net, source, rows
        self.held, self.gift, self.passed = held, gift, passed
        self.plus, self.minus, self.last = plus, minus, last
        self.gifts, self.loads = {}, {}
        for dx in (2, 1, 3, 0):
            for dy in (1, 0):
                self.gifts[dx, dy] = net.push(
                    self.block(dx, dy, 1), gift.at[2 * dx + dy], "c"
                )
                self.loads[dx, dy] = net.copy(self.block(dx, dy, 0), held.at[2 * dx + dy])
        self.e1, self.e2, self.raw, self.sums = {}, {}, {}, {}

    def block(self, dx, dy, dc):
        return self.source.at[span(self.net.here.block(dx=dx, dy=dy, dc=dc), self.rows)]

    def pair(self, dx, dy):
        slot = 2 * dx + dy
        self.gifts[dx, dy].wait_recv()
        self.loads[dx, dy].wait()
        self.held[slot] = self.held[slot] + self.gift[slot]
        half = self.rows // 2
        one, two = pl.ds(0, half), pl.ds(half, half)
        held = self.held
        if dx == 2:
            self.e1[dy] = self.net.push(held.at[slot, one], self.passed.at[dy, one], "x+")
            self.e2[dy] = self.net.push(held.at[slot, two], self.passed.at[dy, two], "x-")
        if dx == 1:
            self.raw[1, dy] = self.net.push(held.at[slot, two], self.plus.at[dy, two], "x+")
        if dx == 3:
            self.raw[3, dy] = self.net.push(held.at[slot, one], self.minus.at[dy, one], "x-")

    def pass_on(self, dy):
        half = self.rows // 2
        one, two = pl.ds(0, half), pl.ds(half, half)
        held, passed = self.held, self.passed
        self.e1[dy].wait_recv()
        slot = 2 + dy
        held[slot, one] = held[slot, one] + passed[dy, one]
        self.sums[1, dy] = self.net.push(held.at[slot, one], self.plus.at[dy, one], "x+")
        self.e2[dy].wait_recv()
        slot = 6 + dy
        held[slot, two] = held[slot, two] + passed[dy, two]
        self.sums[3, dy] = self.net.push(held.at[slot, two], self.minus.at[dy, two], "x-")

    def close(self, dy):
        for copy in (self.raw[1, dy], self.raw[3, dy], self.sums[1, dy], self.sums[3, dy]):
            copy.wait_recv()
        self.held[dy] = (
            self.held[dy].astype(F32) + self.plus[dy].astype(F32) + self.minus[dy].astype(F32)
        ).astype(BF16)
        if dy:
            self.cross = self.net.push(self.held.at[1], self.last, "y")

    def result(self):
        self.cross.wait_recv()
        return self.held[0].astype(F32) + self.last[...].astype(F32)


def shard_sum_scratch(rows, width):
    def block(*lead):
        return pltpu.VMEM((*lead, rows, width), BF16)

    return [block(8), block(8), block(2), block(2), block(2), block()]


def gain_row(gains, row):
    return jnp.concatenate(
        [gains[s * GROWS : s * GROWS + 16, :][row : row + 1].astype(F32) for s in range(16)], 1
    )


def factor_of(rows):
    return lax.rsqrt(jnp.mean(rows * rows, -1, keepdims=True) + EPSILON)


def turn(rows, cosine, sine):
    first, second = rows[:, :HALF], rows[:, HALF:]
    return first * cosine - second * sine, second * cosine + first * sine


def tiles(count, body):
    def step(i, carry):
        body(i)
        return carry

    lax.fori_loop(0, count, step, 0)


def span(index, size):
    return pl.ds(pl.multiple_of(index * size, size), size)


def kernel_a(
    tok, cot, ablk, fblk, gblk, cosine, sine, allowed,
    n1_o, q_o, k_o, v_o, a_o, p_o, h_o, n2_o, aw_o, g_o, fw, cf,
    xf, n1, q, k, v, a, p, part, passed, plus, minus, mine, other, aw, gains,
    send, recv, local,
):
    here = Place()
    net = Net(here, send, recv, local)
    net.greet(ALL_NEAR)
    xs = RingGather(net, tok, xf)
    gg = ShardGather(net, gblk, gains, GROWS)
    gg.begin()
    ag = ShardGather(net, ablk, aw, BLOCK)
    ag.begin()
    saved = [
        net.copy(ablk, ag.at()),
        net.copy(gblk, gg.at()),
        net.copy(fblk, fw.at[pl.ds(pl.multiple_of(here.shard * BLOCK, BLOCK), BLOCK)]),
        net.copy(cot, cf.at[chunk(here.z)]),
    ]
    xf[xs.at(0), :] = tok[...]
    gg.across()
    ag.across()
    gg.near(0)
    gg.near(1)
    ag.near(0)
    gg.far(0)
    gg.far(1)
    xs.forward()
    ag.near(1)
    gg.finish()
    saved[0].wait()
    saved[1].wait()
    ag.far(0)
    ag.far(1)
    fg = ShardGather(net, fblk, fw, BLOCK)
    fg.begin()
    cs = RingGather(net, cot, cf)
    gain_one = gain_row(gains, 0)

    def normed(step):
        at = xs.at(step)
        rows = xf[at, :].astype(F32)
        n1[at, :] = (rows * factor_of(rows) * gain_one).astype(BF16)

    def project(step):
        at = xs.at(step)
        rows = n1[at, :]
        co, si = cosine[at, :], sine[at, :]
        for dst, i in ((q, 0), (k, 1)):
            first, second = turn(nn(rows, aw[:, i * HEAD : (i + 1) * HEAD]), co, si)
            dst[at, :HALF] = first.astype(BF16)
            dst[at, HALF:] = second.astype(BF16)
        v[at, :] = nn(rows, aw[:, 2 * HEAD : 3 * HEAD]).astype(BF16)

    normed(0)
    ag.finish()
    project(0)
    xs.left()
    normed(3)
    project(3)
    xs.right()
    normed(1)
    project(1)
    xs.far()
    normed(2)
    project(2)
    fg.across()
    out_copies = [
        net.copy(n1, n1_o), net.copy(aw, aw_o), net.copy(q, q_o), net.copy(k, k_o),
        net.copy(v, v_o), net.copy(gains, g_o),
    ]

    sums = RingSum(net, part, passed, plus, minus, mine, other, 2)

    def attend(step):
        at = sums.at(step)
        scores = jnp.where(
            allowed[at, :].astype(F32) > 0.5,
            nt(q[at, :], k[...]) * (1.0 / math.sqrt(HEAD)),
            NEGATIVE,
        )
        weight = jnp.exp(scores - jnp.max(scores, -1, keepdims=True))
        probs = weight / jnp.sum(weight, -1, keepdims=True)
        p[at, :] = probs
        a[at, :] = nn(probs.astype(BF16), v[...]).astype(BF16)

    def branch(step):
        at = sums.at(step)
        rows = a[at, :]

        def body(j):
            part[at, span(j, 512)] = nt(
                rows, aw[span(j, 512), 3 * HEAD : 4 * HEAD]
            ).astype(BF16)

        tiles(4, body)

    attend(2)
    branch(2)
    sums.far(0)
    sums.far(1)
    attend(1)
    branch(1)
    attend(3)
    branch(3)
    sums.raw(0)
    sums.raw(1)
    fg.near(0)
    sums.add(0)
    cs.forward()
    attend(0)
    branch(0)
    sums.add(1)
    out_copies += [net.copy(a, a_o), net.copy(p, p_o)]
    fg.near(1)
    sums.cross(0)
    fg.far(0)
    sums.cross(1)
    fg.far(1)
    cs.left()
    cs.right()
    cs.far()
    sums.arrive(0)
    sums.arrive(1)
    hidden = tok[...].astype(F32) + mine[...].astype(F32) + other[...].astype(F32)
    h_o[...] = hidden
    n2_o[...] = (hidden * factor_of(hidden) * gain_row(gains, 1)).astype(BF16)
    fg.finish()
    for copy in saved[2:] + out_copies:
        copy.wait()
    net.drain()


def out(shape, kind=BF16):
    return jax.ShapeDtypeStruct(shape, kind)


def params(number):
    return pltpu.CompilerParams(
        collective_id=number, has_side_effects=True, vmem_limit_bytes=60 * 1024 * 1024
    )


def call_a(tok, cot, ablk, fblk, gblk, cosine, sine, allowed):
    rows_b = pltpu.VMEM((TREE, WIDTH), BF16)
    head_b = pltpu.VMEM((TREE, HEAD), BF16)
    return pl.pallas_call(
        kernel_a,
        out_shape=[
            out((TREE, WIDTH)), out((TREE, HEAD)), out((TREE, HEAD)), out((TREE, HEAD)),
            out((TREE, HEAD)), out((TREE, TREE), F32), out((ROWS, WIDTH), F32),
            out((ROWS, WIDTH)), out((WIDTH, 4 * HEAD)), out((16 * GROWS, 128)),
            out((WIDTH, 3 * FFD)), out((TREE, WIDTH)),
        ],
        in_specs=[VM] * 8,
        out_specs=[ANY] * 6 + [VM] * 2 + [ANY] * 4,
        scratch_shapes=[
            rows_b, rows_b, head_b, head_b, head_b, head_b, pltpu.VMEM((TREE, TREE), F32), rows_b,
            *ring_sum_scratch(),
            pltpu.VMEM((WIDTH, 4 * HEAD), BF16), pltpu.VMEM((16 * GROWS, 128), BF16),
            *near_sems(96, 16),
        ],
        compiler_params=params(0),
        name="attend",
    )(tok, cot, ablk, fblk, gblk, cosine, sine, allowed)


def kernel_f(
    n2_in, h_in, fw, cf, gains,
    dh_o, low_o, out_o, grads_o, term_o,
    w, c, n2, dgu, hid,
    part, passed, plus, minus, mine, other,
    part2, passed2, plus2, minus2, mine2, other2,
    send, recv, local,
):
    here = Place()
    net = Net(here, send, recv, local)
    net.greet(("z+", "z-", "t"))
    ns = RingGather(net, n2_in, n2)
    loads = [net.copy(fw, w), net.copy(cf, c)]
    n2[ns.at(0), :] = n2_in[...]
    for copy in loads:
        copy.wait()

    def feed(step):
        at = ns.at(step)

        def body(j):
            cols = span(j, 256)
            rows = n2[at, :]
            g = nn(rows, w[:, cols])
            u = nn(rows, w[:, pl.ds(pl.multiple_of(FFD + j * 256, 256), 256)])
            d = nn(c[at, :], w[:, pl.ds(pl.multiple_of(2 * FFD + j * 256, 256), 256)])
            s = jax.nn.sigmoid(g)
            swish = g * s
            hid[at, cols] = (swish * u).astype(BF16)
            dgu[at, cols] = (d * u * s * (1.0 + g * (1.0 - s))).astype(BF16)
            dgu[at, pl.ds(pl.multiple_of(FFD + j * 256, 256), 256)] = (d * swish).astype(BF16)

        tiles(4, body)

    feed(0)
    ns.forward()
    ns.left()
    feed(3)
    ns.right()
    feed(1)
    ns.far()
    feed(2)
    sums = RingSum(net, part, passed, plus, minus, mine, other, 2)
    outs = RingSum(net, part2, passed2, plus2, minus2, mine2, other2, 2)

    def back(step):
        at = sums.at(step)

        def body(j):
            part[at, span(j, 512)] = nt(dgu[at, :], w[span(j, 512), : 2 * FFD]).astype(BF16)

        tiles(4, body)

    def down(step):
        at = sums.at(step)

        def body(j):
            part2[at, span(j, 512)] = nt(hid[at, :], w[span(j, 512), 2 * FFD :]).astype(BF16)

        tiles(4, body)

    back(2)
    sums.far(0)
    sums.far(1)
    back(1)
    back(3)
    sums.raw(0)
    sums.raw(1)
    sums.add(0)
    back(0)
    sums.add(1)
    down(2)
    outs.far(0)
    outs.far(1)
    down(1)
    down(3)
    outs.raw(0)
    outs.raw(1)
    down(0)
    sums.cross(0)

    def grad(i):
        turned = n2[:, span(i, 256)].T
        for j in range(4):
            w[span(i, 256), j * 512 : (j + 1) * 512] = nn(
                turned, dgu[:, j * 512 : (j + 1) * 512]
            ).astype(BF16)

    def grad_down(i):
        turned = c[:, span(i, 256)].T
        for j in range(2):
            w[span(i, 256), 2 * FFD + j * 512 : 2 * FFD + (j + 1) * 512] = nn(
                turned, hid[:, j * 512 : (j + 1) * 512]
            ).astype(BF16)

    tiles(4, grad)
    sums.cross(1)
    outs.add(0)
    outs.add(1)
    tiles(4, lambda i: grad(i + 4))
    tiles(8, grad_down)
    saves = [net.copy(w, grads_o)]
    sums.arrive(0)
    sums.arrive(1)
    hidden = h_in[...]
    upstream = mine[...].astype(F32) + other[...].astype(F32)
    factor = factor_of(hidden)
    weighted = upstream * gain_row(gains, 1)
    inner = jnp.mean(weighted * hidden, -1, keepdims=True)
    dh = (
        c[ns.at(0), :].astype(F32) + factor * weighted - hidden * (factor * factor * factor) * inner
    )
    dh_o[...] = dh
    low_o[...] = dh.astype(BF16)
    term_o[...] = jnp.sum(upstream * hidden * factor, 0, keepdims=True)
    outs.cross(0)
    outs.cross(1)
    outs.arrive(0)
    outs.arrive(1)
    out_o[...] = (
        h_in[...] + (mine2[...].astype(F32) + other2[...].astype(F32))
    ).astype(BF16)
    for copy in saves:
        copy.wait()
    net.drain()


def call_f(n2_in, h_in, fw, cf, gains):
    rows_b = pltpu.VMEM((TREE, WIDTH), BF16)
    return pl.pallas_call(
        kernel_f,
        out_shape=[
            out((ROWS, WIDTH), F32), out((ROWS, WIDTH)), out((ROWS, WIDTH)),
            out((WIDTH, 3 * FFD)), out((1, WIDTH), F32),
        ],
        in_specs=[VM, VM, ANY, ANY, VM],
        out_specs=[VM, VM, VM, ANY, VM],
        scratch_shapes=[
            pltpu.VMEM((WIDTH, 3 * FFD), BF16), rows_b, rows_b, rows_b,
            pltpu.VMEM((TREE, FFD), BF16),
            rows_b, *ring_sum_scratch(), rows_b, *ring_sum_scratch(),
            *near_sems(40, 8),
        ],
        compiler_params=params(1),
        name="feed",
    )(n2_in, h_in, fw, cf, gains)


def kernel_b(
    low_in, dh_in, tok, cosine, sine, gains, term_in, p_in, q_in, k_in, v_in, a_in, n1_in, aw_in, fgrads,
    dtok_o, agrads_o, terms_o, fblk_o,
    low, p, q, k, v, a, n1, aw, da, d, dk, dv,
    part, passed, plus, minus, mine, other,
    held, gift, fpassed, fplus, fminus, flast,
    send, recv, local,
):
    here = Place()
    net = Net(here, send, recv, local)
    net.greet(ALL_NEAR)
    ls = RingGather(net, low_in, low)
    loads = [
        net.copy(src, dst)
        for src, dst in (
            (aw_in, aw), (v_in, v), (p_in, p), (k_in, k), (q_in, q), (a_in, a), (n1_in, n1)
        )
    ]
    fs = ShardSum(net, fgrads, BLOCK, held, gift, fpassed, fplus, fminus, flast)
    low[ls.at(0), :] = low_in[...]

    def attended(step):
        at = ls.at(step)
        da[at, :] = nn(low[at, :], aw[:, 3 * HEAD : 4 * HEAD]).astype(BF16)

    loads[0].wait()
    attended(0)
    ls.forward()
    fs.pair(2, 1)
    fs.pair(2, 0)
    ls.left()
    attended(3)
    ls.right()
    attended(1)
    fs.pair(1, 1)
    fs.pair(3, 1)
    fs.pair(1, 0)
    fs.pair(3, 0)
    for copy in loads[1:]:
        copy.wait()
    fs.pass_on(1)
    ls.far()
    attended(2)

    def attend(step):
        at = ls.at(step)
        da_rows, probs = da[at, :], p[at, :]
        dp = nt(da_rows, v[...])
        ds = probs * (dp - jnp.sum(probs * dp, -1, keepdims=True))
        draw = (ds * (1.0 / math.sqrt(HEAD))).astype(BF16)
        first, second = turn(nn(draw, k[...]), cosine[at, :], -sine[at, :])
        d[at, :HALF] = first.astype(BF16)
        d[at, HALF:HEAD] = second.astype(BF16)
        dk_more, dv_more = tn(draw, q[at, :]), tn(probs.astype(BF16), da_rows)
        if step == 0:
            dk[...] = dk_more
            dv[...] = dv_more
        else:
            dk[...] += dk_more
            dv[...] += dv_more

    for step in range(4):
        attend(step)
    first, second = turn(dk[...], cosine[...], -sine[...])
    d[:, HEAD : HEAD + HALF] = first.astype(BF16)
    d[:, HEAD + HALF : 2 * HEAD] = second.astype(BF16)
    d[:, 2 * HEAD :] = dv[...].astype(BF16)

    sums = RingSum(net, part, passed, plus, minus, mine, other, 2)

    def back(step):
        at = sums.at(step)

        def body(j):
            part[at, span(j, 512)] = nt(d[at, :], aw[span(j, 512), : 3 * HEAD]).astype(BF16)

        tiles(4, body)

    back(2)
    sums.far(0)
    sums.far(1)
    back(1)
    back(3)
    sums.raw(0)
    sums.raw(1)
    fs.pass_on(0)
    sums.add(0)
    back(0)
    sums.add(1)

    def grad(i):
        turned = n1[:, span(i, 256)].T
        aw[span(i, 256), : 3 * HEAD] = nn(turned, d[...]).astype(BF16)
        turned = low[:, span(i, 256)].T
        aw[span(i, 256), 3 * HEAD :] = nn(turned, a[...]).astype(BF16)

    tiles(8, grad)
    saves = [net.copy(aw, agrads_o)]
    fs.pair(0, 1)
    fs.pair(0, 0)
    sums.cross(0)
    sums.cross(1)
    fs.close(1)
    fs.close(0)
    sums.arrive(0)
    sums.arrive(1)
    inputs = tok[...].astype(F32)
    upstream = mine[...].astype(F32) + other[...].astype(F32)
    factor = factor_of(inputs)
    weighted = upstream * gain_row(gains, 0)
    inner = jnp.mean(weighted * inputs, -1, keepdims=True)
    dtok_o[...] = (
        dh_in[...] + (factor * weighted - inputs * (factor * factor * factor) * inner)
    ).astype(BF16)
    term_one = jnp.sum(upstream * inputs * factor, 0, keepdims=True)
    term_two = term_in[...]
    row = lax.broadcasted_iota(jnp.int32, (GROWS, 128), 0)
    for s in range(16):
        cols = slice(s * 128, (s + 1) * 128)
        terms_o[s * GROWS : (s + 1) * GROWS, :] = jnp.where(
            row == 0, term_one[:, cols], jnp.where(row == 1, term_two[:, cols], 0.0)
        ).astype(BF16)
    fblk_o[...] = fs.result().astype(BF16)
    for copy in saves:
        copy.wait()
    net.drain()


def call_b(low, dh, tok, cosine, sine, gains, term, p, q, k, v, a, n1, aw, fgrads):
    rows_b = pltpu.VMEM((TREE, WIDTH), BF16)
    head_b = pltpu.VMEM((TREE, HEAD), BF16)
    head_f = pltpu.VMEM((TREE, HEAD), F32)
    return pl.pallas_call(
        kernel_b,
        out_shape=[
            out((ROWS, WIDTH)), out((WIDTH, 4 * HEAD)), out((16 * GROWS, 128)),
            out((BLOCK, 3 * FFD)),
        ],
        in_specs=[VM] * 7 + [ANY] * 8,
        out_specs=[VM, ANY, VM, VM],
        scratch_shapes=[
            rows_b, pltpu.VMEM((TREE, TREE), F32), head_b, head_b, head_b, head_b, rows_b,
            pltpu.VMEM((WIDTH, 4 * HEAD), BF16), head_b, pltpu.VMEM((TREE, 3 * HEAD), BF16),
            head_f, head_f,
            rows_b, *ring_sum_scratch(),
            *shard_sum_scratch(BLOCK, 3 * FFD),
            *near_sems(64, 24),
        ],
        compiler_params=params(2),
        name="attend_back",
    )(low, dh, tok, cosine, sine, gains, term, p, q, k, v, a, n1, aw, fgrads)


def kernel_r(
    agrads, terms, fblk,
    gone_o, query_o, key_o, value_o, wout_o, gtwo_o, gate_o, up_o, down_o,
    ffull, afull, gfull, ablk, gblk,
    held, gift, passed, plus, minus, last,
    gheld, ggift, gpassed, gplus, gminus, glast,
    send, recv, local,
):
    here = Place()
    net = Net(here, send, recv, local)
    net.greet(ALL_NEAR)
    gs = ShardSum(net, terms, GROWS, gheld, ggift, gpassed, gplus, gminus, glast)
    at = ShardSum(net, agrads, BLOCK, held, gift, passed, plus, minus, last)
    fz = RingGather(net, fblk, ffull)

    for shares in (gs, at):
        for dx in (2, 1, 3):
            for dy in (1, 0):
                shares.pair(dx, dy)
    gs.pass_on(1)
    gs.pass_on(0)
    at.pass_on(1)
    at.pass_on(0)
    for shares in (gs, at):
        shares.pair(0, 1)
        shares.pair(0, 0)
    fz.forward()

    def spread(zz, block):
        gate_o[:, span(zz, FFD)] = block[:, :FFD].astype(F32)
        up_o[:, span(zz, FFD)] = block[:, FFD : 2 * FFD].astype(F32)
        down_o[span(zz, FFD), :] = block[:, 2 * FFD :].astype(F32).T

    spread(here.z, fblk[...])
    for shares in (gs, at):
        shares.close(1)
        shares.close(0)
    gblk[...] = gs.result().astype(BF16)
    gz = RingGather(net, gblk, gfull)
    ablk[...] = at.result().astype(BF16)
    az = RingGather(net, ablk, afull)
    afull[az.at(0), :] = ablk[...]
    gfull[gz.at(0), :] = gblk[...]
    fz.left()
    spread(ring(here.z, 3), ffull[fz.at(3), :])
    fz.right()
    spread(ring(here.z, 1), ffull[fz.at(1), :])
    gz.forward()
    az.forward()
    fz.far()
    spread(ring(here.z, 2), ffull[fz.at(2), :])
    for shares in (gz, az):
        shares.left()
        shares.right()
        shares.far()
    blocks = [afull[i * BLOCK : (i + 1) * BLOCK, :].astype(F32) for i in range(4)]
    for i in range(4):
        query_o[:, i * HEAD : (i + 1) * HEAD] = blocks[i][:, :HEAD]
        wout_o[i * HEAD : (i + 1) * HEAD, :] = blocks[i][:, 3 * HEAD :].T
    for g in range(2):
        pair = blocks[2 * g][:, HEAD : 3 * HEAD] + blocks[2 * g + 1][:, HEAD : 3 * HEAD]
        key_o[:, g * HEAD : (g + 1) * HEAD] = pair[:, :HEAD]
        value_o[:, g * HEAD : (g + 1) * HEAD] = pair[:, HEAD:]
    gain = sum(gfull[i * GROWS : (i + 1) * GROWS, :].astype(F32) for i in range(4))
    gone_o[...] = gain[0:1]
    gtwo_o[...] = gain[1:2]
    net.drain()


def call_r(agrads, terms, fblk):
    return pl.pallas_call(
        kernel_r,
        out_shape=[
            out((1, 128), F32), out((BLOCK, 4 * HEAD), F32), out((BLOCK, 2 * HEAD), F32),
            out((BLOCK, 2 * HEAD), F32), out((4 * HEAD, BLOCK), F32), out((1, 128), F32),
            out((BLOCK, 4 * FFD), F32), out((BLOCK, 4 * FFD), F32), out((4 * FFD, BLOCK), F32),
        ],
        in_specs=[ANY, ANY, VM],
        out_specs=[VM] * 9,
        scratch_shapes=[
            pltpu.VMEM((4 * BLOCK, 3 * FFD), BF16), pltpu.VMEM((4 * BLOCK, 4 * HEAD), BF16),
            pltpu.VMEM((4 * GROWS, 128), BF16), pltpu.VMEM((BLOCK, 4 * HEAD), BF16),
            pltpu.VMEM((GROWS, 128), BF16),
            *shard_sum_scratch(BLOCK, 4 * HEAD), *shard_sum_scratch(GROWS, 128),
            *near_sems(80, 24),
        ],
        compiler_params=params(3),
        name="gather_grads",
    )(agrads, terms, fblk)


def tables(parent_row):
    index = jnp.arange(NSEG)
    links = (parent_row[:, None] == index[None, :]).astype(F32)
    reached = links + jnp.eye(NSEG, dtype=F32)
    for _ in range(4):
        reached = jnp.minimum(jnp.dot(reached, reached, precision=HIGHEST), 1.0)
    depth = jnp.sum(reached, 1) - 1.0
    token = jnp.arange(TREE)
    segment = token // SEG
    offset = token % SEG
    onehot = (segment[:, None] == index[None, :]).astype(F32)
    position = jnp.dot(onehot, depth, precision=HIGHEST) * SEG + offset.astype(F32)
    frequency = jnp.power(THETA, -(jnp.arange(HALF, dtype=F32) * 2.0) / HEAD)
    angles = position[:, None] * frequency[None, :]
    linked = nt(jnp.dot(onehot, reached, precision=HIGHEST), onehot) > 0.5
    allowed = linked & (
        (segment[:, None] != segment[None, :]) | (offset[None, :] <= offset[:, None])
    )
    return jnp.cos(angles), jnp.sin(angles), allowed.astype(BF16)


def local(
    tokens, parents, gain_attn, w_query, key_weight, value_weight, w_out, gain_ffn, w_gate, w_up,
    w_down, cotangent,
):
    z = lax.axis_index("ctx")

    def cols(w, at, size):
        return lax.dynamic_slice_in_dim(w, at, size, 1)

    def rows(w, at, size):
        return lax.dynamic_slice_in_dim(w, at, size, 0)

    gblk = jnp.pad(jnp.stack([gain_attn, gain_ffn], 0), ((0, GROWS - 2), (0, 0)))
    ablk = jnp.concatenate(
        [
            cols(w_query, z * HEAD, HEAD),
            cols(key_weight, (z // 2) * HEAD, HEAD),
            cols(value_weight, (z // 2) * HEAD, HEAD),
            rows(w_out, z * HEAD, HEAD).T,
        ],
        1,
    )
    fblk = jnp.concatenate(
        [cols(w_gate, z * FFD, FFD), cols(w_up, z * FFD, FFD), rows(w_down, z * FFD, FFD).T], 1
    )
    cosine, sine, allowed = tables(parents[0])
    n1, q, k, v, a, p, hidden, n2, aw, gains, fw, cf = call_a(
        tokens, cotangent, ablk, fblk, gblk, cosine, sine, allowed
    )
    dh, low, output, fgrads, term = call_f(n2, hidden, fw, cf, gains)
    d_tokens, agrads, terms, fsum = call_b(
        low, dh, tokens, cosine, sine, gains, term, p, q, k, v, a, n1, aw, fgrads
    )
    g_one, query, key, value, wout, g_two, gate, up, down = call_r(agrads, terms, fsum)
    return (
        output, d_tokens, g_one.reshape(128), query, key, value, wout, g_two.reshape(128), gate, up,
        down,
    )


def solution(mesh):
    rows = P(("shard", "ctx"), None)
    weight = P("shard", "tp")
    turned = P("tp", "shard")
    vector = P("shard")
    return jax.shard_map(
        local,
        mesh=mesh,
        in_specs=(
            rows, P("shard", None), vector, weight, weight, weight, turned, vector,
            weight, weight, turned, rows,
        ),
        out_specs=(
            rows, rows, vector, weight, weight, weight, turned, vector, weight, weight, turned,
        ),
        check_vma=False,
    )
```

```python
import functools
import math

import jax
import jax.numpy as jnp
import numpy as np
from jax import lax
from jax.experimental import pallas as pl
from jax.experimental.pallas import tpu as pltpu
from jax.sharding import PartitionSpec as P

HEAD = 256
HALF = HEAD // 2
SEG = 48
NSEG = 16
ROWS = 192
TREE = 768
WIDTH = 2048
FFD = 1024
BLOCK = 128
GROWS = 32
SUBS = 4

EPSILON = 1e-06
THETA = 1000042.0
NEGATIVE = -1e30
HIGHEST = lax.Precision.HIGHEST
F32 = jnp.float32
BF16 = jnp.bfloat16
MESH = pl.DeviceIdType.MESH
ANY = pl.BlockSpec(memory_space=pl.ANY)
VM = pl.BlockSpec(memory_space=pltpu.VMEM)


def nn(left, right):
    return jnp.dot(left, right, preferred_element_type=F32)


def nt(left, right):
    return lax.dot_general(left, right, (((1,), (1,)), ((), ())), preferred_element_type=F32)


def tn(left, right):
    return lax.dot_general(left, right, (((0,), (0,)), ((), ())), preferred_element_type=F32)


def ring(value, step):
    return lax.rem(value + step, 4)


class Place:
    def __init__(self):
        shard = lax.axis_index("shard")
        self.shard = shard
        self.y = shard // 8
        self.x = lax.rem(shard // 2, 4)
        self.c = lax.rem(shard, 2)
        self.z = lax.axis_index("ctx")
        self.t = lax.axis_index("tp")

    def block(self, dy=0, dx=0, dc=0):
        y = 1 - self.y if dy else self.y
        c = 1 - self.c if dc else self.c
        return y * 8 + ring(self.x, dx) * 2 + c

    def to(self, dy=0, dx=0, dc=0, dz=0, dt=0):
        t = 1 - self.t if dt else self.t
        return (self.block(dy, dx, dc), ring(self.z, dz), t)


ALL_NEAR = ("y", "x+", "x-", "c", "z+", "z-", "t")
NEAR = {
    "y": dict(dy=1), "x+": dict(dx=1), "x-": dict(dx=3), "c": dict(dc=1),
    "z+": dict(dz=1), "z-": dict(dz=3), "t": dict(dt=1),
}


class Net:
    def __init__(self, here, send, recv, local):
        self.here, self.send, self.recv, self.local = here, send, recv, local
        self.sent, self.count, self.copies = [], 0, 0

    def greet(self, names):
        barrier = pltpu.get_barrier_semaphore()
        for name in names:
            pl.semaphore_signal(
                barrier, inc=1, device_id=self.here.to(**NEAR[name]), device_id_type=MESH
            )
        pl.semaphore_wait(barrier, len(names))

    def push(self, src, dst, name):
        index = self.count
        self.count += 1
        copy = pltpu.make_async_remote_copy(
            src_ref=src,
            dst_ref=dst,
            send_sem=self.send.at[index],
            recv_sem=self.recv.at[index],
            device_id=self.here.to(**NEAR[name]),
            device_id_type=MESH,
        )
        copy.start()
        self.sent.append(copy)
        return copy

    def copy(self, src, dst):
        index = self.copies
        self.copies += 1
        copy = pltpu.make_async_copy(src, dst, self.local.at[index])
        copy.start()
        return copy

    def drain(self):
        for copy in self.sent:
            copy.wait_send()


def near_sems(remote, local):
    return [
        pltpu.SemaphoreType.DMA((remote,)),
        pltpu.SemaphoreType.DMA((remote,)),
        pltpu.SemaphoreType.DMA((local,)),
    ]


def chunk(index):
    return pl.ds(pl.multiple_of(index * ROWS, ROWS), ROWS)


class RingGather:
    def __init__(self, net, own, full, shared=False):
        self.net, self.full, self.rows, self.shared = net, full, own.shape[0], shared
        half = self.rows // 2
        one, two = own.at[pl.ds(0, half)], own.at[pl.ds(half, half)]
        width = own.shape[1] // 2
        self.cols = pl.ds(pl.multiple_of(net.here.t * width, width), width)
        near_one, near_two = self.half(0, 0), self.half(0, 1)
        self.a1 = net.push(one, near_one, "z+")
        self.b2 = net.push(two, near_two, "z-")
        if shared:
            one, two = one.at[:, self.cols], two.at[:, self.cols]
            near_one, near_two = near_one.at[:, self.cols], near_two.at[:, self.cols]
        self.a2 = net.push(two, near_two, "z+")
        self.b1 = net.push(one, near_one, "z-")

    def half(self, step, part):
        half = self.rows // 2
        start = ring(self.net.here.z, step) * self.rows + part * half
        return self.full.at[pl.ds(pl.multiple_of(start, half), half)]

    def at(self, step):
        return span(ring(self.net.here.z, step), self.rows)

    def forward(self):
        self.a1.wait_recv()
        self.f1 = self.net.push(self.half(3, 0), self.half(3, 0), "z+")
        self.b2.wait_recv()
        self.f2 = self.net.push(self.half(1, 1), self.half(1, 1), "z-")

    def share(self):
        self.a2.wait_recv()
        piece = self.half(3, 1).at[:, self.cols]
        self.a2 = self.net.push(piece, piece, "t")
        self.b1.wait_recv()
        piece = self.half(1, 0).at[:, self.cols]
        self.b1 = self.net.push(piece, piece, "t")

    def left(self):
        self.a2.wait_recv()

    def right(self):
        self.b1.wait_recv()

    def far(self):
        self.f1.wait_recv()
        self.f2.wait_recv()


class HalfGather:
    def __init__(self, net, own, full):
        width = own.shape[1] // 2
        self.net = net
        cols = pl.ds(pl.multiple_of(net.here.t * width, width), width)
        self.full = full.at[:, cols]
        self.ring = RingGather(net, own.at[:, cols], self.full)
        self.given = []

    def give(self, step):
        (None, self.ring.right, self.ring.far, self.ring.left)[step]()
        piece = self.full.at[self.ring.at(step)]
        self.given.append(self.net.push(piece, piece, "t"))

    def finish(self):
        for copy in self.given:
            copy.wait_recv()


class RingSum:
    def __init__(self, net, part, passed, plus, minus, mine, other, subs):
        self.net, self.part, self.passed = net, part, passed
        self.plus, self.minus, self.mine, self.other = plus, minus, mine, other
        width = part.shape[1] // subs
        self.cols = [
            (pl.ds(i * width, width // 2), pl.ds(i * width + width // 2, width // 2))
            for i in range(subs)
        ]
        self.subs = subs
        self.width = width
        self.e1, self.e2, self.r1, self.r2 = {}, {}, {}, {}
        self.s1, self.s2, self.t = {}, {}, {}

    def at(self, step):
        return chunk(ring(self.net.here.z, step))

    def far(self, i):
        one, two = self.cols[i]
        self.e1[i] = self.net.push(self.part.at[self.at(2), one], self.passed.at[:, one], "z+")
        self.e2[i] = self.net.push(self.part.at[self.at(2), two], self.passed.at[:, two], "z-")

    def raw(self, i):
        one, two = self.cols[i]
        self.r1[i] = self.net.push(self.part.at[self.at(1), two], self.plus.at[:, two], "z+")
        self.r2[i] = self.net.push(self.part.at[self.at(3), one], self.minus.at[:, one], "z-")

    def add(self, i):
        one, two = self.cols[i]
        part, passed = self.part, self.passed
        self.e1[i].wait_recv()
        part[self.at(1), one] = (
            part[self.at(1), one].astype(F32) + passed[:, one].astype(F32)
        ).astype(BF16)
        self.s1[i] = self.net.push(part.at[self.at(1), one], self.plus.at[:, one], "z+")
        self.e2[i].wait_recv()
        part[self.at(3), two] = (
            part[self.at(3), two].astype(F32) + passed[:, two].astype(F32)
        ).astype(BF16)
        self.s2[i] = self.net.push(part.at[self.at(3), two], self.minus.at[:, two], "z-")

    def settle(self, i):
        for copy in (self.r1[i], self.r2[i], self.s1[i], self.s2[i]):
            copy.wait_recv()

    def cross(self, i):
        self.settle(i)
        both = pl.ds(i * self.width, self.width)
        self.mine[:, both] = (
            self.part[self.at(0), both].astype(F32)
            + self.plus[:, both].astype(F32)
            + self.minus[:, both].astype(F32)
        ).astype(BF16)
        self.t[i] = self.net.push(self.mine.at[:, both], self.other.at[:, both], "t")

    def arrive(self, i):
        self.t[i].wait_recv()


def ring_sum_scratch():
    return [pltpu.VMEM((ROWS, WIDTH), BF16) for _ in range(5)]


class ShardGather:
    def __init__(self, net, own, full, rows):
        self.net, self.own, self.full, self.rows = net, own, full, rows
        self.to_sibling = []

    def at(self, part=None, **step):
        block = self.net.here.block(**step)
        if part is None:
            return self.full.at[pl.ds(pl.multiple_of(block * self.rows, self.rows), self.rows)]
        half = self.rows // 2
        start = block * self.rows + part * half
        return self.full.at[pl.ds(pl.multiple_of(start, half), half)]

    def relay(self, name, part=None, **step):
        ref = self.at(part, **step)
        return self.net.push(ref, ref, name)

    def sibling(self, part=None, **step):
        self.to_sibling.append(self.relay("c", part, **step))

    def begin(self):
        self.y0, self.p0, self.m0, c0 = (
            self.net.push(self.own, self.at(), name) for name in ("y", "x+", "x-", "c")
        )
        self.to_sibling.append(c0)

    def across(self):
        self.y0.wait_recv()
        self.p1 = self.relay("x+", dy=1)
        self.m1 = self.relay("x-", dy=1)
        self.sibling(dy=1)

    def near(self, dy):
        plus, minus = (self.p1, self.m1) if dy else (self.p0, self.m0)
        plus.wait_recv()
        fp = self.relay("x+", 0, dy=dy, dx=3)
        self.sibling(dy=dy, dx=3)
        minus.wait_recv()
        fm = self.relay("x-", 1, dy=dy, dx=1)
        self.sibling(dy=dy, dx=1)
        if dy:
            self.fp1, self.fm1 = fp, fm
        else:
            self.fp0, self.fm0 = fp, fm

    def far(self, dy):
        plus, minus = (self.fp1, self.fm1) if dy else (self.fp0, self.fm0)
        plus.wait_recv()
        self.sibling(0, dy=dy, dx=2)
        minus.wait_recv()
        self.sibling(1, dy=dy, dx=2)

    def finish(self):
        for copy in self.to_sibling:
            copy.wait_recv()


class ShardSum:
    def __init__(self, net, source, rows, gift, passed, plus, minus, last, held=None):
        self.net, self.source, self.rows, self.held = net, source, rows, held
        self.gift, self.passed, self.plus, self.minus, self.last = gift, passed, plus, minus, last
        self.gifts, self.loads = {}, {}
        for dx in (2, 1, 3, 0):
            for dy in (1, 0):
                self.gifts[dx, dy] = net.push(
                    self.block(dx, dy, 1), gift.at[2 * dx + dy], "c"
                )
                if held is not None:
                    self.loads[dx, dy] = net.copy(self.block(dx, dy, 0), held.at[2 * dx + dy])
        self.e1, self.e2, self.raw, self.sums = {}, {}, {}, {}

    def block(self, dx, dy, dc):
        return self.source.at[span(self.net.here.block(dx=dx, dy=dy, dc=dc), self.rows)]

    def kept(self, dx, dy, part=None):
        half = self.rows // 2
        if self.held is not None:
            ref = self.held.at[2 * dx + dy]
            return ref if part is None else ref.at[pl.ds(part * half, half)]
        block = self.net.here.block(dx=dx, dy=dy)
        if part is None:
            return self.source.at[span(block, self.rows)]
        return self.source.at[pl.ds(pl.multiple_of(block * self.rows + part * half, half), half)]

    def pair(self, dx, dy):
        self.gifts[dx, dy].wait_recv()
        if self.held is not None:
            self.loads[dx, dy].wait()
        ref = self.kept(dx, dy)
        ref[...] = ref[...] + self.gift[2 * dx + dy]
        half = self.rows // 2
        one, two = pl.ds(0, half), pl.ds(half, half)
        if dx == 2:
            self.e1[dy] = self.net.push(self.kept(2, dy, 0), self.passed.at[dy, one], "x+")
            self.e2[dy] = self.net.push(self.kept(2, dy, 1), self.passed.at[dy, two], "x-")
        if dx == 1:
            self.raw[1, dy] = self.net.push(self.kept(1, dy, 1), self.plus.at[dy, two], "x+")
        if dx == 3:
            self.raw[3, dy] = self.net.push(self.kept(3, dy, 0), self.minus.at[dy, one], "x-")

    def pass_on(self, dy):
        half = self.rows // 2
        one, two = pl.ds(0, half), pl.ds(half, half)
        self.e1[dy].wait_recv()
        ref = self.kept(1, dy, 0)
        ref[...] = ref[...] + self.passed[dy, one]
        self.sums[1, dy] = self.net.push(ref, self.plus.at[dy, one], "x+")
        self.e2[dy].wait_recv()
        ref = self.kept(3, dy, 1)
        ref[...] = ref[...] + self.passed[dy, two]
        self.sums[3, dy] = self.net.push(ref, self.minus.at[dy, two], "x-")

    def close(self, dy):
        for copy in (self.raw[1, dy], self.raw[3, dy], self.sums[1, dy], self.sums[3, dy]):
            copy.wait_recv()
        ref = self.kept(0, dy)
        ref[...] = (
            ref[...].astype(F32) + self.plus[dy].astype(F32) + self.minus[dy].astype(F32)
        ).astype(BF16)
        if dy:
            self.cross = self.net.push(ref, self.last, "y")

    def result(self):
        self.cross.wait_recv()
        return self.kept(0, 0)[...].astype(F32) + self.last[...].astype(F32)


def shard_sum_scratch(rows, width):
    def block(*lead):
        return pltpu.VMEM((*lead, rows, width), BF16)

    return [block(8), block(2), block(2), block(2), block()]


def gain_row(gains, row):
    return jnp.concatenate(
        [gains[s * GROWS : s * GROWS + 16, :][row : row + 1].astype(F32) for s in range(16)], 1
    )


def factor_of(rows):
    return lax.rsqrt(jnp.mean(rows * rows, -1, keepdims=True) + EPSILON)


def turn(rows, cosine, sine):
    first, second = rows[:, :HALF], rows[:, HALF:]
    return first * cosine - second * sine, second * cosine + first * sine


def tiles(count, body):
    def step(i, carry):
        body(i)
        return carry

    lax.fori_loop(0, count, step, 0)


def span(index, size):
    return pl.ds(pl.multiple_of(index * size, size), size)


def kernel_a(
    tok, cot, parents, frequency, gblk, wq, wk, wv, wo, wg, wu, wd,
    n1_o, q_o, k_o, v_o, a_o, p_o, h_o, n2_o, cosine, sine, aw_o, g_o, fw, cf,
    xf, n1, q, k, v, a, p, part, passed, plus, minus, mine, other, aw, gains,
    ablk, fblk, wo_s, wd_s, onehot, reach,
    send, recv, local,
):
    here = Place()
    net = Net(here, send, recv, local)
    head = span(here.z, HEAD)
    group = span(here.z // 2, HEAD)
    ff = span(here.z, FFD)
    own_a = [
        net.copy(wq.at[:, head], ablk.at[:, pl.ds(0, HEAD)]),
        net.copy(wk.at[:, group], ablk.at[:, pl.ds(HEAD, HEAD)]),
        net.copy(wv.at[:, group], ablk.at[:, pl.ds(2 * HEAD, HEAD)]),
        net.copy(wo.at[head], wo_s),
    ]
    own_f = [
        net.copy(wg.at[:, ff], fblk.at[:, pl.ds(0, FFD)]),
        net.copy(wu.at[:, ff], fblk.at[:, pl.ds(FFD, FFD)]),
        net.copy(wd.at[ff], wd_s),
    ]
    net.greet(ALL_NEAR)
    xs = RingGather(net, tok, xf)
    gg = ShardGather(net, gblk, gains, GROWS)
    gg.begin()
    for copy in own_a:
        copy.wait()
    ablk[:, 3 * HEAD :] = wo_s[...].astype(F32).T.astype(BF16)
    ag = ShardGather(net, ablk, aw, BLOCK)
    ag.begin()
    saved = [
        net.copy(ablk, ag.at()),
        net.copy(gblk, gg.at()),
        net.copy(cot, cf.at[chunk(here.z)]),
    ]
    xf[xs.at(0), :] = tok[...]
    for copy in own_f:
        copy.wait()
    fblk[:, 2 * FFD :] = wd_s[...].astype(F32).T.astype(BF16)
    gg.across()
    ag.across()
    gg.near(0)
    gg.near(1)
    ag.near(0)
    gg.far(0)
    gg.far(1)
    xs.forward()
    cs = HalfGather(net, cot, cf)
    ag.near(1)
    fg = ShardGather(net, fblk, fw, BLOCK)
    fg.begin()
    saved.append(net.copy(fblk, fg.at()))

    segment = lax.broadcasted_iota(jnp.int32, (NSEG, NSEG), 0)
    links = jnp.where(parents[...] == segment, 1.0, 0.0)
    links += jnp.where(segment == lax.broadcasted_iota(jnp.int32, (NSEG, NSEG), 1), 1.0, 0.0)
    links = links.astype(BF16)
    for _ in range(4):
        links = jnp.minimum(nn(links, links), 1.0).astype(BF16)
    token = lax.broadcasted_iota(jnp.int32, (TREE, NSEG), 0)
    first = lax.broadcasted_iota(jnp.int32, (TREE, NSEG), 1) * SEG
    inside = (token >= first) & (token < first + SEG)
    members = jnp.where(inside, 1.0, 0.0)
    onehot[...] = members.astype(BF16)
    reached = nt(onehot[...], links)
    reach[...] = reached.astype(BF16)
    offset = (token[:, :1] - jnp.sum(jnp.where(inside, first, 0), -1, keepdims=True)).astype(F32)
    position = (jnp.sum(reached, -1, keepdims=True) - 1.0) * SEG + offset

    def table(i):
        rows = slice(i * ROWS, (i + 1) * ROWS)
        angles = position[rows] * frequency[...]
        cosine[rows, :] = jnp.cos(angles)
        sine[rows, :] = jnp.sin(angles)

    table(0)
    gg.finish()
    saved[0].wait()
    saved[1].wait()
    ag.far(0)
    table(1)
    ag.far(1)
    table(2)
    table(3)
    gain_one = gain_row(gains, 0)

    def normed(step):
        at = xs.at(step)
        rows = xf[at, :].astype(F32)
        n1[at, :] = (rows * factor_of(rows) * gain_one).astype(BF16)

    def project(step):
        at = xs.at(step)
        rows = n1[at, :]
        co, si = cosine[at, :], sine[at, :]
        for dst, i in ((q, 0), (k, 1)):
            first, second = turn(nn(rows, aw[:, i * HEAD : (i + 1) * HEAD]), co, si)
            dst[at, :HALF] = first.astype(BF16)
            dst[at, HALF:] = second.astype(BF16)
        v[at, :] = nn(rows, aw[:, 2 * HEAD : 3 * HEAD]).astype(BF16)

    normed(0)
    ag.finish()
    project(0)
    xs.left()
    normed(3)
    project(3)
    xs.right()
    normed(1)
    project(1)
    xs.far()
    normed(2)
    project(2)
    cs.ring.forward()
    fg.across()
    cs.give(3)
    cs.give(1)
    out_copies = [
        net.copy(n1, n1_o), net.copy(aw, aw_o), net.copy(q, q_o), net.copy(k, k_o),
        net.copy(v, v_o), net.copy(gains, g_o),
    ]

    sums = RingSum(net, part, passed, plus, minus, mine, other, SUBS)

    def attend(step):
        at = sums.at(step)
        row = lax.broadcasted_iota(jnp.int32, (ROWS, TREE), 0) + ring(here.z, step) * ROWS
        column = lax.broadcasted_iota(jnp.int32, (ROWS, TREE), 1)
        linked = nt(reach[at, :], onehot[...])
        same = nt(onehot[at, :], onehot[...])
        allowed = (linked > 0.5) & ((same < 0.5) | (column <= row))
        scores = jnp.where(allowed, nt(q[at, :], k[...]) * (1.0 / math.sqrt(HEAD)), NEGATIVE)
        weight = jnp.exp(scores - jnp.max(scores, -1, keepdims=True))
        probs = weight / jnp.sum(weight, -1, keepdims=True)
        p[at, :] = probs
        a[at, :] = nn(probs.astype(BF16), v[...]).astype(BF16)

    def branch(step):
        at = sums.at(step)
        rows = a[at, :]

        def body(j):
            part[at, span(j, 512)] = nt(
                rows, aw[span(j, 512), 3 * HEAD : 4 * HEAD]
            ).astype(BF16)

        tiles(4, body)

    attend(2)
    branch(2)
    for i in range(SUBS):
        sums.far(i)
    cs.give(2)
    attend(1)
    branch(1)
    fg.near(0)
    attend(3)
    branch(3)
    for i in range(SUBS):
        sums.raw(i)
        sums.add(i)
    fg.near(1)
    attend(0)
    branch(0)
    out_copies += [net.copy(a, a_o), net.copy(p, p_o)]
    for i in range(SUBS):
        sums.cross(i)
    fg.far(0)
    fg.far(1)
    for i in range(SUBS):
        sums.arrive(i)
    hidden = tok[...].astype(F32) + mine[...].astype(F32) + other[...].astype(F32)
    h_o[...] = hidden
    n2_o[...] = (hidden * factor_of(hidden) * gain_row(gains, 1)).astype(BF16)
    cs.finish()
    fg.finish()
    for copy in saved[2:] + out_copies:
        copy.wait()
    net.drain()


def out(shape, kind=BF16):
    return jax.ShapeDtypeStruct(shape, kind)


def params(number):
    return pltpu.CompilerParams(
        collective_id=number, has_side_effects=True, vmem_limit_bytes=60 * 1024 * 1024
    )


def call_a(tok, cot, parents, frequency, gblk, *weights):
    rows_b = pltpu.VMEM((TREE, WIDTH), BF16)
    head_b = pltpu.VMEM((TREE, HEAD), BF16)
    return pl.pallas_call(
        kernel_a,
        out_shape=[
            out((TREE, WIDTH)), out((TREE, HEAD)), out((TREE, HEAD)), out((TREE, HEAD)),
            out((TREE, HEAD)), out((TREE, TREE), F32), out((ROWS, WIDTH), F32),
            out((ROWS, WIDTH)), out((TREE, HALF), F32), out((TREE, HALF), F32),
            out((WIDTH, 4 * HEAD)), out((16 * GROWS, 128)),
            out((WIDTH, 3 * FFD)), out((TREE, WIDTH)),
        ],
        in_specs=[VM] * 5 + [ANY] * 7,
        out_specs=[ANY] * 6 + [VM] * 4 + [ANY] * 4,
        scratch_shapes=[
            rows_b, rows_b, head_b, head_b, head_b, head_b, pltpu.VMEM((TREE, TREE), F32), rows_b,
            *ring_sum_scratch(),
            pltpu.VMEM((WIDTH, 4 * HEAD), BF16), pltpu.VMEM((16 * GROWS, 128), BF16),
            pltpu.VMEM((BLOCK, 4 * HEAD), BF16), pltpu.VMEM((BLOCK, 3 * FFD), BF16),
            pltpu.VMEM((HEAD, BLOCK), BF16), pltpu.VMEM((FFD, BLOCK), BF16),
            pltpu.VMEM((TREE, NSEG), BF16), pltpu.VMEM((TREE, NSEG), BF16),
            *near_sems(112, 24),
        ],
        compiler_params=params(0),
        name="attend",
    )(tok, cot, parents, frequency, gblk, *weights)


def kernel_f(
    n2_in, h_in, fw, cf, gains,
    dh_o, low_o, outh_o, grads_o, term_o,
    w, c, n2, dgu, hid,
    part, passed, plus, minus, mine, other,
    given, taken, part2, passed2, plus2, minus2,
    send, recv, local,
):
    here = Place()
    net = Net(here, send, recv, local)
    net.greet(("z+", "z-", "t"))
    ns = RingGather(net, n2_in, n2)
    loads = [net.copy(fw, w), net.copy(cf, c)]
    n2[ns.at(0), :] = n2_in[...]
    for copy in loads:
        copy.wait()

    def feed(step):
        at = ns.at(step)

        def body(j):
            cols = span(j, 256)
            rows = n2[at, :]
            g = nn(rows, w[:, cols])
            u = nn(rows, w[:, pl.ds(pl.multiple_of(FFD + j * 256, 256), 256)])
            d = nn(c[at, :], w[:, pl.ds(pl.multiple_of(2 * FFD + j * 256, 256), 256)])
            s = jax.nn.sigmoid(g)
            swish = g * s
            hid[at, cols] = (swish * u).astype(BF16)
            dgu[at, cols] = (d * u * s * (1.0 + g * (1.0 - s))).astype(BF16)
            dgu[at, pl.ds(pl.multiple_of(FFD + j * 256, 256), 256)] = (d * swish).astype(BF16)

        tiles(4, body)

    half = WIDTH // 2

    def down(step, t, dst):
        at = ns.at(step)

        def body(j):
            rows = pl.ds(pl.multiple_of(t * half + j * 512, 512), 512)
            dst[at, span(j, 512)] = nt(hid[at, :], w[rows, 2 * FFD :]).astype(BF16)

        tiles(2, body)

    gifts = {}

    def give(step):
        down(step, 1 - here.t, given)
        at = ns.at(step)
        gifts[step] = net.push(given.at[at], taken.at[at], "t")

    feed(0)
    ns.forward()
    give(0)
    ns.left()
    feed(3)
    give(3)
    ns.right()
    feed(1)
    give(1)
    ns.far()
    feed(2)
    sums = RingSum(net, part, passed, plus, minus, mine, other, SUBS)
    outs = RingSum(net, part2, passed2, plus2, minus2, None, None, 1)

    def back(step):
        at = sums.at(step)

        def body(j):
            part[at, span(j, 512)] = nt(dgu[at, :], w[span(j, 512), : 2 * FFD]).astype(BF16)

        tiles(4, body)

    back(2)
    for i in range(SUBS):
        sums.far(i)
    give(2)
    back(1)
    back(3)
    for i in range(SUBS):
        sums.raw(i)
        sums.add(i)
    back(0)

    def keep(step):
        down(step, here.t, part2)

    keep(2)
    keep(1)
    keep(3)
    keep(0)

    def grad(i):
        turned = n2[:, span(i, 256)].T
        for j in range(4):
            w[span(i, 256), j * 512 : (j + 1) * 512] = nn(
                turned, dgu[:, j * 512 : (j + 1) * 512]
            ).astype(BF16)

    def grad_down(i):
        turned = c[:, span(i, 256)].T
        for j in range(2):
            w[span(i, 256), 2 * FFD + j * 512 : 2 * FFD + (j + 1) * 512] = nn(
                turned, hid[:, j * 512 : (j + 1) * 512]
            ).astype(BF16)

    def take(step):
        gifts[step].wait_recv()
        at = ns.at(step)
        part2[at, :] = part2[at, :] + taken[at, :]

    tiles(4, grad_down)
    sums.cross(0)
    sums.cross(1)
    take(2)
    outs.far(0)
    take(1)
    take(3)
    outs.raw(0)
    tiles(4, lambda i: grad_down(i + 4))
    sums.cross(2)
    sums.cross(3)
    tiles(4, grad)
    outs.add(0)
    take(0)
    for i in range(SUBS):
        sums.arrive(i)
    hidden = h_in[...]
    upstream = mine[...].astype(F32) + other[...].astype(F32)
    factor = factor_of(hidden)
    weighted = upstream * gain_row(gains, 1)
    inner = jnp.mean(weighted * hidden, -1, keepdims=True)
    dh = (
        c[ns.at(0), :].astype(F32) + factor * weighted - hidden * (factor * factor * factor) * inner
    )
    dh_o[...] = dh
    low_o[...] = dh.astype(BF16)
    term_o[...] = jnp.sum(upstream * hidden * factor, 0, keepdims=True)
    tiles(4, lambda i: grad(i + 4))
    saves = [net.copy(w, grads_o)]
    outs.settle(0)
    mine_half = span(here.t, half)
    outh_o[...] = (
        h_in[:, mine_half]
        + part2[ns.at(0), :].astype(F32)
        + plus2[...].astype(F32)
        + minus2[...].astype(F32)
    ).astype(BF16)
    for copy in saves:
        copy.wait()
    net.drain()


def call_f(n2_in, h_in, fw, cf, gains):
    rows_b = pltpu.VMEM((TREE, WIDTH), BF16)
    half_b = pltpu.VMEM((TREE, WIDTH // 2), BF16)
    own_b = pltpu.VMEM((ROWS, WIDTH // 2), BF16)
    return pl.pallas_call(
        kernel_f,
        out_shape=[
            out((ROWS, WIDTH), F32), out((ROWS, WIDTH)), out((ROWS, WIDTH // 2)),
            out((WIDTH, 3 * FFD)), out((1, WIDTH), F32),
        ],
        in_specs=[VM, VM, ANY, ANY, VM],
        out_specs=[VM, VM, VM, ANY, VM],
        scratch_shapes=[
            pltpu.VMEM((WIDTH, 3 * FFD), BF16), rows_b, rows_b, rows_b,
            pltpu.VMEM((TREE, FFD), BF16),
            rows_b, *ring_sum_scratch(),
            half_b, half_b, half_b, own_b, own_b, own_b,
            *near_sems(64, 8),
        ],
        compiler_params=params(1),
        name="feed",
    )(n2_in, h_in, fw, cf, gains)


def kernel_b(
    low_in, dh_in, tok, cosine, sine, gains, term_in, outh, p_in, q_in, k_in, v_in, a_in, n1_in, aw_in,
    fgrads,
    dtok_o, out_o, ffull, afull, gfull,
    low, p, q, k, v, a, n1, aw, da, d, dk, dv, terms, fblk, ablk, gblk,
    part, passed, plus, minus, mine, other,
    fgift, fpassed, fplus, fminus, flast, held,
    agift, apassed, aplus, aminus, alast,
    ggift, gpassed, gplus, gminus, glast,
    send, recv, local,
):
    here = Place()
    net = Net(here, send, recv, local)
    net.greet(ALL_NEAR)
    ls = RingGather(net, low_in, low, True)
    loads = [
        net.copy(src, dst)
        for src, dst in (
            (aw_in, aw), (v_in, v), (p_in, p), (k_in, k), (q_in, q), (a_in, a), (n1_in, n1)
        )
    ]
    fs = ShardSum(net, fgrads, BLOCK, fgift, fpassed, fplus, fminus, flast, held)
    my_half = span(here.t, WIDTH // 2)
    out_copy = net.copy(outh, out_o.at[:, my_half])
    out_push = net.push(outh, out_o.at[:, my_half], "t")
    low[ls.at(0), :] = low_in[...]

    def attended(step):
        at = ls.at(step)
        da[at, :] = nn(low[at, :], aw[:, 3 * HEAD : 4 * HEAD]).astype(BF16)

    loads[0].wait()
    attended(0)
    ls.forward()
    fs.pair(2, 1)
    fs.pair(2, 0)
    ls.share()
    fs.pair(1, 1)
    fs.pair(3, 1)
    ls.left()
    attended(3)
    ls.right()
    attended(1)
    fs.pass_on(1)
    fs.pair(1, 0)
    fs.pair(3, 0)
    for copy in loads[1:]:
        copy.wait()
    ls.far()
    attended(2)

    def attend(step):
        at = ls.at(step)
        da_rows, probs = da[at, :], p[at, :]
        dp = nt(da_rows, v[...])
        ds = probs * (dp - jnp.sum(probs * dp, -1, keepdims=True))
        draw = (ds * (1.0 / math.sqrt(HEAD))).astype(BF16)
        first, second = turn(nn(draw, k[...]), cosine[at, :], -sine[at, :])
        d[at, :HALF] = first.astype(BF16)
        d[at, HALF:HEAD] = second.astype(BF16)
        dk_more, dv_more = tn(draw, q[at, :]), tn(probs.astype(BF16), da_rows)
        if step == 0:
            dk[...] = dk_more
            dv[...] = dv_more
        else:
            dk[...] += dk_more
            dv[...] += dv_more

    for step in range(4):
        attend(step)
    first, second = turn(dk[...], cosine[...], -sine[...])
    d[:, HEAD : HEAD + HALF] = first.astype(BF16)
    d[:, HEAD + HALF : 2 * HEAD] = second.astype(BF16)
    d[:, 2 * HEAD :] = dv[...].astype(BF16)

    sums = RingSum(net, part, passed, plus, minus, mine, other, SUBS)

    def back(step):
        at = sums.at(step)

        def body(j):
            part[at, span(j, 512)] = nt(d[at, :], aw[span(j, 512), : 3 * HEAD]).astype(BF16)

        tiles(4, body)

    back(2)
    for i in range(SUBS):
        sums.far(i)
    fs.pass_on(0)
    back(1)
    back(3)
    for i in range(SUBS):
        sums.raw(i)
        sums.add(i)
    fs.pair(0, 1)
    fs.pair(0, 0)
    back(0)

    def grad(i):
        turned = n1[:, span(i, 256)].T
        aw[span(i, 256), : 3 * HEAD] = nn(turned, d[...]).astype(BF16)
        turned = low[:, span(i, 256)].T
        aw[span(i, 256), 3 * HEAD :] = nn(turned, a[...]).astype(BF16)

    tiles(8, grad)
    ws = ShardSum(net, aw, BLOCK, agift, apassed, aplus, aminus, alast)
    fs.close(1)
    sums.cross(0)
    sums.cross(1)
    for dx in (2, 1, 3):
        for dy in (1, 0):
            ws.pair(dx, dy)
    sums.cross(2)
    sums.cross(3)
    fs.close(0)
    fblk[...] = fs.result().astype(BF16)
    fz = RingGather(net, fblk, ffull)
    saves = [net.copy(fblk, ffull.at[fz.at(0)])]
    ws.pass_on(1)
    ws.pass_on(0)
    ws.pair(0, 1)
    ws.pair(0, 0)
    for i in range(SUBS):
        sums.arrive(i)
    inputs = tok[...].astype(F32)
    upstream = mine[...].astype(F32) + other[...].astype(F32)
    factor = factor_of(inputs)
    term_one = jnp.sum(upstream * inputs * factor, 0, keepdims=True)
    term_two = term_in[...]
    row = lax.broadcasted_iota(jnp.int32, (GROWS, 128), 0)
    for s in range(16):
        cols = slice(s * 128, (s + 1) * 128)
        terms[s * GROWS : (s + 1) * GROWS, :] = jnp.where(
            row == 0, term_one[:, cols], jnp.where(row == 1, term_two[:, cols], 0.0)
        ).astype(BF16)
    gs = ShardSum(net, terms, GROWS, ggift, gpassed, gplus, gminus, glast)
    weighted = upstream * gain_row(gains, 0)
    inner = jnp.mean(weighted * inputs, -1, keepdims=True)
    dtok_o[...] = (
        dh_in[...] + (factor * weighted - inputs * (factor * factor * factor) * inner)
    ).astype(BF16)
    for dx in (2, 1, 3, 0):
        for dy in (1, 0):
            gs.pair(dx, dy)
    ws.close(1)
    gs.pass_on(1)
    gs.pass_on(0)
    ws.close(0)
    gs.close(1)
    gs.close(0)
    ablk[...] = ws.result().astype(BF16)
    az = RingGather(net, ablk, afull)
    gblk[...] = gs.result().astype(BF16)
    gz = RingGather(net, gblk, gfull)
    saves += [net.copy(ablk, afull.at[az.at(0)]), net.copy(gblk, gfull.at[gz.at(0)])]
    for shares in (fz, az, gz):
        shares.forward()
    for shares in (fz, az, gz):
        shares.left()
        shares.right()
        shares.far()
    out_push.wait_recv()
    out_copy.wait()
    for copy in saves:
        copy.wait()
    net.drain()


def call_b(low, dh, tok, cosine, sine, gains, term, outh, p, q, k, v, a, n1, aw, fgrads):
    rows_b = pltpu.VMEM((TREE, WIDTH), BF16)
    head_b = pltpu.VMEM((TREE, HEAD), BF16)
    head_f = pltpu.VMEM((TREE, HEAD), F32)
    return pl.pallas_call(
        kernel_b,
        out_shape=[
            out((ROWS, WIDTH)), out((ROWS, WIDTH)), out((4 * BLOCK, 3 * FFD)),
            out((4 * BLOCK, 4 * HEAD)), out((4 * GROWS, 128)),
        ],
        in_specs=[VM] * 8 + [ANY] * 8,
        out_specs=[VM] + [ANY] * 4,
        scratch_shapes=[
            rows_b, pltpu.VMEM((TREE, TREE), F32), head_b, head_b, head_b, head_b, rows_b,
            pltpu.VMEM((WIDTH, 4 * HEAD), BF16), head_b, pltpu.VMEM((TREE, 3 * HEAD), BF16),
            head_f, head_f,
            pltpu.VMEM((16 * GROWS, 128), BF16), pltpu.VMEM((BLOCK, 3 * FFD), BF16),
            pltpu.VMEM((BLOCK, 4 * HEAD), BF16), pltpu.VMEM((GROWS, 128), BF16),
            rows_b, *ring_sum_scratch(),
            *shard_sum_scratch(BLOCK, 3 * FFD), pltpu.VMEM((8, BLOCK, 3 * FFD), BF16),
            *shard_sum_scratch(BLOCK, 4 * HEAD), *shard_sum_scratch(GROWS, 128),
            *near_sems(144, 32),
        ],
        compiler_params=params(2),
        name="attend_back",
    )(low, dh, tok, cosine, sine, gains, term, outh, p, q, k, v, a, n1, aw, fgrads)


def kernel_e(ffn, attn, gain, query_o, key_o, value_o, wout_o, gate_o, up_o, down_o, one_o, two_o):
    z = pl.program_id(0)
    gate_o[...] = ffn[:, :FFD].astype(F32)
    up_o[...] = ffn[:, FFD : 2 * FFD].astype(F32)
    down_o[...] = ffn[:, 2 * FFD :].astype(F32).T
    query_o[...] = attn[:, :HEAD].astype(F32)
    wout_o[...] = attn[:, 3 * HEAD :].astype(F32).T

    @pl.when(lax.rem(z, 2) == 0)
    def _():
        key_o[...] = attn[:, HEAD : 2 * HEAD].astype(F32)
        value_o[...] = attn[:, 2 * HEAD : 3 * HEAD].astype(F32)

    @pl.when(lax.rem(z, 2) == 1)
    def _():
        key_o[...] += attn[:, HEAD : 2 * HEAD].astype(F32)
        value_o[...] += attn[:, 2 * HEAD : 3 * HEAD].astype(F32)

    gains = sum(gain[i * GROWS : i * GROWS + 16, :].astype(F32) for i in range(4))
    one_o[...] = gains[0:1]
    two_o[...] = gains[1:2]


def call_e(ffn, attn, gain):
    def spec(shape, place):
        return pl.BlockSpec(shape, place)

    return pl.pallas_call(
        kernel_e,
        grid=(4,),
        out_shape=[
            out((BLOCK, 4 * HEAD), F32), out((BLOCK, 2 * HEAD), F32), out((BLOCK, 2 * HEAD), F32),
            out((4 * HEAD, BLOCK), F32), out((BLOCK, 4 * FFD), F32), out((BLOCK, 4 * FFD), F32),
            out((4 * FFD, BLOCK), F32), out((1, 128), F32), out((1, 128), F32),
        ],
        in_specs=[
            spec((BLOCK, 3 * FFD), lambda z: (z, 0)), spec((BLOCK, 4 * HEAD), lambda z: (z, 0)),
            spec((4 * GROWS, 128), lambda z: (0, 0)),
        ],
        out_specs=[
            spec((BLOCK, HEAD), lambda z: (0, z)), spec((BLOCK, HEAD), lambda z: (0, z // 2)),
            spec((BLOCK, HEAD), lambda z: (0, z // 2)), spec((HEAD, BLOCK), lambda z: (z, 0)),
            spec((BLOCK, FFD), lambda z: (0, z)), spec((BLOCK, FFD), lambda z: (0, z)),
            spec((FFD, BLOCK), lambda z: (z, 0)), spec((1, 128), lambda z: (0, 0)),
            spec((1, 128), lambda z: (0, 0)),
        ],
        compiler_params=pltpu.CompilerParams(vmem_limit_bytes=60 * 1024 * 1024),
        name="widen",
    )(ffn, attn, gain)


def local(
    tokens, parents, gain_attn, w_query, key_weight, value_weight, w_out, gain_ffn, w_gate, w_up,
    w_down, cotangent,
):
    gblk = jnp.pad(jnp.stack([gain_attn, gain_ffn], 0), ((0, GROWS - 2), (0, 0)))
    frequency = jnp.asarray(
        (THETA ** (-np.arange(HALF, dtype=np.float64) * 2.0 / HEAD)).astype(np.float32)[None, :]
    )
    n1, q, k, v, a, p, hidden, n2, cosine, sine, aw, gains, fw, cf = call_a(
        tokens, cotangent, parents, frequency, gblk, w_query, key_weight, value_weight, w_out,
        w_gate, w_up, w_down,
    )
    dh, low, outh, fgrads, term = call_f(n2, hidden, fw, cf, gains)
    d_tokens, output, ffn, attn, gain = call_b(
        low, dh, tokens, cosine, sine, gains, term, outh, p, q, k, v, a, n1, aw, fgrads
    )
    query, key, value, wout, gate, up, down, one, two = call_e(ffn, attn, gain)
    return (
        output, d_tokens, one.reshape(128), query, key, value, wout, two.reshape(128), gate, up,
        down,
    )


def solution(mesh):
    rows = P(("shard", "ctx"), None)
    weight = P("shard", "tp")
    turned = P("tp", "shard")
    vector = P("shard")
    return jax.shard_map(
        local,
        mesh=mesh,
        in_specs=(
            rows, P("shard", None), vector, weight, weight, weight, turned, vector,
            weight, weight, turned, rows,
        ),
        out_specs=(
            rows, rows, vector, weight, weight, weight, turned, vector, weight, weight, turned,
        ),
        check_vma=False,
    )
```

```python
import functools
import math

import jax
import jax.numpy as jnp
import numpy as np
from jax import lax
from jax.experimental import pallas as pl
from jax.experimental.pallas import tpu as pltpu
from jax.sharding import PartitionSpec as P

HEAD = 256
HALF = HEAD // 2
SEG = 48
NSEG = 16
ROWS = 192
TREE = 768
WIDTH = 2048
FFD = 1024
BLOCK = 128
GROWS = 32
SUBS = 4

EPSILON = 1e-06
THETA = 1000042.0
NEGATIVE = -1e30
HIGHEST = lax.Precision.HIGHEST
F32 = jnp.float32
BF16 = jnp.bfloat16
MESH = pl.DeviceIdType.MESH
ANY = pl.BlockSpec(memory_space=pl.ANY)
VM = pl.BlockSpec(memory_space=pltpu.VMEM)


def nn(left, right):
    return jnp.dot(left, right, preferred_element_type=F32)


def nt(left, right):
    return lax.dot_general(left, right, (((1,), (1,)), ((), ())), preferred_element_type=F32)


def tn(left, right):
    return lax.dot_general(left, right, (((0,), (0,)), ((), ())), preferred_element_type=F32)


def ring(value, step):
    return lax.rem(value + step, 4)


class Place:
    def __init__(self):
        shard = lax.axis_index("shard")
        self.shard = shard
        self.y = shard // 8
        self.x = lax.rem(shard // 2, 4)
        self.c = lax.rem(shard, 2)
        self.z = lax.axis_index("ctx")
        self.t = lax.axis_index("tp")

    def block(self, dy=0, dx=0, dc=0):
        y = 1 - self.y if dy else self.y
        c = 1 - self.c if dc else self.c
        return y * 8 + ring(self.x, dx) * 2 + c

    def to(self, dy=0, dx=0, dc=0, dz=0, dt=0):
        t = 1 - self.t if dt else self.t
        return (self.block(dy, dx, dc), ring(self.z, dz), t)


ALL_NEAR = ("y", "x+", "x-", "c", "z+", "z-", "t")
NEAR = {
    "y": dict(dy=1), "x+": dict(dx=1), "x-": dict(dx=3), "c": dict(dc=1),
    "z+": dict(dz=1), "z-": dict(dz=3), "t": dict(dt=1),
}


class Net:
    def __init__(self, here, send, recv, local):
        self.here, self.send, self.recv, self.local = here, send, recv, local
        self.sent, self.count, self.copies = [], 0, 0

    def greet(self, names):
        barrier = pltpu.get_barrier_semaphore()
        for name in names:
            pl.semaphore_signal(
                barrier, inc=1, device_id=self.here.to(**NEAR[name]), device_id_type=MESH
            )
        pl.semaphore_wait(barrier, len(names))

    def push(self, src, dst, name):
        index = self.count
        self.count += 1
        copy = pltpu.make_async_remote_copy(
            src_ref=src,
            dst_ref=dst,
            send_sem=self.send.at[index],
            recv_sem=self.recv.at[index],
            device_id=self.here.to(**NEAR[name]),
            device_id_type=MESH,
        )
        copy.start()
        self.sent.append(copy)
        return copy

    def copy(self, src, dst):
        index = self.copies
        self.copies += 1
        copy = pltpu.make_async_copy(src, dst, self.local.at[index])
        copy.start()
        return copy

    def drain(self):
        for copy in self.sent:
            copy.wait_send()


def near_sems(remote, local):
    return [
        pltpu.SemaphoreType.DMA((remote,)),
        pltpu.SemaphoreType.DMA((remote,)),
        pltpu.SemaphoreType.DMA((local,)),
    ]


def chunk(index):
    return pl.ds(pl.multiple_of(index * ROWS, ROWS), ROWS)


class RingGather:
    def __init__(self, net, own, full, shared=False):
        self.net, self.full, self.rows, self.shared = net, full, own.shape[0], shared
        half = self.rows // 2
        one, two = own.at[pl.ds(0, half)], own.at[pl.ds(half, half)]
        width = own.shape[1] // 2
        self.cols = pl.ds(pl.multiple_of(net.here.t * width, width), width)
        near_one, near_two = self.half(0, 0), self.half(0, 1)
        self.a1 = net.push(one, near_one, "z+")
        self.b2 = net.push(two, near_two, "z-")
        if shared:
            one, two = one.at[:, self.cols], two.at[:, self.cols]
            near_one, near_two = near_one.at[:, self.cols], near_two.at[:, self.cols]
        self.a2 = net.push(two, near_two, "z+")
        self.b1 = net.push(one, near_one, "z-")

    def half(self, step, part):
        half = self.rows // 2
        start = ring(self.net.here.z, step) * self.rows + part * half
        return self.full.at[pl.ds(pl.multiple_of(start, half), half)]

    def at(self, step):
        return span(ring(self.net.here.z, step), self.rows)

    def forward(self):
        self.a1.wait_recv()
        self.f1 = self.net.push(self.half(3, 0), self.half(3, 0), "z+")
        self.b2.wait_recv()
        self.f2 = self.net.push(self.half(1, 1), self.half(1, 1), "z-")

    def share(self):
        self.a2.wait_recv()
        piece = self.half(3, 1).at[:, self.cols]
        self.a2 = self.net.push(piece, piece, "t")
        self.b1.wait_recv()
        piece = self.half(1, 0).at[:, self.cols]
        self.b1 = self.net.push(piece, piece, "t")

    def left(self):
        self.a2.wait_recv()

    def right(self):
        self.b1.wait_recv()

    def far(self):
        self.f1.wait_recv()
        self.f2.wait_recv()


class HalfGather:
    def __init__(self, net, own, full):
        width = own.shape[1] // 2
        self.net = net
        cols = pl.ds(pl.multiple_of(net.here.t * width, width), width)
        self.full = full.at[:, cols]
        self.ring = RingGather(net, own.at[:, cols], self.full)
        self.given = []

    def give(self, step):
        (None, self.ring.right, self.ring.far, self.ring.left)[step]()
        piece = self.full.at[self.ring.at(step)]
        self.given.append(self.net.push(piece, piece, "t"))

    def finish(self):
        for copy in self.given:
            copy.wait_recv()


class RingSum:
    def __init__(self, net, part, passed, plus, minus, mine, other, subs):
        self.net, self.part, self.passed = net, part, passed
        self.plus, self.minus, self.mine, self.other = plus, minus, mine, other
        width = part.shape[1] // subs
        self.cols = [
            (pl.ds(i * width, width // 2), pl.ds(i * width + width // 2, width // 2))
            for i in range(subs)
        ]
        self.subs = subs
        self.width = width
        self.e1, self.e2, self.r1, self.r2 = {}, {}, {}, {}
        self.s1, self.s2, self.t = {}, {}, {}

    def at(self, step):
        return chunk(ring(self.net.here.z, step))

    def far(self, i):
        one, two = self.cols[i]
        self.e1[i] = self.net.push(self.part.at[self.at(2), one], self.passed.at[:, one], "z+")
        self.e2[i] = self.net.push(self.part.at[self.at(2), two], self.passed.at[:, two], "z-")

    def raw(self, i):
        one, two = self.cols[i]
        self.r1[i] = self.net.push(self.part.at[self.at(1), two], self.plus.at[:, two], "z+")
        self.r2[i] = self.net.push(self.part.at[self.at(3), one], self.minus.at[:, one], "z-")

    def add(self, i):
        one, two = self.cols[i]
        part, passed = self.part, self.passed
        self.e1[i].wait_recv()
        part[self.at(1), one] = (
            part[self.at(1), one].astype(F32) + passed[:, one].astype(F32)
        ).astype(BF16)
        self.s1[i] = self.net.push(part.at[self.at(1), one], self.plus.at[:, one], "z+")
        self.e2[i].wait_recv()
        part[self.at(3), two] = (
            part[self.at(3), two].astype(F32) + passed[:, two].astype(F32)
        ).astype(BF16)
        self.s2[i] = self.net.push(part.at[self.at(3), two], self.minus.at[:, two], "z-")

    def settle(self, i):
        for copy in (self.r1[i], self.r2[i], self.s1[i], self.s2[i]):
            copy.wait_recv()

    def cross(self, i):
        self.settle(i)
        both = pl.ds(i * self.width, self.width)
        self.mine[:, both] = (
            self.part[self.at(0), both].astype(F32)
            + self.plus[:, both].astype(F32)
            + self.minus[:, both].astype(F32)
        ).astype(BF16)
        self.t[i] = self.net.push(self.mine.at[:, both], self.other.at[:, both], "t")

    def arrive(self, i):
        self.t[i].wait_recv()


class FoldedSum(RingSum):
    def __init__(self, net, part, passed, plus, minus, mine, other, fold):
        super().__init__(net, part, passed, plus, minus, mine, other, SUBS)
        self.fold = fold
        self.folds, self.cols, self.both = {}, [], []
        width = self.width
        for j in range(SUBS):
            start = lax.rem(j + (SUBS // 2) * net.here.t, SUBS) * width
            self.both.append(pl.ds(pl.multiple_of(start, width), width))
            half = width // 2
            self.cols.append(
                tuple(pl.ds(pl.multiple_of(start + k * half, half), half) for k in range(2))
            )

    def exchange(self):
        for j in range(SUBS // 2, SUBS):
            one, two = self.cols[j]
            self.folds[j] = (
                self.net.push(self.part.at[self.at(1), two], self.fold.at[:, two], "t"),
                self.net.push(self.part.at[self.at(3), one], self.fold.at[:, one], "t"),
            )

    def raw(self, j):
        for copy in self.folds[j + SUBS // 2]:
            copy.wait_recv()
        one, two = self.cols[j]
        part, fold = self.part, self.fold
        part[self.at(1), two] = part[self.at(1), two] + fold[:, two]
        part[self.at(3), one] = part[self.at(3), one] + fold[:, one]
        super().raw(j)

    def cross(self, j):
        both, (one, two) = self.both[j], self.cols[j]
        self.s1[j].wait_recv()
        self.s2[j].wait_recv()
        if j < SUBS // 2:
            self.r1[j].wait_recv()
            self.r2[j].wait_recv()
            self.mine[:, both] = (
                self.part[self.at(0), both].astype(F32)
                + self.plus[:, both].astype(F32)
                + self.minus[:, both].astype(F32)
            ).astype(BF16)
        else:
            self.mine[:, one] = self.part[self.at(0), one] + self.plus[:, one]
            self.mine[:, two] = self.part[self.at(0), two] + self.minus[:, two]
        self.t[j] = self.net.push(self.mine.at[:, both], self.other.at[:, both], "t")


def ring_sum_scratch():
    return [pltpu.VMEM((ROWS, WIDTH), BF16) for _ in range(5)]


class ShardGather:
    def __init__(self, net, own, full, rows):
        self.net, self.own, self.full, self.rows = net, own, full, rows
        self.to_sibling = []

    def at(self, part=None, **step):
        block = self.net.here.block(**step)
        if part is None:
            return self.full.at[pl.ds(pl.multiple_of(block * self.rows, self.rows), self.rows)]
        half = self.rows // 2
        start = block * self.rows + part * half
        return self.full.at[pl.ds(pl.multiple_of(start, half), half)]

    def relay(self, name, part=None, **step):
        ref = self.at(part, **step)
        return self.net.push(ref, ref, name)

    def sibling(self, part=None, **step):
        self.to_sibling.append(self.relay("c", part, **step))

    def begin(self):
        self.y0, self.p0, self.m0, c0 = (
            self.net.push(self.own, self.at(), name) for name in ("y", "x+", "x-", "c")
        )
        self.to_sibling.append(c0)

    def across(self):
        self.y0.wait_recv()
        self.p1 = self.relay("x+", dy=1)
        self.m1 = self.relay("x-", dy=1)
        self.sibling(dy=1)

    def near(self, dy):
        plus, minus = (self.p1, self.m1) if dy else (self.p0, self.m0)
        plus.wait_recv()
        fp = self.relay("x+", 0, dy=dy, dx=3)
        self.sibling(dy=dy, dx=3)
        minus.wait_recv()
        fm = self.relay("x-", 1, dy=dy, dx=1)
        self.sibling(dy=dy, dx=1)
        if dy:
            self.fp1, self.fm1 = fp, fm
        else:
            self.fp0, self.fm0 = fp, fm

    def far(self, dy):
        plus, minus = (self.fp1, self.fm1) if dy else (self.fp0, self.fm0)
        plus.wait_recv()
        self.sibling(0, dy=dy, dx=2)
        minus.wait_recv()
        self.sibling(1, dy=dy, dx=2)

    def finish(self):
        for copy in self.to_sibling:
            copy.wait_recv()


class ShardSum:
    def __init__(self, net, source, rows, gift, passed, plus, minus, last, held=None):
        self.net, self.source, self.rows, self.held = net, source, rows, held
        self.gift, self.passed, self.plus, self.minus, self.last = gift, passed, plus, minus, last
        self.gifts, self.loads = {}, {}
        for dx in (2, 1, 3, 0):
            for dy in (1, 0):
                self.gifts[dx, dy] = net.push(
                    self.block(dx, dy, 1), gift.at[2 * dx + dy], "c"
                )
                if held is not None:
                    self.loads[dx, dy] = net.copy(self.block(dx, dy, 0), held.at[2 * dx + dy])
        self.e1, self.e2, self.raw, self.sums = {}, {}, {}, {}

    def block(self, dx, dy, dc):
        return self.source.at[span(self.net.here.block(dx=dx, dy=dy, dc=dc), self.rows)]

    def kept(self, dx, dy, part=None):
        half = self.rows // 2
        if self.held is not None:
            ref = self.held.at[2 * dx + dy]
            return ref if part is None else ref.at[pl.ds(part * half, half)]
        block = self.net.here.block(dx=dx, dy=dy)
        if part is None:
            return self.source.at[span(block, self.rows)]
        return self.source.at[pl.ds(pl.multiple_of(block * self.rows + part * half, half), half)]

    def pair(self, dx, dy):
        self.gifts[dx, dy].wait_recv()
        if self.held is not None:
            self.loads[dx, dy].wait()
        ref = self.kept(dx, dy)
        ref[...] = ref[...] + self.gift[2 * dx + dy]
        half = self.rows // 2
        one, two = pl.ds(0, half), pl.ds(half, half)
        if dx == 2:
            self.e1[dy] = self.net.push(self.kept(2, dy, 0), self.passed.at[dy, one], "x+")
            self.e2[dy] = self.net.push(self.kept(2, dy, 1), self.passed.at[dy, two], "x-")
        if dx == 1:
            self.raw[1, dy] = self.net.push(self.kept(1, dy, 1), self.plus.at[dy, two], "x+")
        if dx == 3:
            self.raw[3, dy] = self.net.push(self.kept(3, dy, 0), self.minus.at[dy, one], "x-")

    def pass_on(self, dy):
        half = self.rows // 2
        one, two = pl.ds(0, half), pl.ds(half, half)
        self.e1[dy].wait_recv()
        ref = self.kept(1, dy, 0)
        ref[...] = ref[...] + self.passed[dy, one]
        self.sums[1, dy] = self.net.push(ref, self.plus.at[dy, one], "x+")
        self.e2[dy].wait_recv()
        ref = self.kept(3, dy, 1)
        ref[...] = ref[...] + self.passed[dy, two]
        self.sums[3, dy] = self.net.push(ref, self.minus.at[dy, two], "x-")

    def close(self, dy, send=True):
        for copy in (self.raw[1, dy], self.raw[3, dy], self.sums[1, dy], self.sums[3, dy]):
            copy.wait_recv()
        ref = self.kept(0, dy)
        ref[...] = (
            ref[...].astype(F32) + self.plus[dy].astype(F32) + self.minus[dy].astype(F32)
        ).astype(BF16)
        if dy and send:
            self.cross = self.net.push(ref, self.last, "y")

    def result(self):
        self.cross.wait_recv()
        return self.kept(0, 0)[...].astype(F32) + self.last[...].astype(F32)


def shard_sum_scratch(rows, width):
    def block(*lead):
        return pltpu.VMEM((*lead, rows, width), BF16)

    return [block(8), block(2), block(2), block(2), block()]


def gain_row(gains, row):
    return jnp.concatenate(
        [gains[s * GROWS : s * GROWS + 16, :][row : row + 1].astype(F32) for s in range(16)], 1
    )


def factor_of(rows):
    return lax.rsqrt(jnp.mean(rows * rows, -1, keepdims=True) + EPSILON)


def turn(rows, cosine, sine):
    first, second = rows[:, :HALF], rows[:, HALF:]
    return first * cosine - second * sine, second * cosine + first * sine


def tiles(count, body):
    def step(i, carry):
        body(i)
        return carry

    lax.fori_loop(0, count, step, 0)


def span(index, size):
    return pl.ds(pl.multiple_of(index * size, size), size)


def kernel_a(
    tok, cot, parents, frequency, gblk, wq, wk, wv, wo, wg, wu, wd,
    n1_o, q_o, k_o, v_o, a_o, p_o, h_o, n2_o, cosine, sine, aw_o, g_o, fw, cf,
    xf, n1, q, k, v, a, p, part, passed, plus, minus, mine, other, aw, gains,
    ablk, fblk, wo_s, wd_s, onehot, reach,
    send, recv, local,
):
    here = Place()
    net = Net(here, send, recv, local)
    head = span(here.z, HEAD)
    group = span(here.z // 2, HEAD)
    ff = span(here.z, FFD)
    own_a = [
        net.copy(wq.at[:, head], ablk.at[:, pl.ds(0, HEAD)]),
        net.copy(wk.at[:, group], ablk.at[:, pl.ds(HEAD, HEAD)]),
        net.copy(wv.at[:, group], ablk.at[:, pl.ds(2 * HEAD, HEAD)]),
        net.copy(wo.at[head], wo_s),
    ]
    own_f = [
        net.copy(wg.at[:, ff], fblk.at[:, pl.ds(0, FFD)]),
        net.copy(wu.at[:, ff], fblk.at[:, pl.ds(FFD, FFD)]),
        net.copy(wd.at[ff], wd_s),
    ]
    net.greet(ALL_NEAR)
    xs = RingGather(net, tok, xf)
    gg = ShardGather(net, gblk, gains, GROWS)
    gg.begin()
    for copy in own_a:
        copy.wait()
    ablk[:, 3 * HEAD :] = wo_s[...].astype(F32).T.astype(BF16)
    ag = ShardGather(net, ablk, aw, BLOCK)
    ag.begin()
    saved = [
        net.copy(ablk, ag.at()),
        net.copy(gblk, gg.at()),
        net.copy(cot, cf.at[chunk(here.z)]),
    ]
    xf[xs.at(0), :] = tok[...]
    for copy in own_f:
        copy.wait()
    fblk[:, 2 * FFD :] = wd_s[...].astype(F32).T.astype(BF16)
    gg.across()
    ag.across()
    gg.near(0)
    gg.near(1)
    ag.near(0)
    gg.far(0)
    gg.far(1)
    xs.forward()
    ag.near(1)
    feeds = [
        ShardGather(
            net,
            fblk.at[:, pl.ds(i * FFD, FFD)],
            fw.at[:, pl.ds(i * FFD, FFD)],
            BLOCK,
        )
        for i in range(3)
    ]
    cs = HalfGather(net, cot, cf)
    for fg in feeds:
        fg.begin()
        saved.append(net.copy(fg.own, fg.at()))
    steps = [
        functools.partial(step, fg, *arguments)
        for step, *arguments in (
            (ShardGather.across,), (ShardGather.near, 0), (ShardGather.near, 1),
            (ShardGather.far, 0), (ShardGather.far, 1),
        )
        for fg in feeds
    ]

    def advance(count):
        for _ in range(count):
            steps.pop(0)()

    segment = lax.broadcasted_iota(jnp.int32, (NSEG, NSEG), 0)
    links = jnp.where(parents[...] == segment, 1.0, 0.0)
    links += jnp.where(segment == lax.broadcasted_iota(jnp.int32, (NSEG, NSEG), 1), 1.0, 0.0)
    links = links.astype(BF16)
    for _ in range(4):
        links = jnp.minimum(nn(links, links), 1.0).astype(BF16)
    token = lax.broadcasted_iota(jnp.int32, (TREE, NSEG), 0)
    first = lax.broadcasted_iota(jnp.int32, (TREE, NSEG), 1) * SEG
    inside = (token >= first) & (token < first + SEG)
    members = jnp.where(inside, 1.0, 0.0)
    onehot[...] = members.astype(BF16)
    reached = nt(onehot[...], links)
    reach[...] = reached.astype(BF16)
    offset = (token[:, :1] - jnp.sum(jnp.where(inside, first, 0), -1, keepdims=True)).astype(F32)
    position = (jnp.sum(reached, -1, keepdims=True) - 1.0) * SEG + offset

    def table(i):
        rows = slice(i * ROWS, (i + 1) * ROWS)
        angles = position[rows] * frequency[...]
        cosine[rows, :] = jnp.cos(angles)
        sine[rows, :] = jnp.sin(angles)

    table(0)
    gg.finish()
    saved[0].wait()
    saved[1].wait()
    ag.far(0)
    table(1)
    ag.far(1)
    table(2)
    table(3)
    gain_one = gain_row(gains, 0)

    def normed(step):
        at = xs.at(step)
        rows = xf[at, :].astype(F32)
        n1[at, :] = (rows * factor_of(rows) * gain_one).astype(BF16)

    def project(step):
        at = xs.at(step)
        rows = n1[at, :]
        co, si = cosine[at, :], sine[at, :]
        for dst, i in ((q, 0), (k, 1)):
            first, second = turn(nn(rows, aw[:, i * HEAD : (i + 1) * HEAD]), co, si)
            dst[at, :HALF] = first.astype(BF16)
            dst[at, HALF:] = second.astype(BF16)
        v[at, :] = nn(rows, aw[:, 2 * HEAD : 3 * HEAD]).astype(BF16)

    normed(0)
    ag.finish()
    project(0)
    xs.left()
    normed(3)
    project(3)
    xs.right()
    normed(1)
    project(1)
    advance(1)
    xs.far()
    normed(2)
    project(2)
    cs.ring.forward()
    advance(2)
    out_copies = [
        net.copy(n1, n1_o), net.copy(aw, aw_o), net.copy(q, q_o), net.copy(k, k_o),
        net.copy(v, v_o), net.copy(gains, g_o),
    ]

    sums = RingSum(net, part, passed, plus, minus, mine, other, SUBS)

    def attend(step):
        at = sums.at(step)
        row = lax.broadcasted_iota(jnp.int32, (ROWS, TREE), 0) + ring(here.z, step) * ROWS
        column = lax.broadcasted_iota(jnp.int32, (ROWS, TREE), 1)
        linked = nt(reach[at, :], onehot[...])
        same = nt(onehot[at, :], onehot[...])
        allowed = (linked > 0.5) & ((same < 0.5) | (column <= row))
        scores = jnp.where(allowed, nt(q[at, :], k[...]) * (1.0 / math.sqrt(HEAD)), NEGATIVE)
        weight = jnp.exp(scores - jnp.max(scores, -1, keepdims=True))
        probs = weight / jnp.sum(weight, -1, keepdims=True)
        p[at, :] = probs
        a[at, :] = nn(probs.astype(BF16), v[...]).astype(BF16)

    def branch(step):
        at = sums.at(step)
        rows = a[at, :]

        def body(j):
            part[at, span(j, 512)] = nt(
                rows, aw[span(j, 512), 3 * HEAD : 4 * HEAD]
            ).astype(BF16)

        tiles(4, body)

    attend(2)
    branch(2)
    for i in range(SUBS):
        sums.far(i)
    cs.give(3)
    cs.give(1)
    advance(1)
    attend(1)
    branch(1)
    advance(2)
    attend(3)
    branch(3)
    for i in range(SUBS):
        sums.raw(i)
        sums.add(i)
    advance(2)
    attend(0)
    branch(0)
    out_copies += [net.copy(a, a_o), net.copy(p, p_o)]
    for i in range(SUBS):
        sums.cross(i)
        if i:
            advance(2)
    advance(1)
    for i in range(SUBS):
        sums.arrive(i)
    hidden = tok[...].astype(F32) + mine[...].astype(F32) + other[...].astype(F32)
    h_o[...] = hidden
    n2_o[...] = (hidden * factor_of(hidden) * gain_row(gains, 1)).astype(BF16)
    cs.ring.far()
    cs.finish()
    for fg in feeds:
        fg.finish()
    for copy in saved[2:] + out_copies:
        copy.wait()
    net.drain()


def out(shape, kind=BF16):
    return jax.ShapeDtypeStruct(shape, kind)


def params(number):
    return pltpu.CompilerParams(
        collective_id=number, has_side_effects=True, vmem_limit_bytes=60 * 1024 * 1024
    )


def call_a(tok, cot, parents, frequency, gblk, *weights):
    rows_b = pltpu.VMEM((TREE, WIDTH), BF16)
    head_b = pltpu.VMEM((TREE, HEAD), BF16)
    return pl.pallas_call(
        kernel_a,
        out_shape=[
            out((TREE, WIDTH)), out((TREE, HEAD)), out((TREE, HEAD)), out((TREE, HEAD)),
            out((TREE, HEAD)), out((TREE, TREE), F32), out((ROWS, WIDTH), F32),
            out((ROWS, WIDTH)), out((TREE, HALF), F32), out((TREE, HALF), F32),
            out((WIDTH, 4 * HEAD)), out((16 * GROWS, 128)),
            out((WIDTH, 3 * FFD)), out((TREE, WIDTH)),
        ],
        in_specs=[VM] * 5 + [ANY] * 7,
        out_specs=[ANY] * 6 + [VM] * 4 + [ANY] * 4,
        scratch_shapes=[
            rows_b, rows_b, head_b, head_b, head_b, head_b, pltpu.VMEM((TREE, TREE), F32), rows_b,
            *ring_sum_scratch(),
            pltpu.VMEM((WIDTH, 4 * HEAD), BF16), pltpu.VMEM((16 * GROWS, 128), BF16),
            pltpu.VMEM((BLOCK, 4 * HEAD), BF16), pltpu.VMEM((BLOCK, 3 * FFD), BF16),
            pltpu.VMEM((HEAD, BLOCK), BF16), pltpu.VMEM((FFD, BLOCK), BF16),
            pltpu.VMEM((TREE, NSEG), BF16), pltpu.VMEM((TREE, NSEG), BF16),
            *near_sems(160, 24),
        ],
        compiler_params=params(0),
        name="attend",
    )(tok, cot, parents, frequency, gblk, *weights)


def kernel_f(
    n2_in, h_in, fw, cf, gains,
    dh_o, low_o, outh_o, dsum_o, term_o, grads_o,
    w, c, n2, dgu, hid, dh_s,
    part, passed, plus, minus, mine, other,
    given, taken, part2, passed2, plus2, minus2,
    dgrad, dgift, dpassed, dplus, dminus,
    send, recv, local,
):
    here = Place()
    net = Net(here, send, recv, local)
    net.greet(ALL_NEAR)
    ns = RingGather(net, n2_in, n2)
    half = WIDTH // 2
    tp_cols = span(here.t, half)
    loads = [net.copy(fw, w)]
    loads += [net.copy(cf.at[ns.at(i)], c.at[ns.at(i)]) for i in (0, 1, 3)]
    loads.append(net.copy(cf.at[ns.at(2), tp_cols], c.at[ns.at(2), tp_cols]))
    c_far = net.push(cf.at[ns.at(2), tp_cols], c.at[ns.at(2), tp_cols], "t")
    n2[ns.at(0), :] = n2_in[...]
    for copy in loads:
        copy.wait()

    def third(j, i):
        return pl.ds(pl.multiple_of(i * FFD + j * 256, 256), 256)

    def pull(step):
        at = ns.at(step)

        def body(j):
            dh_s[at, span(j, 256)] = nn(c[at, :], w[:, third(j, 2)])

        tiles(4, body)

    def feed(step):
        at = ns.at(step)

        def body(j):
            cols = span(j, 256)
            rows = n2[at, :]
            g = nn(rows, w[:, cols])
            u = nn(rows, w[:, third(j, 1)])
            d = dh_s[at, cols]
            s = jax.nn.sigmoid(g)
            swish = g * s
            hid[at, cols] = (swish * u).astype(BF16)
            dgu[at, cols] = (d * u * s * (1.0 + g * (1.0 - s))).astype(BF16)
            dgu[at, third(j, 1)] = (d * swish).astype(BF16)

        tiles(4, body)

    def down(step, t, dst):
        at = ns.at(step)

        def body(j):
            rows = pl.ds(pl.multiple_of(t * half + j * 512, 512), 512)
            dst[at, span(j, 512)] = nt(hid[at, :], w[rows, 2 * FFD :]).astype(BF16)

        tiles(2, body)

    gifts = {}

    def give(step):
        down(step, 1 - here.t, given)
        at = ns.at(step)
        gifts[step] = net.push(given.at[at], taken.at[at], "t")

    sums = RingSum(net, part, passed, plus, minus, mine, other, SUBS)
    outs = RingSum(net, part2, passed2, plus2, minus2, None, None, 1)
    term_o[...] = jnp.zeros_like(term_o)

    def back(step, side=None):
        at = sums.at(step)
        width = WIDTH // SUBS // (1 if side is None else 2)

        def body(j):
            cols = pl.ds(pl.multiple_of(j * (WIDTH // SUBS) + (side or 0) * width, width), width)
            rows = nt(dgu[at, :], w[cols, : 2 * FFD])
            part[at, cols] = rows.astype(BF16)
            term_o[:, cols] += jnp.sum(rows * n2[at, cols].astype(F32), 0, keepdims=True)

        tiles(SUBS, body)

    def keep(step):
        down(step, here.t, part2)

    def grad(i):
        turned = n2[:, span(i, 256)].T
        for j in range(4):
            w[span(i, 256), j * 512 : (j + 1) * 512] = nn(
                turned, dgu[:, j * 512 : (j + 1) * 512]
            ).astype(BF16)

    def grad_down(i):
        turned = c[:, span(i, 256)].T
        for j in range(2):
            dgrad[span(i, 256), j * 512 : (j + 1) * 512] = nn(
                turned, hid[:, j * 512 : (j + 1) * 512]
            ).astype(BF16)

    def take(step):
        gifts[step].wait_recv()
        at = ns.at(step)
        part2[at, :] = part2[at, :] + taken[at, :]

    pull(0)
    feed(0)
    ns.forward()
    give(0)
    pull(3)
    pull(1)
    c_far.wait_recv()
    pull(2)
    ns.left()
    feed(3)
    give(3)
    ns.right()
    feed(1)
    back(1, 1)
    back(3, 0)
    for i in range(SUBS):
        sums.raw(i)
    give(1)
    ns.far()
    feed(2)
    back(2)
    for i in range(SUBS):
        sums.far(i)
    give(2)
    back(1, 0)
    back(3, 1)
    tiles(8, grad_down)
    ds = ShardSum(net, dgrad, BLOCK, dgift, dpassed, dplus, dminus, None)
    sums.add(0)
    sums.add(1)
    back(0)
    sums.add(2)
    ds.pair(2, 1)
    ds.pair(2, 0)
    sums.add(3)
    keep(2)
    sums.cross(0)
    keep(1)
    keep(3)
    sums.cross(1)
    keep(0)
    take(2)
    outs.far(0)
    sums.cross(2)
    take(1)
    take(3)
    outs.raw(0)
    for dx in (1, 3):
        for dy in (1, 0):
            ds.pair(dx, dy)
    sums.cross(3)
    tiles(3, grad)
    ds.pass_on(1)
    ds.pass_on(0)
    outs.add(0)
    tiles(5, lambda i: grad(i + 3))
    saves = [net.copy(w.at[:, pl.ds(0, 2 * FFD)], grads_o)]
    ds.pair(0, 1)
    ds.pair(0, 0)
    take(0)
    for i in range(SUBS):
        sums.arrive(i)
    gain_two = gain_row(gains, 1)
    hidden = h_in[...]
    upstream = mine[...].astype(F32) + other[...].astype(F32)
    factor = factor_of(hidden)
    weighted = upstream * gain_two
    inner = jnp.mean(weighted * hidden, -1, keepdims=True)
    dh = (
        c[ns.at(0), :].astype(F32) + factor * weighted - hidden * (factor * factor * factor) * inner
    )
    dh_o[...] = dh
    low_o[...] = dh.astype(BF16)
    term_o[...] = term_o[...] / gain_two
    outs.settle(0)
    mine_half = span(here.t, half)
    outh_o[...] = (
        h_in[:, mine_half]
        + part2[ns.at(0), :].astype(F32)
        + plus2[...].astype(F32)
        + minus2[...].astype(F32)
    ).astype(BF16)
    for dy in (0, 1):
        ds.close(dy, False)
        dsum_o[dy * BLOCK : (dy + 1) * BLOCK, :] = ds.kept(0, dy)[...]
    for copy in saves:
        copy.wait()
    net.drain()


def call_f(n2_in, h_in, fw, cf, gains):
    rows_b = pltpu.VMEM((TREE, WIDTH), BF16)
    half_b = pltpu.VMEM((TREE, WIDTH // 2), BF16)
    own_b = pltpu.VMEM((ROWS, WIDTH // 2), BF16)
    return pl.pallas_call(
        kernel_f,
        out_shape=[
            out((ROWS, WIDTH), F32), out((ROWS, WIDTH)), out((ROWS, WIDTH // 2)),
            out((2 * BLOCK, FFD)), out((1, WIDTH), F32), out((WIDTH, 2 * FFD)),
        ],
        in_specs=[VM, VM, ANY, ANY, VM],
        out_specs=[VM, VM, VM, VM, VM, ANY],
        scratch_shapes=[
            pltpu.VMEM((WIDTH, 3 * FFD), BF16), rows_b, rows_b, rows_b,
            pltpu.VMEM((TREE, FFD), BF16), pltpu.VMEM((TREE, FFD), F32),
            rows_b, *ring_sum_scratch(),
            half_b, half_b, half_b, own_b, own_b, own_b,
            pltpu.VMEM((WIDTH, FFD), BF16), *shard_sum_scratch(BLOCK, FFD)[:-1],
            *near_sems(80, 12),
        ],
        compiler_params=params(1),
        name="feed",
    )(n2_in, h_in, fw, cf, gains)


def kernel_b(
    low_in, dh_in, tok, cosine, sine, gains, term_in, outh, dsum,
    p_in, q_in, k_in, v_in, a_in, n1_in, aw_in, fgrads,
    dtok_o, out_o, gate_o, up_o, down_o, attn_o, gain_o,
    low, p, q, k, v, a, n1, aw, da, d, dk, dv, terms, gblk_f, ublk, ablk, gblk, gother, term, wgrad, dother,
    part, passed, plus, minus, mine, other,
    ggift, gpassed, gplus, gminus, glast, gheld,
    ugift, upassed, uplus, uminus, ulast, uheld,
    agift, apassed, aplus, aminus, alast,
    tgift, tpassed, tplus, tminus, tlast,
    send, recv, local,
):
    here = Place()
    net = Net(here, send, recv, local)
    net.greet(ALL_NEAR)
    ls = RingGather(net, low_in, low, True)
    loads = [
        net.copy(src, dst)
        for src, dst in (
            (aw_in, aw), (v_in, v), (p_in, p), (k_in, k), (q_in, q), (a_in, a), (n1_in, n1)
        )
    ]
    gate = ShardSum(
        net, fgrads.at[:, pl.ds(0, FFD)], BLOCK, ggift, gpassed, gplus, gminus, glast, gheld
    )
    down_push = net.push(dsum.at[pl.ds(BLOCK, BLOCK)], dother, "y")
    my_half = span(here.t, WIDTH // 2)
    out_push = net.push(outh, out_o.at[:, my_half], "t")
    saves = [net.copy(outh, out_o.at[:, my_half])]
    low[ls.at(0), :] = low_in[...]

    def attended(step):
        at = ls.at(step)
        da[at, :] = nn(low[at, :], aw[:, 3 * HEAD : 4 * HEAD]).astype(BF16)

    def attend(step):
        at = ls.at(step)
        da_rows, probs = da[at, :], p[at, :]
        dp = nt(da_rows, v[...])
        ds = probs * (dp - jnp.sum(probs * dp, -1, keepdims=True))
        draw = (ds * (1.0 / math.sqrt(HEAD))).astype(BF16)
        first, second = turn(nn(draw, k[...]), cosine[at, :], -sine[at, :])
        d[at, :HALF] = first.astype(BF16)
        d[at, HALF:HEAD] = second.astype(BF16)
        dk_more, dv_more = tn(draw, q[at, :]), tn(probs.astype(BF16), da_rows)
        if step == 0:
            dk[...] = dk_more
            dv[...] = dv_more
        else:
            dk[...] += dk_more
            dv[...] += dv_more

    loads[0].wait()
    attended(0)
    gate.pair(2, 1)
    gate.pair(2, 0)
    ls.forward()
    up = ShardSum(
        net, fgrads.at[:, pl.ds(FFD, FFD)], BLOCK, ugift, upassed, uplus, uminus, ulast, uheld
    )
    for dx in (1, 3):
        for dy in (1, 0):
            gate.pair(dx, dy)
    for copy in loads[1:]:
        copy.wait()
    attend(0)
    ls.share()
    down_push.wait_recv()
    dother[...] = (dother[...].astype(F32) + dsum[:BLOCK, :].astype(F32)).astype(BF16)
    dz = RingGather(net, dother, down_o)
    saves.append(net.copy(dother, down_o.at[dz.at(0)]))
    up.pair(2, 1)
    up.pair(2, 0)
    gate.pass_on(1)
    gate.pass_on(0)
    ls.left()
    attended(3)
    attend(3)
    for dx in (1, 3):
        for dy in (1, 0):
            up.pair(dx, dy)
    ls.right()
    attended(1)
    attend(1)
    gate.pair(0, 1)
    gate.pair(0, 0)
    dz.forward()
    ls.far()
    attended(2)
    attend(2)
    first, second = turn(dk[...], cosine[...], -sine[...])
    d[:, HEAD : HEAD + HALF] = first.astype(BF16)
    d[:, HEAD + HALF : 2 * HEAD] = second.astype(BF16)
    d[:, 2 * HEAD :] = dv[...].astype(BF16)

    sums = RingSum(net, part, passed, plus, minus, mine, other, SUBS)
    term[...] = jnp.zeros_like(term)

    def back(step):
        at = sums.at(step)

        def body(j):
            cols = span(j, 512)
            rows = nt(d[at, :], aw[cols, : 3 * HEAD])
            part[at, cols] = rows.astype(BF16)
            term[:, cols] += jnp.sum(rows * n1[at, cols].astype(F32), 0, keepdims=True)

        tiles(4, body)

    def grad(i):
        turned = n1[:, span(i, 256)].T
        wgrad[span(i, 256), : 3 * HEAD] = nn(turned, d[...]).astype(BF16)
        turned = low[:, span(i, 256)].T
        wgrad[span(i, 256), 3 * HEAD :] = nn(turned, a[...]).astype(BF16)

    back(2)
    for i in range(SUBS):
        sums.far(i)
    gate.close(1)
    up.pass_on(1)
    tiles(8, grad)
    ws = ShardSum(net, wgrad, BLOCK, agift, apassed, aplus, aminus, alast)
    gate.close(0)
    up.pass_on(0)
    back(1)
    back(3)
    for i in range(SUBS):
        sums.raw(i)
        sums.add(i)
    back(0)
    gblk_f[...] = gate.result().astype(BF16)
    gz = RingGather(net, gblk_f, gate_o)
    saves.append(net.copy(gblk_f, gate_o.at[gz.at(0)]))
    gain_one = gain_row(gains, 0)
    term_one = term[...] / gain_one
    term_two = term_in[...]
    row = lax.broadcasted_iota(jnp.int32, (GROWS, 128), 0)
    for s in range(16):
        cols = slice(s * 128, (s + 1) * 128)
        terms[s * GROWS : (s + 1) * GROWS, :] = jnp.where(
            row == 0, term_one[:, cols], jnp.where(row == 1, term_two[:, cols], 0.0)
        ).astype(BF16)
    ts = ShardSum(net, terms, GROWS, tgift, tpassed, tplus, tminus, tlast)
    up.pair(0, 1)
    up.pair(0, 0)
    up.close(1)
    for shares in (ws, ts):
        for dx in (2, 1, 3):
            for dy in (1, 0):
                shares.pair(dx, dy)
    sums.cross(0)
    sums.cross(1)
    gz.forward()
    up.close(0)
    for shares in (ws, ts):
        for dy in (1, 0):
            shares.pair(0, dy)
    ublk[...] = up.result().astype(BF16)
    uz = RingGather(net, ublk, up_o)
    saves.append(net.copy(ublk, up_o.at[uz.at(0)]))
    sums.cross(2)
    for shares in (ws, ts):
        for dy in (1, 0):
            shares.pass_on(dy)
    sums.cross(3)
    uz.forward()
    for dy in (1, 0):
        for shares in (ws, ts):
            shares.close(dy)
    for i in range(SUBS):
        sums.arrive(i)
    inputs = tok[...].astype(F32)
    upstream = mine[...].astype(F32) + other[...].astype(F32)
    factor = factor_of(inputs)
    weighted = upstream * gain_one
    inner = jnp.mean(weighted * inputs, -1, keepdims=True)
    dtok_o[...] = (
        dh_in[...] + (factor * weighted - inputs * (factor * factor * factor) * inner)
    ).astype(BF16)
    gblk[...] = ts.result().astype(BF16)
    cross = net.push(gblk, gother, "t")
    ablk[...] = ws.result().astype(BF16)
    az = RingGather(net, ablk, attn_o)
    saves.append(net.copy(ablk, attn_o.at[az.at(0)]))
    cross.wait_recv()
    gother[...] = (gblk[...].astype(F32) + gother[...].astype(F32)).astype(BF16)
    tz = RingGather(net, gother, gain_o)
    saves.append(net.copy(gother, gain_o.at[tz.at(0)]))
    for shares in (az, tz):
        shares.forward()
    for shares in (dz, gz, uz, az, tz):
        shares.left()
        shares.right()
        shares.far()
    out_push.wait_recv()
    for copy in saves:
        copy.wait()
    net.drain()


def call_b(low, dh, tok, cosine, sine, gains, term, outh, dsum, *rest):
    rows_b = pltpu.VMEM((TREE, WIDTH), BF16)
    head_b = pltpu.VMEM((TREE, HEAD), BF16)
    head_f = pltpu.VMEM((TREE, HEAD), F32)
    ffn_b = pltpu.VMEM((BLOCK, FFD), BF16)
    held = pltpu.VMEM((8, BLOCK, FFD), BF16)
    gain_b = pltpu.VMEM((GROWS, 128), BF16)
    full = out((4 * BLOCK, FFD))
    return pl.pallas_call(
        kernel_b,
        out_shape=[
            out((ROWS, WIDTH)), out((ROWS, WIDTH)), full, full, full, full, out((4 * GROWS, 128)),
        ],
        in_specs=[VM] * 9 + [ANY] * 8,
        out_specs=[VM] + [ANY] * 6,
        scratch_shapes=[
            rows_b, pltpu.VMEM((TREE, TREE), F32), head_b, head_b, head_b, head_b, rows_b,
            pltpu.VMEM((WIDTH, 4 * HEAD), BF16), head_b, pltpu.VMEM((TREE, 3 * HEAD), BF16),
            head_f, head_f,
            pltpu.VMEM((16 * GROWS, 128), BF16), ffn_b, ffn_b, ffn_b, gain_b, gain_b,
            pltpu.VMEM((1, WIDTH), F32), pltpu.VMEM((WIDTH, 4 * HEAD), BF16), ffn_b,
            rows_b, *ring_sum_scratch(),
            *shard_sum_scratch(BLOCK, FFD), held,
            *shard_sum_scratch(BLOCK, FFD), held,
            *shard_sum_scratch(BLOCK, 4 * HEAD), *shard_sum_scratch(GROWS, 128),
            *near_sems(176, 40),
        ],
        compiler_params=params(2),
        name="attend_back",
    )(low, dh, tok, cosine, sine, gains, term, outh, dsum, *rest)


def kernel_e(gate, up, down, attn, gain, query_o, key_o, value_o, wout_o, gate_o, up_o, down_o, one_o, two_o):
    z = pl.program_id(0)
    gate_o[...] = gate[...].astype(F32)
    up_o[...] = up[...].astype(F32)
    down_o[...] = down[...].astype(F32).T
    query_o[...] = attn[:, :HEAD].astype(F32)
    wout_o[...] = attn[:, 3 * HEAD :].astype(F32).T

    @pl.when(lax.rem(z, 2) == 0)
    def _():
        key_o[...] = attn[:, HEAD : 2 * HEAD].astype(F32)
        value_o[...] = attn[:, 2 * HEAD : 3 * HEAD].astype(F32)

    @pl.when(lax.rem(z, 2) == 1)
    def _():
        key_o[...] += attn[:, HEAD : 2 * HEAD].astype(F32)
        value_o[...] += attn[:, 2 * HEAD : 3 * HEAD].astype(F32)

    gains = sum(gain[i * GROWS : i * GROWS + 16, :].astype(F32) for i in range(4))
    one_o[...] = gains[0:1]
    two_o[...] = gains[1:2]


def call_e(*blocks):
    def spec(shape, place):
        return pl.BlockSpec(shape, place)

    return pl.pallas_call(
        kernel_e,
        grid=(4,),
        out_shape=[
            out((BLOCK, 4 * HEAD), F32), out((BLOCK, 2 * HEAD), F32), out((BLOCK, 2 * HEAD), F32),
            out((4 * HEAD, BLOCK), F32), out((BLOCK, 4 * FFD), F32), out((BLOCK, 4 * FFD), F32),
            out((4 * FFD, BLOCK), F32), out((1, 128), F32), out((1, 128), F32),
        ],
        in_specs=[
            *[spec((BLOCK, FFD), lambda z: (z, 0))] * 4,
            spec((4 * GROWS, 128), lambda z: (0, 0)),
        ],
        out_specs=[
            spec((BLOCK, HEAD), lambda z: (0, z)), spec((BLOCK, HEAD), lambda z: (0, z // 2)),
            spec((BLOCK, HEAD), lambda z: (0, z // 2)), spec((HEAD, BLOCK), lambda z: (z, 0)),
            spec((BLOCK, FFD), lambda z: (0, z)), spec((BLOCK, FFD), lambda z: (0, z)),
            spec((FFD, BLOCK), lambda z: (z, 0)), spec((1, 128), lambda z: (0, 0)),
            spec((1, 128), lambda z: (0, 0)),
        ],
        compiler_params=pltpu.CompilerParams(vmem_limit_bytes=60 * 1024 * 1024),
        name="widen",
    )(*blocks)


def local(
    tokens, parents, gain_attn, w_query, key_weight, value_weight, w_out, gain_ffn, w_gate, w_up,
    w_down, cotangent,
):
    gblk = jnp.pad(jnp.stack([gain_attn, gain_ffn], 0), ((0, GROWS - 2), (0, 0)))
    frequency = jnp.asarray(
        (THETA ** (-np.arange(HALF, dtype=np.float64) * 2.0 / HEAD)).astype(np.float32)[None, :]
    )
    n1, q, k, v, a, p, hidden, n2, cosine, sine, aw, gains, fw, cf = call_a(
        tokens, cotangent, parents, frequency, gblk, w_query, key_weight, value_weight, w_out,
        w_gate, w_up, w_down,
    )
    dh, low, outh, dsum, term, fgrads = call_f(n2, hidden, fw, cf, gains)
    d_tokens, output, gate, up, down, attn, gain = call_b(
        low, dh, tokens, cosine, sine, gains, term, outh, dsum, p, q, k, v, a, n1, aw, fgrads
    )
    query, key, value, wout, gate, up, down, one, two = call_e(gate, up, down, attn, gain)
    return (
        output, d_tokens, one.reshape(128), query, key, value, wout, two.reshape(128), gate, up,
        down,
    )


def solution(mesh):
    rows = P(("shard", "ctx"), None)
    weight = P("shard", "tp")
    turned = P("tp", "shard")
    vector = P("shard")
    return jax.shard_map(
        local,
        mesh=mesh,
        in_specs=(
            rows, P("shard", None), vector, weight, weight, weight, turned, vector,
            weight, weight, turned, rows,
        ),
        out_specs=(
            rows, rows, vector, weight, weight, weight, turned, vector, weight, weight, turned,
        ),
        check_vma=False,
    )
```

```python
import functools
import math

import jax
import jax.numpy as jnp
import numpy as np
from jax import lax
from jax.experimental import pallas as pl
from jax.experimental.pallas import tpu as pltpu
from jax.sharding import PartitionSpec as P

HEAD = 256
HALF = HEAD // 2
SEG = 48
NSEG = 16
ROWS = 192
TREE = 768
WIDTH = 2048
FFD = 1024
BLOCK = 128
GROWS = 32
SUBS = 4

EPSILON = 1e-06
THETA = 1000042.0
NEGATIVE = -1e30
HIGHEST = lax.Precision.HIGHEST
F32 = jnp.float32
BF16 = jnp.bfloat16
MESH = pl.DeviceIdType.MESH
ANY = pl.BlockSpec(memory_space=pl.ANY)
VM = pl.BlockSpec(memory_space=pltpu.VMEM)


def nn(left, right):
    return jnp.dot(left, right, preferred_element_type=F32)


def nt(left, right):
    return lax.dot_general(left, right, (((1,), (1,)), ((), ())), preferred_element_type=F32)


def tn(left, right):
    return lax.dot_general(left, right, (((0,), (0,)), ((), ())), preferred_element_type=F32)


def ring(value, step):
    return lax.rem(value + step, 4)


class Place:
    def __init__(self):
        shard = lax.axis_index("shard")
        self.shard = shard
        self.y = shard // 8
        self.x = lax.rem(shard // 2, 4)
        self.c = lax.rem(shard, 2)
        self.z = lax.axis_index("ctx")
        self.t = lax.axis_index("tp")

    def block(self, dy=0, dx=0, dc=0):
        y = 1 - self.y if dy else self.y
        c = 1 - self.c if dc else self.c
        return y * 8 + ring(self.x, dx) * 2 + c

    def to(self, dy=0, dx=0, dc=0, dz=0, dt=0):
        t = 1 - self.t if dt else self.t
        return (self.block(dy, dx, dc), ring(self.z, dz), t)


ALL_NEAR = ("y", "x+", "x-", "c", "z+", "z-", "t")
NEAR = {
    "y": dict(dy=1), "x+": dict(dx=1), "x-": dict(dx=3), "c": dict(dc=1),
    "z+": dict(dz=1), "z-": dict(dz=3), "t": dict(dt=1),
}


class Net:
    def __init__(self, here, send, recv, local):
        self.here, self.send, self.recv, self.local = here, send, recv, local
        self.sent, self.count, self.copies = [], 0, 0

    def greet(self, names):
        barrier = pltpu.get_barrier_semaphore()
        for name in names:
            pl.semaphore_signal(
                barrier, inc=1, device_id=self.here.to(**NEAR[name]), device_id_type=MESH
            )
        pl.semaphore_wait(barrier, len(names))

    def push(self, src, dst, name):
        index = self.count
        self.count += 1
        copy = pltpu.make_async_remote_copy(
            src_ref=src,
            dst_ref=dst,
            send_sem=self.send.at[index],
            recv_sem=self.recv.at[index],
            device_id=self.here.to(**NEAR[name]),
            device_id_type=MESH,
        )
        copy.start()
        self.sent.append(copy)
        return copy

    def copy(self, src, dst):
        index = self.copies
        self.copies += 1
        copy = pltpu.make_async_copy(src, dst, self.local.at[index])
        copy.start()
        return copy

    def drain(self):
        for copy in self.sent:
            copy.wait_send()


def rows_toward(here, dx, body):
    tiles(2, lambda j: body(lax.rem(here.y + 1 + j, 2) * 4 + ring(here.x, dx)))


def near_sems(remote, local):
    return [
        pltpu.SemaphoreType.DMA((remote,)),
        pltpu.SemaphoreType.DMA((remote,)),
        pltpu.SemaphoreType.DMA((local,)),
    ]


def chunk(index):
    return pl.ds(pl.multiple_of(index * ROWS, ROWS), ROWS)


class RingGather:
    def __init__(self, net, own, full, shared=False):
        self.net, self.full, self.rows, self.shared = net, full, own.shape[0], shared
        half = self.rows // 2
        one, two = own.at[pl.ds(0, half)], own.at[pl.ds(half, half)]
        width = own.shape[1] // 2
        self.cols = pl.ds(pl.multiple_of(net.here.t * width, width), width)
        near_one, near_two = self.half(0, 0), self.half(0, 1)
        self.a1 = net.push(one, near_one, "z+")
        self.b2 = net.push(two, near_two, "z-")
        if shared:
            one, two = one.at[:, self.cols], two.at[:, self.cols]
            near_one, near_two = near_one.at[:, self.cols], near_two.at[:, self.cols]
        self.a2 = net.push(two, near_two, "z+")
        self.b1 = net.push(one, near_one, "z-")

    def half(self, step, part):
        half = self.rows // 2
        start = ring(self.net.here.z, step) * self.rows + part * half
        return self.full.at[pl.ds(pl.multiple_of(start, half), half)]

    def at(self, step):
        return span(ring(self.net.here.z, step), self.rows)

    def forward(self):
        self.a1.wait_recv()
        self.f1 = self.net.push(self.half(3, 0), self.half(3, 0), "z+")
        self.b2.wait_recv()
        self.f2 = self.net.push(self.half(1, 1), self.half(1, 1), "z-")

    def share(self):
        self.a2.wait_recv()
        piece = self.half(3, 1).at[:, self.cols]
        self.a2 = self.net.push(piece, piece, "t")
        self.b1.wait_recv()
        piece = self.half(1, 0).at[:, self.cols]
        self.b1 = self.net.push(piece, piece, "t")

    def left(self):
        self.a2.wait_recv()

    def right(self):
        self.b1.wait_recv()

    def far(self):
        self.f1.wait_recv()
        self.f2.wait_recv()


class HalfGather:
    def __init__(self, net, own, full):
        width = own.shape[1] // 2
        self.net = net
        cols = pl.ds(pl.multiple_of(net.here.t * width, width), width)
        self.full = full.at[:, cols]
        self.ring = RingGather(net, own.at[:, cols], self.full)
        self.given = []

    def give(self, step):
        (None, self.ring.right, self.ring.far, self.ring.left)[step]()
        piece = self.full.at[self.ring.at(step)]
        self.given.append(self.net.push(piece, piece, "t"))

    def finish(self):
        for copy in self.given:
            copy.wait_recv()


class RingSum:
    def __init__(self, net, part, passed, plus, minus, mine, other, subs):
        self.net, self.part, self.passed = net, part, passed
        self.plus, self.minus, self.mine, self.other = plus, minus, mine, other
        width = part.shape[1] // subs
        self.cols = [
            (pl.ds(i * width, width // 2), pl.ds(i * width + width // 2, width // 2))
            for i in range(subs)
        ]
        self.subs = subs
        self.width = width
        self.e1, self.e2, self.r1, self.r2 = {}, {}, {}, {}
        self.s1, self.s2, self.t = {}, {}, {}

    def at(self, step):
        return chunk(ring(self.net.here.z, step))

    def far(self, i):
        one, two = self.cols[i]
        self.e1[i] = self.net.push(self.part.at[self.at(2), one], self.passed.at[:, one], "z+")
        self.e2[i] = self.net.push(self.part.at[self.at(2), two], self.passed.at[:, two], "z-")

    def raw(self, i):
        one, two = self.cols[i]
        self.r1[i] = self.net.push(self.part.at[self.at(1), two], self.plus.at[:, two], "z+")
        self.r2[i] = self.net.push(self.part.at[self.at(3), one], self.minus.at[:, one], "z-")

    def add(self, i):
        one, two = self.cols[i]
        part, passed = self.part, self.passed
        self.e1[i].wait_recv()
        part[self.at(1), one] = (
            part[self.at(1), one].astype(F32) + passed[:, one].astype(F32)
        ).astype(BF16)
        self.s1[i] = self.net.push(part.at[self.at(1), one], self.plus.at[:, one], "z+")
        self.e2[i].wait_recv()
        part[self.at(3), two] = (
            part[self.at(3), two].astype(F32) + passed[:, two].astype(F32)
        ).astype(BF16)
        self.s2[i] = self.net.push(part.at[self.at(3), two], self.minus.at[:, two], "z-")

    def settle(self, i):
        for copy in (self.r1[i], self.r2[i], self.s1[i], self.s2[i]):
            copy.wait_recv()

    def cross(self, i):
        self.settle(i)
        both = pl.ds(i * self.width, self.width)
        self.mine[:, both] = (
            self.part[self.at(0), both].astype(F32)
            + self.plus[:, both].astype(F32)
            + self.minus[:, both].astype(F32)
        ).astype(BF16)
        self.t[i] = self.net.push(self.mine.at[:, both], self.other.at[:, both], "t")

    def arrive(self, i):
        self.t[i].wait_recv()


class FoldedSum(RingSum):
    def __init__(self, net, part, passed, plus, minus, mine, other, fold):
        super().__init__(net, part, passed, plus, minus, mine, other, SUBS)
        self.fold = fold
        self.folds, self.cols, self.both = {}, [], []
        width = self.width
        for j in range(SUBS):
            start = lax.rem(j + (SUBS // 2) * net.here.t, SUBS) * width
            self.both.append(pl.ds(pl.multiple_of(start, width), width))
            half = width // 2
            self.cols.append(
                tuple(pl.ds(pl.multiple_of(start + k * half, half), half) for k in range(2))
            )

    def exchange(self):
        for j in range(SUBS // 2, SUBS):
            one, two = self.cols[j]
            self.folds[j] = (
                self.net.push(self.part.at[self.at(1), two], self.fold.at[:, two], "t"),
                self.net.push(self.part.at[self.at(3), one], self.fold.at[:, one], "t"),
            )

    def raw(self, j):
        for copy in self.folds[j + SUBS // 2]:
            copy.wait_recv()
        one, two = self.cols[j]
        part, fold = self.part, self.fold
        part[self.at(1), two] = part[self.at(1), two] + fold[:, two]
        part[self.at(3), one] = part[self.at(3), one] + fold[:, one]
        super().raw(j)

    def cross(self, j):
        both, (one, two) = self.both[j], self.cols[j]
        self.s1[j].wait_recv()
        self.s2[j].wait_recv()
        if j < SUBS // 2:
            self.r1[j].wait_recv()
            self.r2[j].wait_recv()
            self.mine[:, both] = (
                self.part[self.at(0), both].astype(F32)
                + self.plus[:, both].astype(F32)
                + self.minus[:, both].astype(F32)
            ).astype(BF16)
        else:
            self.mine[:, one] = self.part[self.at(0), one] + self.plus[:, one]
            self.mine[:, two] = self.part[self.at(0), two] + self.minus[:, two]
        self.t[j] = self.net.push(self.mine.at[:, both], self.other.at[:, both], "t")


def ring_sum_scratch():
    return [pltpu.VMEM((ROWS, WIDTH), BF16) for _ in range(5)]


class ShardGather:
    def __init__(self, net, own, full, rows):
        self.net, self.own, self.full, self.rows = net, own, full, rows
        self.to_sibling = []

    def at(self, part=None, **step):
        block = self.net.here.block(**step)
        if part is None:
            return self.full.at[pl.ds(pl.multiple_of(block * self.rows, self.rows), self.rows)]
        half = self.rows // 2
        start = block * self.rows + part * half
        return self.full.at[pl.ds(pl.multiple_of(start, half), half)]

    def relay(self, name, part=None, **step):
        ref = self.at(part, **step)
        return self.net.push(ref, ref, name)

    def sibling(self, part=None, **step):
        self.to_sibling.append(self.relay("c", part, **step))

    def begin(self):
        self.y0, self.p0, self.m0, c0 = (
            self.net.push(self.own, self.at(), name) for name in ("y", "x+", "x-", "c")
        )
        self.to_sibling.append(c0)

    def across(self):
        self.y0.wait_recv()
        self.p1 = self.relay("x+", dy=1)
        self.m1 = self.relay("x-", dy=1)
        self.sibling(dy=1)

    def near(self, dy):
        plus, minus = (self.p1, self.m1) if dy else (self.p0, self.m0)
        plus.wait_recv()
        fp = self.relay("x+", 0, dy=dy, dx=3)
        self.sibling(dy=dy, dx=3)
        minus.wait_recv()
        fm = self.relay("x-", 1, dy=dy, dx=1)
        self.sibling(dy=dy, dx=1)
        if dy:
            self.fp1, self.fm1 = fp, fm
        else:
            self.fp0, self.fm0 = fp, fm

    def far(self, dy):
        plus, minus = (self.fp1, self.fm1) if dy else (self.fp0, self.fm0)
        plus.wait_recv()
        self.sibling(0, dy=dy, dx=2)
        minus.wait_recv()
        self.sibling(1, dy=dy, dx=2)

    def finish(self):
        for copy in self.to_sibling:
            copy.wait_recv()


class ShardSum:
    def __init__(
        self, net, source, rows, gift, passed, plus, minus, last, held=None, whole=True
    ):
        self.net, self.source, self.rows, self.held = net, source, rows, held
        self.gift, self.passed, self.plus, self.minus, self.last = gift, passed, plus, minus, last
        self.gifts, self.loads = {}, {}
        self.e1, self.e2, self.raw, self.sums = {}, {}, {}, {}
        if whole:
            for dx in (2, 1, 3, 0):
                self.offer(dx)

    def offer(self, dx):
        for dy in (1, 0):
            self.gifts[dx, dy] = self.net.push(
                self.block(dx, dy, 1), self.gift.at[2 * dx + dy], "c"
            )
            if self.held is not None:
                self.loads[dx, dy] = self.net.copy(
                    self.block(dx, dy, 0), self.held.at[2 * dx + dy]
                )

    def block(self, dx, dy, dc):
        return self.source.at[span(self.net.here.block(dx=dx, dy=dy, dc=dc), self.rows)]

    def kept(self, dx, dy, part=None):
        half = self.rows // 2
        if self.held is not None:
            ref = self.held.at[2 * dx + dy]
            return ref if part is None else ref.at[pl.ds(part * half, half)]
        block = self.net.here.block(dx=dx, dy=dy)
        if part is None:
            return self.source.at[span(block, self.rows)]
        return self.source.at[pl.ds(pl.multiple_of(block * self.rows + part * half, half), half)]

    def pair(self, dx, dy):
        self.gifts[dx, dy].wait_recv()
        if self.held is not None:
            self.loads[dx, dy].wait()
        ref = self.kept(dx, dy)
        ref[...] = ref[...] + self.gift[2 * dx + dy]
        half = self.rows // 2
        one, two = pl.ds(0, half), pl.ds(half, half)
        if dx == 2:
            self.e1[dy] = self.net.push(self.kept(2, dy, 0), self.passed.at[dy, one], "x+")
            self.e2[dy] = self.net.push(self.kept(2, dy, 1), self.passed.at[dy, two], "x-")
        if dx == 1:
            self.raw[1, dy] = self.net.push(self.kept(1, dy, 1), self.plus.at[dy, two], "x+")
        if dx == 3:
            self.raw[3, dy] = self.net.push(self.kept(3, dy, 0), self.minus.at[dy, one], "x-")

    def pass_on(self, dy):
        half = self.rows // 2
        one, two = pl.ds(0, half), pl.ds(half, half)
        self.e1[dy].wait_recv()
        ref = self.kept(1, dy, 0)
        ref[...] = ref[...] + self.passed[dy, one]
        self.sums[1, dy] = self.net.push(ref, self.plus.at[dy, one], "x+")
        self.e2[dy].wait_recv()
        ref = self.kept(3, dy, 1)
        ref[...] = ref[...] + self.passed[dy, two]
        self.sums[3, dy] = self.net.push(ref, self.minus.at[dy, two], "x-")

    def close(self, dy, send=True):
        for copy in (self.raw[1, dy], self.raw[3, dy], self.sums[1, dy], self.sums[3, dy]):
            copy.wait_recv()
        ref = self.kept(0, dy)
        ref[...] = (
            ref[...].astype(F32) + self.plus[dy].astype(F32) + self.minus[dy].astype(F32)
        ).astype(BF16)
        if dy and send:
            self.cross = self.net.push(ref, self.last, "y")

    def result(self):
        self.cross.wait_recv()
        return self.kept(0, 0)[...].astype(F32) + self.last[...].astype(F32)


def shard_sum_scratch(rows, width):
    def block(*lead):
        return pltpu.VMEM((*lead, rows, width), BF16)

    return [block(8), block(2), block(2), block(2), block()]


def gain_row(gains, row):
    return jnp.concatenate(
        [gains[s * GROWS : s * GROWS + 16, :][row : row + 1].astype(F32) for s in range(16)], 1
    )


def factor_of(rows):
    return lax.rsqrt(jnp.mean(rows * rows, -1, keepdims=True) + EPSILON)


def turn(rows, cosine, sine):
    first, second = rows[:, :HALF], rows[:, HALF:]
    return first * cosine - second * sine, second * cosine + first * sine


def tiles(count, body):
    def step(i, carry):
        body(i)
        return carry

    lax.fori_loop(0, count, step, 0)


def span(index, size):
    return pl.ds(pl.multiple_of(index * size, size), size)


def kernel_a(
    tok, cot, parents, frequency, gone, gtwo, wq, wk, wv, wo, wg, wu, wd,
    n1_o, q_o, k_o, v_o, a_o, p_o, h_o, n2_o, co_o, si_o, aw_o, g_o, fw, cf,
    xf, n1, q, k, v, a, p, part, passed, plus, minus, mine, other, aw, gains,
    ablk, fblk, wo_s, wd_s, onehot, reach, cosine, sine, gblk,
    send, recv, local,
):
    here = Place()
    net = Net(here, send, recv, local)
    head = span(here.z, HEAD)
    group = span(here.z // 2, HEAD)
    ff = span(here.z, FFD)
    own_a = [
        net.copy(wq.at[:, head], ablk.at[:, pl.ds(0, HEAD)]),
        net.copy(wk.at[:, group], ablk.at[:, pl.ds(HEAD, HEAD)]),
        net.copy(wv.at[:, group], ablk.at[:, pl.ds(2 * HEAD, HEAD)]),
        net.copy(wo.at[head], wo_s),
    ]
    own_f = [
        net.copy(wg.at[:, ff], fblk.at[:, pl.ds(0, FFD)]),
        net.copy(wu.at[:, ff], fblk.at[:, pl.ds(FFD, FFD)]),
        net.copy(wd.at[ff], wd_s),
    ]
    row = lax.broadcasted_iota(jnp.int32, (GROWS, 128), 0)
    gblk[...] = jnp.where(
        row == 0, gone[...].astype(F32), jnp.where(row == 1, gtwo[...].astype(F32), 0.0)
    ).astype(BF16)
    net.greet(ALL_NEAR)
    xs = RingGather(net, tok, xf)
    gg = ShardGather(net, gblk, gains, GROWS)
    gg.begin()
    for copy in own_a:
        copy.wait()
    ablk[:, 3 * HEAD :] = wo_s[...].astype(F32).T.astype(BF16)
    ag = ShardGather(net, ablk, aw, BLOCK)
    ag.begin()
    saved = [
        net.copy(ablk, ag.at()),
        net.copy(gblk, gg.at()),
        net.copy(cot, cf.at[chunk(here.z)]),
    ]
    xf[xs.at(0), :] = tok[...]
    for copy in own_f:
        copy.wait()
    fblk[:, 2 * FFD :] = wd_s[...].astype(F32).T.astype(BF16)
    gg.across()
    ag.across()
    gg.near(0)
    gg.near(1)
    ag.near(0)
    gg.far(0)
    gg.far(1)
    xs.forward()
    ag.near(1)
    feeds = [
        ShardGather(
            net,
            fblk.at[:, pl.ds(i * FFD, FFD)],
            fw.at[:, pl.ds(i * FFD, FFD)],
            BLOCK,
        )
        for i in range(3)
    ]
    cs = HalfGather(net, cot, cf)
    for fg in feeds:
        fg.begin()
        saved.append(net.copy(fg.own, fg.at()))
    steps = [
        functools.partial(step, fg, *arguments)
        for step, *arguments in (
            (ShardGather.across,), (ShardGather.near, 0), (ShardGather.near, 1),
            (ShardGather.far, 0), (ShardGather.far, 1),
        )
        for fg in feeds
    ]

    def advance(count):
        for _ in range(count):
            steps.pop(0)()

    segment = lax.broadcasted_iota(jnp.int32, (NSEG, NSEG), 0)
    links = jnp.where(parents[...] == segment, 1.0, 0.0)
    links += jnp.where(segment == lax.broadcasted_iota(jnp.int32, (NSEG, NSEG), 1), 1.0, 0.0)
    links = links.astype(BF16)
    for _ in range(4):
        links = jnp.minimum(nn(links, links), 1.0).astype(BF16)
    token = lax.broadcasted_iota(jnp.int32, (TREE, NSEG), 0)
    first = lax.broadcasted_iota(jnp.int32, (TREE, NSEG), 1) * SEG
    inside = (token >= first) & (token < first + SEG)
    members = jnp.where(inside, 1.0, 0.0)
    onehot[...] = members.astype(BF16)
    reached = nt(onehot[...], links)
    reach[...] = reached.astype(BF16)
    offset = (token[:, :1] - jnp.sum(jnp.where(inside, first, 0), -1, keepdims=True)).astype(F32)
    position = (jnp.sum(reached, -1, keepdims=True) - 1.0) * SEG + offset

    def table(i):
        rows = slice(i * ROWS, (i + 1) * ROWS)
        angles = position[rows] * frequency[...]
        cosine[rows, :] = jnp.cos(angles)
        sine[rows, :] = jnp.sin(angles)

    table(0)
    gg.finish()
    saved[0].wait()
    saved[1].wait()
    ag.far(0)
    table(1)
    ag.far(1)
    table(2)
    table(3)
    saved += [net.copy(cosine, co_o), net.copy(sine, si_o)]
    gain_one = gain_row(gains, 0)

    def normed(step):
        at = xs.at(step)
        rows = xf[at, :].astype(F32)
        n1[at, :] = (rows * factor_of(rows) * gain_one).astype(BF16)

    def project(step):
        at = xs.at(step)
        rows = n1[at, :]
        co, si = cosine[at, :], sine[at, :]
        for dst, i in ((q, 0), (k, 1)):
            first, second = turn(nn(rows, aw[:, i * HEAD : (i + 1) * HEAD]), co, si)
            dst[at, :HALF] = first.astype(BF16)
            dst[at, HALF:] = second.astype(BF16)
        v[at, :] = nn(rows, aw[:, 2 * HEAD : 3 * HEAD]).astype(BF16)

    normed(0)
    ag.finish()
    project(0)
    xs.left()
    normed(3)
    project(3)
    xs.right()
    normed(1)
    project(1)
    advance(1)
    xs.far()
    normed(2)
    project(2)
    cs.ring.forward()
    advance(2)
    out_copies = [
        net.copy(n1, n1_o), net.copy(aw, aw_o), net.copy(q, q_o), net.copy(k, k_o),
        net.copy(v, v_o), net.copy(gains, g_o),
    ]

    sums = RingSum(net, part, passed, plus, minus, mine, other, SUBS)

    def attend(step):
        at = sums.at(step)
        row = lax.broadcasted_iota(jnp.int32, (ROWS, TREE), 0) + ring(here.z, step) * ROWS
        column = lax.broadcasted_iota(jnp.int32, (ROWS, TREE), 1)
        linked = nt(reach[at, :], onehot[...])
        same = nt(onehot[at, :], onehot[...])
        allowed = (linked > 0.5) & ((same < 0.5) | (column <= row))
        scores = jnp.where(allowed, nt(q[at, :], k[...]) * (1.0 / math.sqrt(HEAD)), NEGATIVE)
        weight = jnp.exp(scores - jnp.max(scores, -1, keepdims=True))
        probs = weight / jnp.sum(weight, -1, keepdims=True)
        p[at, :] = probs
        a[at, :] = nn(probs.astype(BF16), v[...]).astype(BF16)

    def branch(step):
        at = sums.at(step)
        rows = a[at, :]

        def body(j):
            part[at, span(j, 512)] = nt(
                rows, aw[span(j, 512), 3 * HEAD : 4 * HEAD]
            ).astype(BF16)

        tiles(4, body)

    attend(2)
    branch(2)
    for i in range(SUBS):
        sums.far(i)
    cs.give(3)
    cs.give(1)
    advance(1)
    attend(1)
    branch(1)
    advance(2)
    attend(3)
    branch(3)
    for i in range(SUBS):
        sums.raw(i)
        sums.add(i)
    advance(2)
    attend(0)
    branch(0)
    out_copies += [net.copy(a, a_o), net.copy(p, p_o)]
    for i in range(SUBS):
        sums.cross(i)
        if i:
            advance(2)
    advance(1)
    for i in range(SUBS):
        sums.arrive(i)
    hidden = tok[...].astype(F32) + mine[...].astype(F32) + other[...].astype(F32)
    h_o[...] = hidden
    n2_o[...] = (hidden * factor_of(hidden) * gain_row(gains, 1)).astype(BF16)
    cs.ring.far()
    cs.finish()
    for fg in feeds:
        fg.finish()
    for copy in saved[2:] + out_copies:
        copy.wait()
    net.drain()


def out(shape, kind=BF16):
    return jax.ShapeDtypeStruct(shape, kind)


def params(number):
    return pltpu.CompilerParams(
        collective_id=number, has_side_effects=True, vmem_limit_bytes=60 * 1024 * 1024
    )


def call_a(tok, cot, parents, frequency, gone, gtwo, *weights):
    rows_b = pltpu.VMEM((TREE, WIDTH), BF16)
    head_b = pltpu.VMEM((TREE, HEAD), BF16)
    return pl.pallas_call(
        kernel_a,
        out_shape=[
            out((TREE, WIDTH)), out((TREE, HEAD)), out((TREE, HEAD)), out((TREE, HEAD)),
            out((TREE, HEAD)), out((TREE, TREE), F32), out((ROWS, WIDTH), F32),
            out((ROWS, WIDTH)), out((TREE, HALF), F32), out((TREE, HALF), F32),
            out((WIDTH, 4 * HEAD)), out((16 * GROWS, 128)),
            out((WIDTH, 3 * FFD)), out((TREE, WIDTH)),
        ],
        in_specs=[VM, ANY, VM, VM, VM, VM] + [ANY] * 7,
        out_specs=[ANY] * 6 + [VM] * 2 + [ANY] * 6,
        scratch_shapes=[
            rows_b, rows_b, head_b, head_b, head_b, head_b, pltpu.VMEM((TREE, TREE), F32), rows_b,
            *ring_sum_scratch(),
            pltpu.VMEM((WIDTH, 4 * HEAD), BF16), pltpu.VMEM((16 * GROWS, 128), BF16),
            pltpu.VMEM((BLOCK, 4 * HEAD), BF16), pltpu.VMEM((BLOCK, 3 * FFD), BF16),
            pltpu.VMEM((HEAD, BLOCK), BF16), pltpu.VMEM((FFD, BLOCK), BF16),
            pltpu.VMEM((TREE, NSEG), BF16), pltpu.VMEM((TREE, NSEG), BF16),
            pltpu.VMEM((TREE, HALF), F32), pltpu.VMEM((TREE, HALF), F32),
            pltpu.VMEM((GROWS, 128), BF16),
            *near_sems(160, 24),
        ],
        compiler_params=params(0),
        name="attend",
    )(tok, cot, parents, frequency, gone, gtwo, *weights)


def kernel_f(
    n2_in, h_any, fw, cf, gains,
    dh_o, low_o, outh_o, dsum_o, term_o, grads_o,
    w, c, n2, dgu, hid, dh_s, h_in,
    part, passed, plus, minus, mine, other,
    given, taken, part2, passed2, plus2, minus2,
    dgrad, dgift, dpassed, dplus, dminus,
    send, recv, local,
):
    here = Place()
    net = Net(here, send, recv, local)
    net.greet(ALL_NEAR)
    ns = RingGather(net, n2_in, n2)
    half = WIDTH // 2
    tp_cols = span(here.t, half)
    loads = [net.copy(fw, w)]
    loads += [net.copy(cf.at[ns.at(i)], c.at[ns.at(i)]) for i in (0, 1, 3)]
    loads.append(net.copy(cf.at[ns.at(2), tp_cols], c.at[ns.at(2), tp_cols]))
    h_load = net.copy(h_any, h_in)
    c_far = net.push(cf.at[ns.at(2), tp_cols], c.at[ns.at(2), tp_cols], "t")
    n2[ns.at(0), :] = n2_in[...]
    for copy in loads:
        copy.wait()

    def third(j, i):
        return pl.ds(pl.multiple_of(i * FFD + j * 256, 256), 256)

    def pull(step):
        at = ns.at(step)

        def body(j):
            dh_s[at, span(j, 256)] = nn(c[at, :], w[:, third(j, 2)])

        tiles(4, body)

    def feed(step):
        at = ns.at(step)

        def body(j):
            cols = span(j, 256)
            rows = n2[at, :]
            g = nn(rows, w[:, cols])
            u = nn(rows, w[:, third(j, 1)])
            d = dh_s[at, cols]
            s = jax.nn.sigmoid(g)
            swish = g * s
            hid[at, cols] = (swish * u).astype(BF16)
            dgu[at, cols] = (d * u * s * (1.0 + g * (1.0 - s))).astype(BF16)
            dgu[at, third(j, 1)] = (d * swish).astype(BF16)

        tiles(4, body)

    def down(step, t, dst):
        at = ns.at(step)

        def body(j):
            rows = pl.ds(pl.multiple_of(t * half + j * 512, 512), 512)
            dst[at, span(j, 512)] = nt(hid[at, :], w[rows, 2 * FFD :]).astype(BF16)

        tiles(2, body)

    gifts = {}

    def give(step):
        down(step, 1 - here.t, given)
        at = ns.at(step)
        gifts[step] = net.push(given.at[at], taken.at[at], "t")

    sums = RingSum(net, part, passed, plus, minus, mine, other, SUBS)
    outs = RingSum(net, part2, passed2, plus2, minus2, None, None, 1)
    term_o[...] = jnp.zeros_like(term_o)

    def back(step, side=None):
        at = sums.at(step)
        width = WIDTH // SUBS // (1 if side is None else 2)

        def body(j):
            cols = pl.ds(pl.multiple_of(j * (WIDTH // SUBS) + (side or 0) * width, width), width)
            rows = nt(dgu[at, :], w[cols, : 2 * FFD])
            part[at, cols] = rows.astype(BF16)
            term_o[:, cols] += jnp.sum(rows * n2[at, cols].astype(F32), 0, keepdims=True)

        tiles(SUBS, body)

    def keep(step):
        down(step, here.t, part2)

    def grad(i):
        turned = n2[:, span(i, 256)].T
        for j in range(4):
            w[span(i, 256), j * 512 : (j + 1) * 512] = nn(
                turned, dgu[:, j * 512 : (j + 1) * 512]
            ).astype(BF16)

    def grad_down(i):
        turned = c[:, span(i, 256)].T
        for j in range(2):
            dgrad[span(i, 256), j * 512 : (j + 1) * 512] = nn(
                turned, hid[:, j * 512 : (j + 1) * 512]
            ).astype(BF16)

    def take(step):
        gifts[step].wait_recv()
        at = ns.at(step)
        part2[at, :] = part2[at, :] + taken[at, :]

    pull(0)
    feed(0)
    ns.forward()
    give(0)
    pull(3)
    pull(1)
    c_far.wait_recv()
    pull(2)
    ns.left()
    feed(3)
    give(3)
    ns.right()
    feed(1)
    back(1, 1)
    back(3, 0)
    for i in range(SUBS):
        sums.raw(i)
    give(1)
    ns.far()
    feed(2)
    back(2)
    for i in range(SUBS):
        sums.far(i)
    give(2)
    back(1, 0)
    back(3, 1)
    tiles(8, grad_down)
    ds = ShardSum(net, dgrad, BLOCK, dgift, dpassed, dplus, dminus, None)
    sums.add(0)
    sums.add(1)
    back(0)
    sums.add(2)
    ds.pair(2, 1)
    ds.pair(2, 0)
    sums.add(3)
    keep(2)
    sums.cross(0)
    keep(1)
    keep(3)
    sums.cross(1)
    keep(0)
    take(2)
    outs.far(0)
    sums.cross(2)
    take(1)
    take(3)
    outs.raw(0)
    for dx in (1, 3):
        for dy in (1, 0):
            ds.pair(dx, dy)
    sums.cross(3)
    tiles(3, grad)
    ds.pass_on(1)
    ds.pass_on(0)
    outs.add(0)
    tiles(5, lambda i: grad(i + 3))
    saves = [net.copy(w.at[:, pl.ds(0, 2 * FFD)], grads_o)]
    ds.pair(0, 1)
    ds.pair(0, 0)
    take(0)
    for i in range(SUBS):
        sums.arrive(i)
    gain_two = gain_row(gains, 1)
    h_load.wait()
    hidden = h_in[...]
    upstream = mine[...].astype(F32) + other[...].astype(F32)
    factor = factor_of(hidden)
    weighted = upstream * gain_two
    inner = jnp.mean(weighted * hidden, -1, keepdims=True)
    dh = (
        c[ns.at(0), :].astype(F32) + factor * weighted - hidden * (factor * factor * factor) * inner
    )
    dh_o[...] = dh
    low_o[...] = dh.astype(BF16)
    term_o[...] = term_o[...] / gain_two
    outs.settle(0)
    mine_half = span(here.t, half)
    outh_o[...] = (
        h_in[:, mine_half]
        + part2[ns.at(0), :].astype(F32)
        + plus2[...].astype(F32)
        + minus2[...].astype(F32)
    ).astype(BF16)
    for dy in (0, 1):
        ds.close(dy, False)
        dsum_o[dy * BLOCK : (dy + 1) * BLOCK, :] = ds.kept(0, dy)[...]
    for copy in saves:
        copy.wait()
    net.drain()


def call_f(n2_in, h_in, fw, cf, gains):
    rows_b = pltpu.VMEM((TREE, WIDTH), BF16)
    half_b = pltpu.VMEM((TREE, WIDTH // 2), BF16)
    own_b = pltpu.VMEM((ROWS, WIDTH // 2), BF16)
    return pl.pallas_call(
        kernel_f,
        out_shape=[
            out((ROWS, WIDTH), F32), out((ROWS, WIDTH)), out((ROWS, WIDTH // 2)),
            out((2 * BLOCK, FFD)), out((1, WIDTH), F32), out((WIDTH, 2 * FFD)),
        ],
        in_specs=[VM, ANY, ANY, ANY, VM],
        out_specs=[VM, VM, VM, VM, VM, ANY],
        scratch_shapes=[
            pltpu.VMEM((WIDTH, 3 * FFD), BF16), rows_b, rows_b, rows_b,
            pltpu.VMEM((TREE, FFD), BF16), pltpu.VMEM((TREE, FFD), F32),
            pltpu.VMEM((ROWS, WIDTH), F32),
            rows_b, *ring_sum_scratch(),
            half_b, half_b, half_b, own_b, own_b, own_b,
            pltpu.VMEM((WIDTH, FFD), BF16), *shard_sum_scratch(BLOCK, FFD)[:-1],
            *near_sems(80, 16),
        ],
        compiler_params=params(1),
        name="feed",
    )(n2_in, h_in, fw, cf, gains)


def kernel_b(
    low_in, dh_any, tok_any, co_any, si_any, outh, gains, term_in, dsum,
    p_in, q_in, k_in, v_in, a_in, n1_in, aw_in, fgrads,
    dtok_o, out_o, gate_o, up_o, down_o, attn_o, gain_o,
    low, p, q, k, v, a, n1, aw, da, d, dk, dv, terms, gblk_f, ublk, ablk, gblk, gother, term, wgrad, dother,
    dh_in, tok, cosine, sine,
    part, passed, plus, minus, mine, other,
    ggift, gpassed, gplus, gminus, glast, gheld,
    ugift, upassed, uplus, uminus, ulast, uheld,
    agift, apassed, aplus, aminus, alast,
    tgift, tpassed, tplus, tminus, tlast,
    send, recv, local,
):
    here = Place()
    net = Net(here, send, recv, local)
    net.greet(ALL_NEAR)
    ls = RingGather(net, low_in, low, True)
    loads = [
        net.copy(src, dst)
        for src, dst in (
            (aw_in, aw), (v_in, v), (p_in, p), (k_in, k), (q_in, q), (co_any, cosine),
            (si_any, sine), (a_in, a), (n1_in, n1), (dh_any, dh_in), (tok_any, tok),
        )
    ]
    gate = ShardSum(
        net, fgrads.at[:, pl.ds(0, FFD)], BLOCK, ggift, gpassed, gplus, gminus, glast, gheld
    )
    down_push = net.push(dsum.at[pl.ds(BLOCK, BLOCK)], dother, "y")
    my_half = span(here.t, WIDTH // 2)
    out_push = net.push(outh, out_o.at[:, my_half], "t")
    saves = [net.copy(outh, out_o.at[:, my_half])]
    low[ls.at(0), :] = low_in[...]

    def attended(step):
        at = ls.at(step)
        da[at, :] = nn(low[at, :], aw[:, 3 * HEAD : 4 * HEAD]).astype(BF16)

    def attend(step):
        at = ls.at(step)
        da_rows, probs = da[at, :], p[at, :]
        dp = nt(da_rows, v[...])
        ds = probs * (dp - jnp.sum(probs * dp, -1, keepdims=True))
        draw = (ds * (1.0 / math.sqrt(HEAD))).astype(BF16)
        first, second = turn(nn(draw, k[...]), cosine[at, :], -sine[at, :])
        d[at, :HALF] = first.astype(BF16)
        d[at, HALF:HEAD] = second.astype(BF16)
        dk_more, dv_more = tn(draw, q[at, :]), tn(probs.astype(BF16), da_rows)
        if step == 0:
            dk[...] = dk_more
            dv[...] = dv_more
        else:
            dk[...] += dk_more
            dv[...] += dv_more

    loads[0].wait()
    attended(0)
    gate.pair(2, 1)
    gate.pair(2, 0)
    ls.forward()
    up = ShardSum(
        net, fgrads.at[:, pl.ds(FFD, FFD)], BLOCK, ugift, upassed, uplus, uminus, ulast, uheld
    )
    for dx in (1, 3):
        for dy in (1, 0):
            gate.pair(dx, dy)
    for copy in loads[1:7]:
        copy.wait()
    attend(0)
    ls.share()
    down_push.wait_recv()
    dother[...] = (dother[...].astype(F32) + dsum[:BLOCK, :].astype(F32)).astype(BF16)
    dz = RingGather(net, dother, down_o)
    saves.append(net.copy(dother, down_o.at[dz.at(0)]))
    up.pair(2, 1)
    up.pair(2, 0)
    gate.pass_on(1)
    gate.pass_on(0)
    ls.left()
    attended(3)
    attend(3)
    for dx in (1, 3):
        for dy in (1, 0):
            up.pair(dx, dy)
    ls.right()
    attended(1)
    attend(1)
    gate.pair(0, 1)
    gate.pair(0, 0)
    dz.forward()
    ls.far()
    attended(2)
    attend(2)
    for copy in loads[7:]:
        copy.wait()
    first, second = turn(dk[...], cosine[...], -sine[...])
    d[:, HEAD : HEAD + HALF] = first.astype(BF16)
    d[:, HEAD + HALF : 2 * HEAD] = second.astype(BF16)
    d[:, 2 * HEAD :] = dv[...].astype(BF16)

    sums = RingSum(net, part, passed, plus, minus, mine, other, SUBS)
    term[...] = jnp.zeros_like(term)

    def back(step):
        at = sums.at(step)

        def body(j):
            cols = span(j, 512)
            rows = nt(d[at, :], aw[cols, : 3 * HEAD])
            part[at, cols] = rows.astype(BF16)
            term[:, cols] += jnp.sum(rows * n1[at, cols].astype(F32), 0, keepdims=True)

        tiles(4, body)

    def grad(i):
        turned = n1[:, span(i, 256)].T
        wgrad[span(i, 256), : 3 * HEAD] = nn(turned, d[...]).astype(BF16)
        turned = low[:, span(i, 256)].T
        wgrad[span(i, 256), 3 * HEAD :] = nn(turned, a[...]).astype(BF16)

    back(2)
    for i in range(SUBS):
        sums.far(i)
    gate.close(1)
    up.pass_on(1)
    tiles(8, grad)
    ws = ShardSum(net, wgrad, BLOCK, agift, apassed, aplus, aminus, alast)
    gate.close(0)
    up.pass_on(0)
    back(1)
    back(3)
    for i in range(SUBS):
        sums.raw(i)
        sums.add(i)
    for dx in (2, 1, 3):
        for dy in (1, 0):
            ws.pair(dx, dy)
    back(0)
    gain_one = gain_row(gains, 0)
    term_one = term[...] / gain_one
    term_two = term_in[...]
    row = lax.broadcasted_iota(jnp.int32, (GROWS, 128), 0)
    for s in range(16):
        cols = slice(s * 128, (s + 1) * 128)
        terms[s * GROWS : (s + 1) * GROWS, :] = jnp.where(
            row == 0, term_one[:, cols], jnp.where(row == 1, term_two[:, cols], 0.0)
        ).astype(BF16)
    ts = ShardSum(net, terms, GROWS, tgift, tpassed, tplus, tminus, tlast)
    up.pair(0, 1)
    up.pair(0, 0)
    up.close(1)
    for dx in (2, 1, 3):
        for dy in (1, 0):
            ts.pair(dx, dy)
    sums.cross(0)
    sums.cross(1)
    up.close(0)
    for shares in (ws, ts):
        for dy in (1, 0):
            shares.pair(0, dy)
    ublk[...] = up.result().astype(BF16)
    uz = RingGather(net, ublk, up_o)
    saves.append(net.copy(ublk, up_o.at[uz.at(0)]))
    sums.cross(2)
    for shares in (ws, ts):
        for dy in (1, 0):
            shares.pass_on(dy)
    sums.cross(3)
    gblk_f[...] = gate.result().astype(BF16)
    gz = RingGather(net, gblk_f, gate_o)
    saves.append(net.copy(gblk_f, gate_o.at[gz.at(0)]))
    uz.forward()
    gz.forward()
    for dy in (1, 0):
        for shares in (ws, ts):
            shares.close(dy)
    for i in range(SUBS):
        sums.arrive(i)
    inputs = tok[...].astype(F32)
    upstream = mine[...].astype(F32) + other[...].astype(F32)
    factor = factor_of(inputs)
    weighted = upstream * gain_one
    inner = jnp.mean(weighted * inputs, -1, keepdims=True)
    dtok_o[...] = (
        dh_in[...] + (factor * weighted - inputs * (factor * factor * factor) * inner)
    ).astype(BF16)
    gblk[...] = ts.result().astype(BF16)
    cross = net.push(gblk, gother, "t")
    ablk[...] = ws.result().astype(BF16)
    az = RingGather(net, ablk, attn_o)
    saves.append(net.copy(ablk, attn_o.at[az.at(0)]))
    cross.wait_recv()
    gother[...] = (gblk[...].astype(F32) + gother[...].astype(F32)).astype(BF16)
    tz = RingGather(net, gother, gain_o)
    saves.append(net.copy(gother, gain_o.at[tz.at(0)]))
    for shares in (az, tz):
        shares.forward()
    for shares in (dz, gz, uz, az, tz):
        shares.left()
        shares.right()
        shares.far()
    out_push.wait_recv()
    for copy in saves:
        copy.wait()
    net.drain()


def call_b(low, dh, tok, cosine, sine, outh, gains, term, dsum, *rest):
    rows_b = pltpu.VMEM((TREE, WIDTH), BF16)
    head_b = pltpu.VMEM((TREE, HEAD), BF16)
    head_f = pltpu.VMEM((TREE, HEAD), F32)
    ffn_b = pltpu.VMEM((BLOCK, FFD), BF16)
    held = pltpu.VMEM((8, BLOCK, FFD), BF16)
    gain_b = pltpu.VMEM((GROWS, 128), BF16)
    full = out((4 * BLOCK, FFD))
    return pl.pallas_call(
        kernel_b,
        out_shape=[
            out((ROWS, WIDTH)), out((ROWS, WIDTH)), full, full, full, full, out((4 * GROWS, 128)),
        ],
        in_specs=[VM] + [ANY] * 5 + [VM] * 3 + [ANY] * 8,
        out_specs=[VM] + [ANY] * 6,
        scratch_shapes=[
            rows_b, pltpu.VMEM((TREE, TREE), F32), head_b, head_b, head_b, head_b, rows_b,
            pltpu.VMEM((WIDTH, 4 * HEAD), BF16), head_b, pltpu.VMEM((TREE, 3 * HEAD), BF16),
            head_f, head_f,
            pltpu.VMEM((16 * GROWS, 128), BF16), ffn_b, ffn_b, ffn_b, gain_b, gain_b,
            pltpu.VMEM((1, WIDTH), F32), pltpu.VMEM((WIDTH, 4 * HEAD), BF16), ffn_b,
            pltpu.VMEM((ROWS, WIDTH), F32), pltpu.VMEM((ROWS, WIDTH), BF16),
            pltpu.VMEM((TREE, HALF), F32), pltpu.VMEM((TREE, HALF), F32),
            rows_b, *ring_sum_scratch(),
            *shard_sum_scratch(BLOCK, FFD), held,
            *shard_sum_scratch(BLOCK, FFD), held,
            *shard_sum_scratch(BLOCK, 4 * HEAD), *shard_sum_scratch(GROWS, 128),
            *near_sems(176, 48),
        ],
        compiler_params=params(2),
        name="attend_back",
    )(low, dh, tok, cosine, sine, outh, gains, term, dsum, *rest)


def kernel_e(
    gate, up, down, attn, gain, result, dtok, query_o, key_o, value_o, wout_o, gate_o, up_o, down_o, one_o, two_o,
    result_o, dtok_o,
):
    z = pl.program_id(0)
    result_o[...] = result[...]
    dtok_o[...] = dtok[...]
    gate_o[...] = gate[...].astype(F32)
    up_o[...] = up[...].astype(F32)
    down_o[...] = down[...].astype(F32).T
    query_o[...] = attn[:, :HEAD].astype(F32)
    wout_o[...] = attn[:, 3 * HEAD :].astype(F32).T

    @pl.when(lax.rem(z, 2) == 0)
    def _():
        key_o[...] = attn[:, HEAD : 2 * HEAD].astype(F32)
        value_o[...] = attn[:, 2 * HEAD : 3 * HEAD].astype(F32)

    @pl.when(lax.rem(z, 2) == 1)
    def _():
        key_o[...] += attn[:, HEAD : 2 * HEAD].astype(F32)
        value_o[...] += attn[:, 2 * HEAD : 3 * HEAD].astype(F32)

    gains = sum(gain[i * GROWS : i * GROWS + 16, :].astype(F32) for i in range(4))
    one_o[...] = gains[0:1]
    two_o[...] = gains[1:2]


def call_e(*blocks):
    def spec(shape, place):
        return pl.BlockSpec(shape, place)

    return pl.pallas_call(
        kernel_e,
        grid=(4,),
        out_shape=[
            out((BLOCK, 4 * HEAD), F32), out((BLOCK, 2 * HEAD), F32), out((BLOCK, 2 * HEAD), F32),
            out((4 * HEAD, BLOCK), F32), out((BLOCK, 4 * FFD), F32), out((BLOCK, 4 * FFD), F32),
            out((4 * FFD, BLOCK), F32), out((1, 128), F32), out((1, 128), F32),
            out((ROWS, WIDTH)), out((ROWS, WIDTH)),
        ],
        in_specs=[
            *[spec((BLOCK, FFD), lambda z: (z, 0))] * 4,
            spec((4 * GROWS, 128), lambda z: (0, 0)),
            *[spec((ROWS // 4, WIDTH), lambda z: (z, 0))] * 2,
        ],
        out_specs=[
            spec((BLOCK, HEAD), lambda z: (0, z)), spec((BLOCK, HEAD), lambda z: (0, z // 2)),
            spec((BLOCK, HEAD), lambda z: (0, z // 2)), spec((HEAD, BLOCK), lambda z: (z, 0)),
            spec((BLOCK, FFD), lambda z: (0, z)), spec((BLOCK, FFD), lambda z: (0, z)),
            spec((FFD, BLOCK), lambda z: (z, 0)), spec((1, 128), lambda z: (0, 0)),
            spec((1, 128), lambda z: (0, 0)),
            *[spec((ROWS // 4, WIDTH), lambda z: (z, 0))] * 2,
        ],
        compiler_params=pltpu.CompilerParams(vmem_limit_bytes=60 * 1024 * 1024),
        name="widen",
    )(*blocks)


def local(
    tokens, parents, gain_attn, w_query, key_weight, value_weight, w_out, gain_ffn, w_gate, w_up,
    w_down, cotangent,
):
    frequency = jnp.asarray(
        (THETA ** (-np.arange(HALF, dtype=np.float64) * 2.0 / HEAD)).astype(np.float32)[None, :]
    )
    n1, q, k, v, a, p, hidden, n2, cosine, sine, aw, gains, fw, cf = call_a(
        tokens, cotangent, parents, frequency, gain_attn.reshape(1, BLOCK),
        gain_ffn.reshape(1, BLOCK), w_query, key_weight, value_weight, w_out,
        w_gate, w_up, w_down,
    )
    dh, low, outh, dsum, term, fgrads = call_f(n2, hidden, fw, cf, gains)
    d_tokens, output, gate, up, down, attn, gain = call_b(
        low, dh, tokens, cosine, sine, outh, gains, term, dsum, p, q, k, v, a, n1, aw, fgrads
    )
    query, key, value, wout, gate, up, down, one, two, output, d_tokens = call_e(
        gate, up, down, attn, gain, output, d_tokens
    )
    return (
        output, d_tokens, one.reshape(128), query, key, value, wout, two.reshape(128), gate, up,
        down,
    )


def solution(mesh):
    rows = P(("shard", "ctx"), None)
    weight = P("shard", "tp")
    turned = P("tp", "shard")
    vector = P("shard")
    return jax.shard_map(
        local,
        mesh=mesh,
        in_specs=(
            rows, P("shard", None), vector, weight, weight, weight, turned, vector,
            weight, weight, turned, rows,
        ),
        out_specs=(
            rows, rows, vector, weight, weight, weight, turned, vector, weight, weight, turned,
        ),
        check_vma=False,
    )
```

```python
import functools
import math

import jax
import jax.numpy as jnp
import numpy as np
from jax import lax
from jax.experimental import pallas as pl
from jax.experimental.pallas import tpu as pltpu
from jax.sharding import PartitionSpec as P

HEAD = 256
HALF = HEAD // 2
SEG = 48
NSEG = 16
ROWS = 192
TREE = 768
WIDTH = 2048
FFD = 1024
BLOCK = 128
GROWS = 32
SUBS = 4

EPSILON = 1e-06
THETA = 1000042.0
NEGATIVE = -1e30
HIGHEST = lax.Precision.HIGHEST
F32 = jnp.float32
BF16 = jnp.bfloat16
MESH = pl.DeviceIdType.MESH
ANY = pl.BlockSpec(memory_space=pl.ANY)
VM = pl.BlockSpec(memory_space=pltpu.VMEM)


def nn(left, right):
    return jnp.dot(left, right, preferred_element_type=F32)


def nt(left, right):
    return lax.dot_general(left, right, (((1,), (1,)), ((), ())), preferred_element_type=F32)


def tn(left, right):
    return lax.dot_general(left, right, (((0,), (0,)), ((), ())), preferred_element_type=F32)


def ring(value, step):
    return lax.rem(value + step, 4)


class Place:
    def __init__(self):
        shard = lax.axis_index("shard")
        self.shard = shard
        self.y = shard // 8
        self.x = lax.rem(shard // 2, 4)
        self.c = lax.rem(shard, 2)
        self.z = lax.axis_index("ctx")
        self.t = lax.axis_index("tp")

    def block(self, dy=0, dx=0, dc=0):
        y = 1 - self.y if dy else self.y
        c = 1 - self.c if dc else self.c
        return y * 8 + ring(self.x, dx) * 2 + c

    def to(self, dy=0, dx=0, dc=0, dz=0, dt=0):
        t = 1 - self.t if dt else self.t
        return (self.block(dy, dx, dc), ring(self.z, dz), t)


ALL_NEAR = ("y", "x+", "x-", "c", "z+", "z-", "t")
NEAR = {
    "y": dict(dy=1), "x+": dict(dx=1), "x-": dict(dx=3), "c": dict(dc=1),
    "z+": dict(dz=1), "z-": dict(dz=3), "t": dict(dt=1),
}


class Net:
    def __init__(self, here, send, recv, local):
        self.here, self.send, self.recv, self.local = here, send, recv, local
        self.sent, self.count, self.copies = [], 0, 0

    def greet(self, names):
        barrier = pltpu.get_barrier_semaphore()
        for name in names:
            pl.semaphore_signal(
                barrier, inc=1, device_id=self.here.to(**NEAR[name]), device_id_type=MESH
            )
        pl.semaphore_wait(barrier, len(names))

    def push(self, src, dst, name):
        index = self.count
        self.count += 1
        copy = pltpu.make_async_remote_copy(
            src_ref=src,
            dst_ref=dst,
            send_sem=self.send.at[index],
            recv_sem=self.recv.at[index],
            device_id=self.here.to(**NEAR[name]),
            device_id_type=MESH,
        )
        copy.start()
        self.sent.append(copy)
        return copy

    def copy(self, src, dst):
        index = self.copies
        self.copies += 1
        copy = pltpu.make_async_copy(src, dst, self.local.at[index])
        copy.start()
        return copy

    def drain(self):
        for copy in self.sent:
            copy.wait_send()


def near_sems(remote, local):
    return [
        pltpu.SemaphoreType.DMA((remote,)),
        pltpu.SemaphoreType.DMA((remote,)),
        pltpu.SemaphoreType.DMA((local,)),
    ]


def chunk(index):
    return pl.ds(pl.multiple_of(index * ROWS, ROWS), ROWS)


class RingGather:
    def __init__(self, net, own, full, shared=False):
        self.net, self.full, self.rows, self.shared = net, full, own.shape[0], shared
        half = self.rows // 2
        one, two = own.at[pl.ds(0, half)], own.at[pl.ds(half, half)]
        width = own.shape[1] // 2
        self.cols = pl.ds(pl.multiple_of(net.here.t * width, width), width)
        near_one, near_two = self.half(0, 0), self.half(0, 1)
        self.a1 = net.push(one, near_one, "z+")
        self.b2 = net.push(two, near_two, "z-")
        if shared:
            one, two = one.at[:, self.cols], two.at[:, self.cols]
            near_one, near_two = near_one.at[:, self.cols], near_two.at[:, self.cols]
        self.a2 = net.push(two, near_two, "z+")
        self.b1 = net.push(one, near_one, "z-")

    def half(self, step, part):
        half = self.rows // 2
        start = ring(self.net.here.z, step) * self.rows + part * half
        return self.full.at[pl.ds(pl.multiple_of(start, half), half)]

    def at(self, step):
        return span(ring(self.net.here.z, step), self.rows)

    def forward(self):
        self.a1.wait_recv()
        self.f1 = self.net.push(self.half(3, 0), self.half(3, 0), "z+")
        self.b2.wait_recv()
        self.f2 = self.net.push(self.half(1, 1), self.half(1, 1), "z-")

    def share(self):
        self.a2.wait_recv()
        piece = self.half(3, 1).at[:, self.cols]
        self.a2 = self.net.push(piece, piece, "t")
        self.b1.wait_recv()
        piece = self.half(1, 0).at[:, self.cols]
        self.b1 = self.net.push(piece, piece, "t")

    def left(self):
        self.a2.wait_recv()

    def right(self):
        self.b1.wait_recv()

    def far(self):
        self.f1.wait_recv()
        self.f2.wait_recv()


class HalfGather:
    def __init__(self, net, own, full):
        width = own.shape[1] // 2
        self.net = net
        cols = pl.ds(pl.multiple_of(net.here.t * width, width), width)
        self.full = full.at[:, cols]
        self.ring = RingGather(net, own.at[:, cols], self.full)
        self.given = []

    def give(self, step):
        (None, self.ring.right, self.ring.far, self.ring.left)[step]()
        piece = self.full.at[self.ring.at(step)]
        self.given.append(self.net.push(piece, piece, "t"))

    def finish(self):
        for copy in self.given:
            copy.wait_recv()


class RingSum:
    def __init__(self, net, part, passed, plus, minus, mine, other, subs):
        self.net, self.part, self.passed = net, part, passed
        self.plus, self.minus, self.mine, self.other = plus, minus, mine, other
        width = part.shape[1] // subs
        self.cols = [
            (pl.ds(i * width, width // 2), pl.ds(i * width + width // 2, width // 2))
            for i in range(subs)
        ]
        self.subs = subs
        self.width = width
        self.e1, self.e2, self.r1, self.r2 = {}, {}, {}, {}
        self.s1, self.s2, self.t = {}, {}, {}

    def at(self, step):
        return chunk(ring(self.net.here.z, step))

    def far(self, i):
        one, two = self.cols[i]
        self.e1[i] = self.net.push(self.part.at[self.at(2), one], self.passed.at[:, one], "z+")
        self.e2[i] = self.net.push(self.part.at[self.at(2), two], self.passed.at[:, two], "z-")

    def raw(self, i):
        one, two = self.cols[i]
        self.r1[i] = self.net.push(self.part.at[self.at(1), two], self.plus.at[:, two], "z+")
        self.r2[i] = self.net.push(self.part.at[self.at(3), one], self.minus.at[:, one], "z-")

    def add(self, i):
        one, two = self.cols[i]
        part, passed = self.part, self.passed
        self.e1[i].wait_recv()
        part[self.at(1), one] = (
            part[self.at(1), one].astype(F32) + passed[:, one].astype(F32)
        ).astype(BF16)
        self.s1[i] = self.net.push(part.at[self.at(1), one], self.plus.at[:, one], "z+")
        self.e2[i].wait_recv()
        part[self.at(3), two] = (
            part[self.at(3), two].astype(F32) + passed[:, two].astype(F32)
        ).astype(BF16)
        self.s2[i] = self.net.push(part.at[self.at(3), two], self.minus.at[:, two], "z-")

    def settle(self, i):
        for copy in (self.r1[i], self.r2[i], self.s1[i], self.s2[i]):
            copy.wait_recv()

    def cross(self, i):
        self.settle(i)
        both = pl.ds(i * self.width, self.width)
        self.mine[:, both] = (
            self.part[self.at(0), both].astype(F32)
            + self.plus[:, both].astype(F32)
            + self.minus[:, both].astype(F32)
        ).astype(BF16)
        self.t[i] = self.net.push(self.mine.at[:, both], self.other.at[:, both], "t")

    def arrive(self, i):
        self.t[i].wait_recv()


class FoldedSum(RingSum):
    def __init__(self, net, part, passed, plus, minus, mine, other, fold):
        super().__init__(net, part, passed, plus, minus, mine, other, SUBS)
        self.fold = fold
        self.folds, self.cols, self.both = {}, [], []
        width = self.width
        for j in range(SUBS):
            start = lax.rem(j + (SUBS // 2) * net.here.t, SUBS) * width
            self.both.append(pl.ds(pl.multiple_of(start, width), width))
            half = width // 2
            self.cols.append(
                tuple(pl.ds(pl.multiple_of(start + k * half, half), half) for k in range(2))
            )

    def exchange(self):
        for j in range(SUBS // 2, SUBS):
            one, two = self.cols[j]
            self.folds[j] = (
                self.net.push(self.part.at[self.at(1), two], self.fold.at[:, two], "t"),
                self.net.push(self.part.at[self.at(3), one], self.fold.at[:, one], "t"),
            )

    def raw(self, j):
        for copy in self.folds[j + SUBS // 2]:
            copy.wait_recv()
        one, two = self.cols[j]
        part, fold = self.part, self.fold
        part[self.at(1), two] = part[self.at(1), two] + fold[:, two]
        part[self.at(3), one] = part[self.at(3), one] + fold[:, one]
        super().raw(j)

    def cross(self, j):
        both, (one, two) = self.both[j], self.cols[j]
        self.s1[j].wait_recv()
        self.s2[j].wait_recv()
        if j < SUBS // 2:
            self.r1[j].wait_recv()
            self.r2[j].wait_recv()
            self.mine[:, both] = (
                self.part[self.at(0), both].astype(F32)
                + self.plus[:, both].astype(F32)
                + self.minus[:, both].astype(F32)
            ).astype(BF16)
        else:
            self.mine[:, one] = self.part[self.at(0), one] + self.plus[:, one]
            self.mine[:, two] = self.part[self.at(0), two] + self.minus[:, two]
        self.t[j] = self.net.push(self.mine.at[:, both], self.other.at[:, both], "t")


def ring_sum_scratch():
    return [pltpu.VMEM((ROWS, WIDTH), BF16) for _ in range(5)]


class ShardGather:
    def __init__(self, net, own, full, rows):
        self.net, self.own, self.full, self.rows = net, own, full, rows
        self.to_sibling = []

    def at(self, part=None, **step):
        block = self.net.here.block(**step)
        if part is None:
            return self.full.at[pl.ds(pl.multiple_of(block * self.rows, self.rows), self.rows)]
        half = self.rows // 2
        start = block * self.rows + part * half
        return self.full.at[pl.ds(pl.multiple_of(start, half), half)]

    def relay(self, name, part=None, **step):
        ref = self.at(part, **step)
        return self.net.push(ref, ref, name)

    def sibling(self, part=None, **step):
        self.to_sibling.append(self.relay("c", part, **step))

    def begin(self):
        self.y0, self.p0, self.m0, c0 = (
            self.net.push(self.own, self.at(), name) for name in ("y", "x+", "x-", "c")
        )
        self.to_sibling.append(c0)

    def across(self):
        self.y0.wait_recv()
        self.p1 = self.relay("x+", dy=1)
        self.m1 = self.relay("x-", dy=1)
        self.sibling(dy=1)

    def near(self, dy):
        plus, minus = (self.p1, self.m1) if dy else (self.p0, self.m0)
        plus.wait_recv()
        fp = self.relay("x+", 0, dy=dy, dx=3)
        self.sibling(dy=dy, dx=3)
        minus.wait_recv()
        fm = self.relay("x-", 1, dy=dy, dx=1)
        self.sibling(dy=dy, dx=1)
        if dy:
            self.fp1, self.fm1 = fp, fm
        else:
            self.fp0, self.fm0 = fp, fm

    def far(self, dy):
        plus, minus = (self.fp1, self.fm1) if dy else (self.fp0, self.fm0)
        plus.wait_recv()
        self.sibling(0, dy=dy, dx=2)
        minus.wait_recv()
        self.sibling(1, dy=dy, dx=2)

    def finish(self):
        for copy in self.to_sibling:
            copy.wait_recv()


class ShardSum:
    def __init__(
        self, net, source, rows, gift, passed, plus, minus, last, held=None, whole=True
    ):
        self.net, self.source, self.rows, self.held = net, source, rows, held
        self.gift, self.passed, self.plus, self.minus, self.last = gift, passed, plus, minus, last
        self.gifts, self.loads = {}, {}
        self.e1, self.e2, self.raw, self.sums = {}, {}, {}, {}
        if whole:
            for dx in (2, 1, 3, 0):
                self.offer(dx)

    def offer(self, dx):
        for dy in (1, 0):
            self.gifts[dx, dy] = self.net.push(
                self.block(dx, dy, 1), self.gift.at[2 * dx + dy], "c"
            )
            if self.held is not None:
                self.loads[dx, dy] = self.net.copy(
                    self.block(dx, dy, 0), self.held.at[2 * dx + dy]
                )

    def block(self, dx, dy, dc):
        return self.source.at[span(self.net.here.block(dx=dx, dy=dy, dc=dc), self.rows)]

    def kept(self, dx, dy, part=None):
        half = self.rows // 2
        if self.held is not None:
            ref = self.held.at[2 * dx + dy]
            return ref if part is None else ref.at[pl.ds(part * half, half)]
        block = self.net.here.block(dx=dx, dy=dy)
        if part is None:
            return self.source.at[span(block, self.rows)]
        return self.source.at[pl.ds(pl.multiple_of(block * self.rows + part * half, half), half)]

    def pair(self, dx, dy):
        self.gifts[dx, dy].wait_recv()
        if self.held is not None:
            self.loads[dx, dy].wait()
        ref = self.kept(dx, dy)
        ref[...] = ref[...] + self.gift[2 * dx + dy]
        half = self.rows // 2
        one, two = pl.ds(0, half), pl.ds(half, half)
        if dx == 2:
            self.e1[dy] = self.net.push(self.kept(2, dy, 0), self.passed.at[dy, one], "x+")
            self.e2[dy] = self.net.push(self.kept(2, dy, 1), self.passed.at[dy, two], "x-")
        if dx == 1:
            self.raw[1, dy] = self.net.push(self.kept(1, dy, 1), self.plus.at[dy, two], "x+")
        if dx == 3:
            self.raw[3, dy] = self.net.push(self.kept(3, dy, 0), self.minus.at[dy, one], "x-")

    def pass_on(self, dy):
        half = self.rows // 2
        one, two = pl.ds(0, half), pl.ds(half, half)
        self.e1[dy].wait_recv()
        ref = self.kept(1, dy, 0)
        ref[...] = ref[...] + self.passed[dy, one]
        self.sums[1, dy] = self.net.push(ref, self.plus.at[dy, one], "x+")
        self.e2[dy].wait_recv()
        ref = self.kept(3, dy, 1)
        ref[...] = ref[...] + self.passed[dy, two]
        self.sums[3, dy] = self.net.push(ref, self.minus.at[dy, two], "x-")

    def close(self, dy, send=True):
        for copy in (self.raw[1, dy], self.raw[3, dy], self.sums[1, dy], self.sums[3, dy]):
            copy.wait_recv()
        ref = self.kept(0, dy)
        ref[...] = (
            ref[...].astype(F32) + self.plus[dy].astype(F32) + self.minus[dy].astype(F32)
        ).astype(BF16)
        if dy and send:
            self.cross = self.net.push(ref, self.last, "y")

    def result(self):
        self.cross.wait_recv()
        return self.kept(0, 0)[...].astype(F32) + self.last[...].astype(F32)


def shard_sum_scratch(rows, width):
    def block(*lead):
        return pltpu.VMEM((*lead, rows, width), BF16)

    return [block(8), block(2), block(2), block(2), block()]


def gain_row(gains, row):
    return jnp.concatenate(
        [gains[s * GROWS : s * GROWS + 16, :][row : row + 1].astype(F32) for s in range(16)], 1
    )


def factor_of(rows):
    return lax.rsqrt(jnp.mean(rows * rows, -1, keepdims=True) + EPSILON)


def turn(rows, cosine, sine):
    first, second = rows[:, :HALF], rows[:, HALF:]
    return first * cosine - second * sine, second * cosine + first * sine


def tiles(count, body):
    def step(i, carry):
        body(i)
        return carry

    lax.fori_loop(0, count, step, 0)


def span(index, size):
    return pl.ds(pl.multiple_of(index * size, size), size)


def kernel_a(
    tok, cot, parents, frequency, gone, gtwo, wq, wk, wv, wo, wg, wu, wd,
    n1_o, q_o, k_o, v_o, a_o, p_o, h_o, n2_o, co_o, si_o, aw_o, g_o, fw, cf,
    xf, n1, q, k, v, a, p, part, passed, plus, minus, mine, other, aw, gains,
    ablk, fblk, wo_s, wd_s, onehot, reach, cosine, sine, gblk,
    send, recv, local,
):
    here = Place()
    net = Net(here, send, recv, local)
    head = span(here.z, HEAD)
    group = span(here.z // 2, HEAD)
    ff = span(here.z, FFD)
    own_a = [
        net.copy(wq.at[:, head], ablk.at[:, pl.ds(0, HEAD)]),
        net.copy(wk.at[:, group], ablk.at[:, pl.ds(HEAD, HEAD)]),
        net.copy(wv.at[:, group], ablk.at[:, pl.ds(2 * HEAD, HEAD)]),
        net.copy(wo.at[head], wo_s),
    ]
    own_f = [
        net.copy(wg.at[:, ff], fblk.at[:, pl.ds(0, FFD)]),
        net.copy(wu.at[:, ff], fblk.at[:, pl.ds(FFD, FFD)]),
        net.copy(wd.at[ff], wd_s),
    ]
    row = lax.broadcasted_iota(jnp.int32, (GROWS, 128), 0)
    gblk[...] = jnp.where(
        row == 0, gone[...].astype(F32), jnp.where(row == 1, gtwo[...].astype(F32), 0.0)
    ).astype(BF16)
    net.greet(ALL_NEAR)
    xs = RingGather(net, tok, xf)
    gg = ShardGather(net, gblk, gains, GROWS)
    gg.begin()
    for copy in own_a:
        copy.wait()
    ablk[:, 3 * HEAD :] = wo_s[...].astype(F32).T.astype(BF16)
    ag = ShardGather(net, ablk, aw, BLOCK)
    ag.begin()
    saved = [
        net.copy(ablk, ag.at()),
        net.copy(gblk, gg.at()),
        net.copy(cot, cf.at[chunk(here.z)]),
    ]
    xf[xs.at(0), :] = tok[...]
    for copy in own_f:
        copy.wait()
    fblk[:, 2 * FFD :] = wd_s[...].astype(F32).T.astype(BF16)
    gg.across()
    ag.across()
    gg.near(0)
    gg.near(1)
    ag.near(0)
    gg.far(0)
    gg.far(1)
    xs.forward()
    ag.near(1)
    feeds = [
        ShardGather(
            net,
            fblk.at[:, pl.ds(i * FFD, FFD)],
            fw.at[:, pl.ds(i * FFD, FFD)],
            BLOCK,
        )
        for i in range(3)
    ]
    cs = HalfGather(net, cot, cf)
    for fg in feeds:
        fg.begin()
        saved.append(net.copy(fg.own, fg.at()))
    steps = [
        functools.partial(step, fg, *arguments)
        for step, *arguments in (
            (ShardGather.across,), (ShardGather.near, 0), (ShardGather.near, 1),
            (ShardGather.far, 0), (ShardGather.far, 1),
        )
        for fg in feeds
    ]

    def advance(count):
        for _ in range(count):
            steps.pop(0)()

    segment = lax.broadcasted_iota(jnp.int32, (NSEG, NSEG), 0)
    links = jnp.where(parents[...] == segment, 1.0, 0.0)
    links += jnp.where(segment == lax.broadcasted_iota(jnp.int32, (NSEG, NSEG), 1), 1.0, 0.0)
    links = links.astype(BF16)
    for _ in range(4):
        links = jnp.minimum(nn(links, links), 1.0).astype(BF16)
    token = lax.broadcasted_iota(jnp.int32, (TREE, NSEG), 0)
    first = lax.broadcasted_iota(jnp.int32, (TREE, NSEG), 1) * SEG
    inside = (token >= first) & (token < first + SEG)
    members = jnp.where(inside, 1.0, 0.0)
    onehot[...] = members.astype(BF16)
    reached = nt(onehot[...], links)
    reach[...] = reached.astype(BF16)
    offset = (token[:, :1] - jnp.sum(jnp.where(inside, first, 0), -1, keepdims=True)).astype(F32)
    position = (jnp.sum(reached, -1, keepdims=True) - 1.0) * SEG + offset

    def table(i):
        rows = slice(i * ROWS, (i + 1) * ROWS)
        angles = position[rows] * frequency[...]
        cosine[rows, :] = jnp.cos(angles)
        sine[rows, :] = jnp.sin(angles)

    table(0)
    gg.finish()
    saved[0].wait()
    saved[1].wait()
    ag.far(0)
    table(1)
    ag.far(1)
    table(2)
    table(3)
    saved += [net.copy(cosine, co_o), net.copy(sine, si_o)]
    gain_one = gain_row(gains, 0)

    def normed(step):
        at = xs.at(step)
        rows = xf[at, :].astype(F32)
        n1[at, :] = (rows * factor_of(rows) * gain_one).astype(BF16)

    def project(step):
        at = xs.at(step)
        rows = n1[at, :]
        co, si = cosine[at, :], sine[at, :]
        for dst, i in ((q, 0), (k, 1)):
            first, second = turn(nn(rows, aw[:, i * HEAD : (i + 1) * HEAD]), co, si)
            dst[at, :HALF] = first.astype(BF16)
            dst[at, HALF:] = second.astype(BF16)
        v[at, :] = nn(rows, aw[:, 2 * HEAD : 3 * HEAD]).astype(BF16)

    normed(0)
    ag.finish()
    project(0)
    xs.left()
    normed(3)
    project(3)
    xs.right()
    normed(1)
    project(1)
    xs.far()
    normed(2)
    project(2)
    cs.ring.forward()
    advance(3)
    out_copies = [
        net.copy(n1, n1_o), net.copy(aw, aw_o), net.copy(q, q_o), net.copy(k, k_o),
        net.copy(v, v_o), net.copy(gains, g_o),
    ]

    sums = RingSum(net, part, passed, plus, minus, mine, other, SUBS)

    def attend(step):
        at = sums.at(step)
        row = lax.broadcasted_iota(jnp.int32, (ROWS, TREE), 0) + ring(here.z, step) * ROWS
        column = lax.broadcasted_iota(jnp.int32, (ROWS, TREE), 1)
        linked = nt(reach[at, :], onehot[...])
        same = nt(onehot[at, :], onehot[...])
        allowed = (linked > 0.5) & ((same < 0.5) | (column <= row))
        scores = jnp.where(allowed, nt(q[at, :], k[...]) * (1.0 / math.sqrt(HEAD)), NEGATIVE)
        weight = jnp.exp(scores - jnp.max(scores, -1, keepdims=True))
        probs = weight / jnp.sum(weight, -1, keepdims=True)
        p[at, :] = probs
        a[at, :] = nn(probs.astype(BF16), v[...]).astype(BF16)

    def branch(step):
        at = sums.at(step)
        rows = a[at, :]

        def body(j):
            part[at, span(j, 512)] = nt(
                rows, aw[span(j, 512), 3 * HEAD : 4 * HEAD]
            ).astype(BF16)

        tiles(4, body)

    attend(2)
    branch(2)
    for i in range(SUBS):
        sums.far(i)
    cs.give(3)
    cs.give(1)
    advance(1)
    attend(1)
    branch(1)
    advance(2)
    attend(3)
    branch(3)
    for i in range(SUBS):
        sums.raw(i)
        sums.add(i)
    advance(2)
    attend(0)
    branch(0)
    out_copies += [net.copy(a, a_o), net.copy(p, p_o)]
    for i in range(SUBS):
        sums.cross(i)
        if i:
            advance(2)
    advance(1)
    for i in range(SUBS):
        sums.arrive(i)
    hidden = tok[...].astype(F32) + mine[...].astype(F32) + other[...].astype(F32)
    h_o[...] = hidden
    n2_o[...] = (hidden * factor_of(hidden) * gain_row(gains, 1)).astype(BF16)
    cs.ring.far()
    cs.finish()
    for fg in feeds:
        fg.finish()
    for copy in saved[2:] + out_copies:
        copy.wait()
    net.drain()


def out(shape, kind=BF16):
    return jax.ShapeDtypeStruct(shape, kind)


def params(number):
    return pltpu.CompilerParams(
        collective_id=number, has_side_effects=True, vmem_limit_bytes=60 * 1024 * 1024
    )


def call_a(tok, cot, parents, frequency, gone, gtwo, *weights):
    rows_b = pltpu.VMEM((TREE, WIDTH), BF16)
    head_b = pltpu.VMEM((TREE, HEAD), BF16)
    return pl.pallas_call(
        kernel_a,
        out_shape=[
            out((TREE, WIDTH)), out((TREE, HEAD)), out((TREE, HEAD)), out((TREE, HEAD)),
            out((TREE, HEAD)), out((TREE, TREE), F32), out((ROWS, WIDTH), F32),
            out((ROWS, WIDTH)), out((TREE, HALF), F32), out((TREE, HALF), F32),
            out((WIDTH, 4 * HEAD)), out((16 * GROWS, 128)),
            out((WIDTH, 3 * FFD)), out((TREE, WIDTH)),
        ],
        in_specs=[VM, ANY, VM, VM, VM, VM] + [ANY] * 7,
        out_specs=[ANY] * 6 + [VM] * 2 + [ANY] * 6,
        scratch_shapes=[
            rows_b, rows_b, head_b, head_b, head_b, head_b, pltpu.VMEM((TREE, TREE), F32), rows_b,
            *ring_sum_scratch(),
            pltpu.VMEM((WIDTH, 4 * HEAD), BF16), pltpu.VMEM((16 * GROWS, 128), BF16),
            pltpu.VMEM((BLOCK, 4 * HEAD), BF16), pltpu.VMEM((BLOCK, 3 * FFD), BF16),
            pltpu.VMEM((HEAD, BLOCK), BF16), pltpu.VMEM((FFD, BLOCK), BF16),
            pltpu.VMEM((TREE, NSEG), BF16), pltpu.VMEM((TREE, NSEG), BF16),
            pltpu.VMEM((TREE, HALF), F32), pltpu.VMEM((TREE, HALF), F32),
            pltpu.VMEM((GROWS, 128), BF16),
            *near_sems(160, 24),
        ],
        compiler_params=params(0),
        name="attend",
    )(tok, cot, parents, frequency, gone, gtwo, *weights)


def kernel_f(
    n2_in, h_any, fw, cf, gains,
    dh_o, low_o, outh_o, dsum_o, term_o, grads_o,
    w, c, n2, dgu, hid, dh_s, h_in,
    part, passed, plus, minus, mine, other,
    given, taken, part2, passed2, plus2, minus2,
    dgrad, dgift, dpassed, dplus, dminus,
    send, recv, local,
):
    here = Place()
    net = Net(here, send, recv, local)
    net.greet(ALL_NEAR)
    ns = RingGather(net, n2_in, n2)
    half = WIDTH // 2
    tp_cols = span(here.t, half)
    loads = [net.copy(fw, w)]
    loads += [net.copy(cf.at[ns.at(i)], c.at[ns.at(i)]) for i in (0, 1, 3)]
    loads.append(net.copy(cf.at[ns.at(2), tp_cols], c.at[ns.at(2), tp_cols]))
    h_load = net.copy(h_any, h_in)
    c_far = net.push(cf.at[ns.at(2), tp_cols], c.at[ns.at(2), tp_cols], "t")
    n2[ns.at(0), :] = n2_in[...]
    for copy in loads:
        copy.wait()

    def third(j, i):
        return pl.ds(pl.multiple_of(i * FFD + j * 256, 256), 256)

    def pull(step):
        at = ns.at(step)

        def body(j):
            dh_s[at, span(j, 256)] = nn(c[at, :], w[:, third(j, 2)])

        tiles(4, body)

    def feed(step):
        at = ns.at(step)

        def body(j):
            cols = span(j, 256)
            rows = n2[at, :]
            g = nn(rows, w[:, cols])
            u = nn(rows, w[:, third(j, 1)])
            d = dh_s[at, cols]
            s = jax.nn.sigmoid(g)
            swish = g * s
            hid[at, cols] = (swish * u).astype(BF16)
            dgu[at, cols] = (d * u * s * (1.0 + g * (1.0 - s))).astype(BF16)
            dgu[at, third(j, 1)] = (d * swish).astype(BF16)

        tiles(4, body)

    def down(step, t, dst):
        at = ns.at(step)

        def body(j):
            rows = pl.ds(pl.multiple_of(t * half + j * 512, 512), 512)
            dst[at, span(j, 512)] = nt(hid[at, :], w[rows, 2 * FFD :]).astype(BF16)

        tiles(2, body)

    gifts = {}

    def give(step):
        down(step, 1 - here.t, given)
        at = ns.at(step)
        gifts[step] = net.push(given.at[at], taken.at[at], "t")

    sums = RingSum(net, part, passed, plus, minus, mine, other, SUBS)
    outs = RingSum(net, part2, passed2, plus2, minus2, None, None, 1)
    term_o[...] = jnp.zeros_like(term_o)

    def back(step, side=None):
        at = sums.at(step)
        width = WIDTH // SUBS // (1 if side is None else 2)

        def body(j):
            cols = pl.ds(pl.multiple_of(j * (WIDTH // SUBS) + (side or 0) * width, width), width)
            rows = nt(dgu[at, :], w[cols, : 2 * FFD])
            part[at, cols] = rows.astype(BF16)
            term_o[:, cols] += jnp.sum(rows * n2[at, cols].astype(F32), 0, keepdims=True)

        tiles(SUBS, body)

    def keep(step):
        down(step, here.t, part2)

    def grad(i):
        turned = n2[:, span(i, 256)].T
        for j in range(4):
            w[span(i, 256), j * 512 : (j + 1) * 512] = nn(
                turned, dgu[:, j * 512 : (j + 1) * 512]
            ).astype(BF16)

    def grad_down(i):
        turned = c[:, span(i, 256)].T
        for j in range(2):
            dgrad[span(i, 256), j * 512 : (j + 1) * 512] = nn(
                turned, hid[:, j * 512 : (j + 1) * 512]
            ).astype(BF16)

    def take(step):
        gifts[step].wait_recv()
        at = ns.at(step)
        part2[at, :] = part2[at, :] + taken[at, :]

    pull(0)
    feed(0)
    ns.forward()
    give(0)
    pull(3)
    pull(1)
    c_far.wait_recv()
    pull(2)
    ns.left()
    feed(3)
    give(3)
    ns.right()
    feed(1)
    back(1, 1)
    back(3, 0)
    for i in range(SUBS):
        sums.raw(i)
    give(1)
    ns.far()
    feed(2)
    back(2)
    for i in range(SUBS):
        sums.far(i)
    give(2)
    back(1, 0)
    back(3, 1)
    tiles(8, grad_down)
    ds = ShardSum(net, dgrad, BLOCK, dgift, dpassed, dplus, dminus, None)
    sums.add(0)
    sums.add(1)
    back(0)
    sums.add(2)
    ds.pair(2, 1)
    ds.pair(2, 0)
    sums.add(3)
    keep(2)
    sums.cross(0)
    keep(1)
    keep(3)
    sums.cross(1)
    keep(0)
    take(2)
    outs.far(0)
    sums.cross(2)
    take(1)
    take(3)
    outs.raw(0)
    for dx in (1, 3):
        for dy in (1, 0):
            ds.pair(dx, dy)
    sums.cross(3)
    tiles(3, grad)
    ds.pass_on(1)
    ds.pass_on(0)
    outs.add(0)
    tiles(5, lambda i: grad(i + 3))
    saves = [net.copy(w.at[:, pl.ds(0, 2 * FFD)], grads_o)]
    ds.pair(0, 1)
    ds.pair(0, 0)
    take(0)
    for i in range(SUBS):
        sums.arrive(i)
    gain_two = gain_row(gains, 1)
    h_load.wait()
    hidden = h_in[...]
    upstream = mine[...].astype(F32) + other[...].astype(F32)
    factor = factor_of(hidden)
    weighted = upstream * gain_two
    inner = jnp.mean(weighted * hidden, -1, keepdims=True)
    dh = (
        c[ns.at(0), :].astype(F32) + factor * weighted - hidden * (factor * factor * factor) * inner
    )
    dh_o[...] = dh
    low_o[...] = dh.astype(BF16)
    term_o[...] = term_o[...] / gain_two
    outs.settle(0)
    mine_half = span(here.t, half)
    outh_o[...] = (
        h_in[:, mine_half]
        + part2[ns.at(0), :].astype(F32)
        + plus2[...].astype(F32)
        + minus2[...].astype(F32)
    ).astype(BF16)
    for dy in (0, 1):
        ds.close(dy, False)
        dsum_o[dy * BLOCK : (dy + 1) * BLOCK, :] = ds.kept(0, dy)[...]
    for copy in saves:
        copy.wait()
    net.drain()


def call_f(n2_in, h_in, fw, cf, gains):
    rows_b = pltpu.VMEM((TREE, WIDTH), BF16)
    half_b = pltpu.VMEM((TREE, WIDTH // 2), BF16)
    own_b = pltpu.VMEM((ROWS, WIDTH // 2), BF16)
    return pl.pallas_call(
        kernel_f,
        out_shape=[
            out((ROWS, WIDTH), F32), out((ROWS, WIDTH)), out((ROWS, WIDTH // 2)),
            out((2 * BLOCK, FFD)), out((1, WIDTH), F32), out((WIDTH, 2 * FFD)),
        ],
        in_specs=[VM, ANY, ANY, ANY, VM],
        out_specs=[VM, VM, VM, VM, VM, ANY],
        scratch_shapes=[
            pltpu.VMEM((WIDTH, 3 * FFD), BF16), rows_b, rows_b, rows_b,
            pltpu.VMEM((TREE, FFD), BF16), pltpu.VMEM((TREE, FFD), F32),
            pltpu.VMEM((ROWS, WIDTH), F32),
            rows_b, *ring_sum_scratch(),
            half_b, half_b, half_b, own_b, own_b, own_b,
            pltpu.VMEM((WIDTH, FFD), BF16), *shard_sum_scratch(BLOCK, FFD)[:-1],
            *near_sems(80, 16),
        ],
        compiler_params=params(1),
        name="feed",
    )(n2_in, h_in, fw, cf, gains)


def kernel_b(
    low_in, dh_any, tok_any, co_any, si_any, outh, gains, term_in, dsum,
    p_in, q_in, k_in, v_in, a_in, n1_in, aw_in, fgrads,
    dtok_o, out_o, gate_o, up_o, down_o, attn_o, gain_o,
    low, p, q, k, v, a, n1, aw, da, d, dk, dv, terms, gblk_f, ublk, ablk, gblk, gother, term, wgrad, dother,
    dh_in, tok, cosine, sine, turned_d,
    part, passed, plus, minus, mine, other,
    ggift, gpassed, gplus, gminus, glast, gheld,
    ugift, upassed, uplus, uminus, ulast, uheld,
    agift, apassed, aplus, aminus, alast,
    tgift, tpassed, tplus, tminus, tlast,
    send, recv, local,
):
    here = Place()
    net = Net(here, send, recv, local)
    net.greet(ALL_NEAR)
    ls = RingGather(net, low_in, low, True)
    loads = [
        net.copy(src, dst)
        for src, dst in (
            (aw_in, aw), (v_in, v), (p_in, p), (k_in, k), (q_in, q), (co_any, cosine),
            (si_any, sine), (a_in, a), (n1_in, n1), (dh_any, dh_in), (tok_any, tok),
        )
    ]
    gate = ShardSum(
        net, fgrads.at[:, pl.ds(0, FFD)], BLOCK, ggift, gpassed, gplus, gminus, glast, gheld
    )
    down_push = net.push(dsum.at[pl.ds(BLOCK, BLOCK)], dother, "y")
    my_half = span(here.t, WIDTH // 2)
    out_push = net.push(outh, out_o.at[:, my_half], "t")
    saves = [net.copy(outh, out_o.at[:, my_half])]
    low[ls.at(0), :] = low_in[...]

    def attended(step):
        at = ls.at(step)
        da[at, :] = nn(low[at, :], aw[:, 3 * HEAD : 4 * HEAD]).astype(BF16)

    def attend(step):
        at = ls.at(step)
        da_rows, probs = da[at, :], p[at, :]
        dp = nt(da_rows, v[...])
        ds = probs * (dp - jnp.sum(probs * dp, -1, keepdims=True))
        draw = (ds * (1.0 / math.sqrt(HEAD))).astype(BF16)
        first, second = turn(nn(draw, k[...]), cosine[at, :], -sine[at, :])
        d[at, :HALF] = first.astype(BF16)
        d[at, HALF:HEAD] = second.astype(BF16)
        dk_more, dv_more = tn(draw, q[at, :]), tn(probs.astype(BF16), da_rows)
        if step == 0:
            dk[...] = dk_more
            dv[...] = dv_more
        else:
            dk[...] += dk_more
            dv[...] += dv_more

    loads[0].wait()
    attended(0)
    gate.pair(2, 1)
    gate.pair(2, 0)
    ls.forward()
    up = ShardSum(
        net, fgrads.at[:, pl.ds(FFD, FFD)], BLOCK, ugift, upassed, uplus, uminus, ulast, uheld
    )
    for dx in (1, 3):
        for dy in (1, 0):
            gate.pair(dx, dy)
    for copy in loads[1:7]:
        copy.wait()
    attend(0)
    ls.share()
    down_push.wait_recv()
    turned_d[...] = (dother[...].astype(F32) + dsum[:BLOCK, :].astype(F32)).T.astype(BF16)
    dz = RingGather(net, turned_d, down_o)
    saves.append(net.copy(turned_d, down_o.at[dz.at(0)]))
    up.pair(2, 1)
    up.pair(2, 0)
    gate.pass_on(1)
    gate.pass_on(0)
    ls.left()
    attended(3)
    attend(3)
    for dx in (1, 3):
        for dy in (1, 0):
            up.pair(dx, dy)
    ls.right()
    attended(1)
    attend(1)
    gate.pair(0, 1)
    gate.pair(0, 0)
    dz.forward()
    ls.far()
    attended(2)
    attend(2)
    for copy in loads[7:]:
        copy.wait()
    first, second = turn(dk[...], cosine[...], -sine[...])
    d[:, HEAD : HEAD + HALF] = first.astype(BF16)
    d[:, HEAD + HALF : 2 * HEAD] = second.astype(BF16)
    d[:, 2 * HEAD :] = dv[...].astype(BF16)

    sums = RingSum(net, part, passed, plus, minus, mine, other, SUBS)
    term[...] = jnp.zeros_like(term)

    def back(step):
        at = sums.at(step)

        def body(j):
            cols = span(j, 512)
            rows = nt(d[at, :], aw[cols, : 3 * HEAD])
            part[at, cols] = rows.astype(BF16)
            term[:, cols] += jnp.sum(rows * n1[at, cols].astype(F32), 0, keepdims=True)

        tiles(4, body)

    def grad(i):
        turned = n1[:, span(i, 256)].T
        wgrad[span(i, 256), : 3 * HEAD] = nn(turned, d[...]).astype(BF16)
        turned = low[:, span(i, 256)].T
        wgrad[span(i, 256), 3 * HEAD :] = nn(turned, a[...]).astype(BF16)

    back(2)
    for i in range(SUBS):
        sums.far(i)
    gate.close(1)
    up.pass_on(1)
    tiles(8, grad)
    ws = ShardSum(net, wgrad, BLOCK, agift, apassed, aplus, aminus, alast)
    gate.close(0)
    up.pass_on(0)
    back(1)
    back(3)
    for i in range(SUBS):
        sums.raw(i)
        sums.add(i)
    for dx in (2, 1, 3):
        for dy in (1, 0):
            ws.pair(dx, dy)
    back(0)
    gain_one = gain_row(gains, 0)
    term_one = term[...] / gain_one
    term_two = term_in[...]
    row = lax.broadcasted_iota(jnp.int32, (GROWS, 128), 0)
    for s in range(16):
        cols = slice(s * 128, (s + 1) * 128)
        terms[s * GROWS : (s + 1) * GROWS, :] = jnp.where(
            row == 0, term_one[:, cols], jnp.where(row == 1, term_two[:, cols], 0.0)
        ).astype(BF16)
    ts = ShardSum(net, terms, GROWS, tgift, tpassed, tplus, tminus, tlast)
    up.pair(0, 1)
    up.pair(0, 0)
    up.close(1)
    for dx in (2, 1, 3):
        for dy in (1, 0):
            ts.pair(dx, dy)
    sums.cross(0)
    sums.cross(1)
    up.close(0)
    for shares in (ws, ts):
        for dy in (1, 0):
            shares.pair(0, dy)
    ublk[...] = up.result().astype(BF16)
    uz = RingGather(net, ublk, up_o)
    saves.append(net.copy(ublk, up_o.at[uz.at(0)]))
    sums.cross(2)
    for shares in (ws, ts):
        for dy in (1, 0):
            shares.pass_on(dy)
    sums.cross(3)
    gblk_f[...] = gate.result().astype(BF16)
    gz = RingGather(net, gblk_f, gate_o)
    saves.append(net.copy(gblk_f, gate_o.at[gz.at(0)]))
    uz.forward()
    gz.forward()
    for dy in (1, 0):
        for shares in (ws, ts):
            shares.close(dy)
    for i in range(SUBS):
        sums.arrive(i)
    inputs = tok[...].astype(F32)
    upstream = mine[...].astype(F32) + other[...].astype(F32)
    factor = factor_of(inputs)
    weighted = upstream * gain_one
    inner = jnp.mean(weighted * inputs, -1, keepdims=True)
    dtok_o[...] = (
        dh_in[...] + (factor * weighted - inputs * (factor * factor * factor) * inner)
    ).astype(BF16)
    gblk[...] = ts.result().astype(BF16)
    cross = net.push(gblk, gother, "t")
    ablk[...] = ws.result().astype(BF16)
    az = RingGather(net, ablk, attn_o)
    saves.append(net.copy(ablk, attn_o.at[az.at(0)]))
    cross.wait_recv()
    gother[...] = (gblk[...].astype(F32) + gother[...].astype(F32)).astype(BF16)
    tz = RingGather(net, gother, gain_o)
    saves.append(net.copy(gother, gain_o.at[tz.at(0)]))
    for shares in (az, tz):
        shares.forward()
    for shares in (dz, gz, uz, az, tz):
        shares.left()
        shares.right()
        shares.far()
    out_push.wait_recv()
    for copy in saves:
        copy.wait()
    net.drain()


def call_b(low, dh, tok, cosine, sine, outh, gains, term, dsum, *rest):
    rows_b = pltpu.VMEM((TREE, WIDTH), BF16)
    head_b = pltpu.VMEM((TREE, HEAD), BF16)
    head_f = pltpu.VMEM((TREE, HEAD), F32)
    ffn_b = pltpu.VMEM((BLOCK, FFD), BF16)
    held = pltpu.VMEM((8, BLOCK, FFD), BF16)
    gain_b = pltpu.VMEM((GROWS, 128), BF16)
    full = out((4 * BLOCK, FFD))
    return pl.pallas_call(
        kernel_b,
        out_shape=[
            out((ROWS, WIDTH)), out((ROWS, WIDTH)), full, full,
            out((4 * FFD, BLOCK)), full, out((4 * GROWS, 128)),
        ],
        in_specs=[VM] + [ANY] * 5 + [VM] * 3 + [ANY] * 8,
        out_specs=[VM] + [ANY] * 6,
        scratch_shapes=[
            rows_b, pltpu.VMEM((TREE, TREE), F32), head_b, head_b, head_b, head_b, rows_b,
            pltpu.VMEM((WIDTH, 4 * HEAD), BF16), head_b, pltpu.VMEM((TREE, 3 * HEAD), BF16),
            head_f, head_f,
            pltpu.VMEM((16 * GROWS, 128), BF16), ffn_b, ffn_b, ffn_b, gain_b, gain_b,
            pltpu.VMEM((1, WIDTH), F32), pltpu.VMEM((WIDTH, 4 * HEAD), BF16), ffn_b,
            pltpu.VMEM((ROWS, WIDTH), F32), pltpu.VMEM((ROWS, WIDTH), BF16),
            pltpu.VMEM((TREE, HALF), F32), pltpu.VMEM((TREE, HALF), F32),
            pltpu.VMEM((FFD, BLOCK), BF16),
            rows_b, *ring_sum_scratch(),
            *shard_sum_scratch(BLOCK, FFD), held,
            *shard_sum_scratch(BLOCK, FFD), held,
            *shard_sum_scratch(BLOCK, 4 * HEAD), *shard_sum_scratch(GROWS, 128),
            *near_sems(176, 48),
        ],
        compiler_params=params(2),
        name="attend_back",
    )(low, dh, tok, cosine, sine, outh, gains, term, dsum, *rest)


def kernel_e(
    gate, up, down, attn, gain, result, dtok, query_o, key_o, value_o, wout_o, gate_o, up_o, down_o,
    one_o, two_o, result_o, dtok_o,
):
    result_o[...] = result[...]
    dtok_o[...] = dtok[...]
    down_o[...] = down[...].astype(F32)
    for i in range(2):
        rows = slice(i * BLOCK, (i + 1) * BLOCK)
        gate_o[:, i * FFD : (i + 1) * FFD] = gate[rows, :].astype(F32)
        up_o[:, i * FFD : (i + 1) * FFD] = up[rows, :].astype(F32)
        query_o[:, i * HEAD : (i + 1) * HEAD] = attn[rows, :HEAD].astype(F32)
        wout_o[i * HEAD : (i + 1) * HEAD, :] = attn[rows, 3 * HEAD :].astype(F32).T
    pair = attn[:BLOCK, HEAD : 3 * HEAD].astype(F32) + attn[BLOCK:, HEAD : 3 * HEAD].astype(F32)
    key_o[...] = pair[:, :HEAD]
    value_o[...] = pair[:, HEAD:]
    gains = sum(gain[i * GROWS : i * GROWS + 16, :].astype(F32) for i in range(4))
    one_o[...] = gains[0:1]
    two_o[...] = gains[1:2]


def call_e(*blocks):
    def across(*shape):
        return pl.BlockSpec(shape, lambda i: (0, i))

    def along(*shape):
        return pl.BlockSpec(shape, lambda i: (i, 0))

    def fixed(*shape):
        return pl.BlockSpec(shape, lambda i: (0, 0))

    return pl.pallas_call(
        kernel_e,
        grid=(2,),
        out_shape=[
            out((BLOCK, 4 * HEAD), F32), out((BLOCK, 2 * HEAD), F32), out((BLOCK, 2 * HEAD), F32),
            out((4 * HEAD, BLOCK), F32), out((BLOCK, 4 * FFD), F32), out((BLOCK, 4 * FFD), F32),
            out((4 * FFD, BLOCK), F32), out((1, 128), F32), out((1, 128), F32),
            out((ROWS, WIDTH)), out((ROWS, WIDTH)),
        ],
        in_specs=[
            along(2 * BLOCK, FFD), along(2 * BLOCK, FFD), along(2 * FFD, BLOCK),
            along(2 * BLOCK, FFD), fixed(4 * GROWS, 128),
            along(ROWS // 2, WIDTH), along(ROWS // 2, WIDTH),
        ],
        out_specs=[
            across(BLOCK, 2 * HEAD), across(BLOCK, HEAD), across(BLOCK, HEAD),
            along(2 * HEAD, BLOCK), across(BLOCK, 2 * FFD), across(BLOCK, 2 * FFD),
            along(2 * FFD, BLOCK), fixed(1, 128), fixed(1, 128),
            along(ROWS // 2, WIDTH), along(ROWS // 2, WIDTH),
        ],
        compiler_params=pltpu.CompilerParams(vmem_limit_bytes=60 * 1024 * 1024),
        name="widen",
    )(*blocks)


def local(
    tokens, parents, gain_attn, w_query, key_weight, value_weight, w_out, gain_ffn, w_gate, w_up,
    w_down, cotangent,
):
    frequency = jnp.asarray(
        (THETA ** (-np.arange(HALF, dtype=np.float64) * 2.0 / HEAD)).astype(np.float32)[None, :]
    )
    n1, q, k, v, a, p, hidden, n2, cosine, sine, aw, gains, fw, cf = call_a(
        tokens, cotangent, parents, frequency, gain_attn.reshape(1, BLOCK),
        gain_ffn.reshape(1, BLOCK), w_query, key_weight, value_weight, w_out,
        w_gate, w_up, w_down,
    )
    dh, low, outh, dsum, term, fgrads = call_f(n2, hidden, fw, cf, gains)
    d_tokens, output, gate, up, down, attn, gain = call_b(
        low, dh, tokens, cosine, sine, outh, gains, term, dsum, p, q, k, v, a, n1, aw, fgrads
    )
    query, key, value, wout, gate, up, down, one, two, output, d_tokens = call_e(
        gate, up, down, attn, gain, output, d_tokens
    )
    return (
        output, d_tokens, one.reshape(128), query, key, value, wout, two.reshape(128), gate, up,
        down,
    )


def solution(mesh):
    rows = P(("shard", "ctx"), None)
    weight = P("shard", "tp")
    turned = P("tp", "shard")
    vector = P("shard")
    return jax.shard_map(
        local,
        mesh=mesh,
        in_specs=(
            rows, P("shard", None), vector, weight, weight, weight, turned, vector,
            weight, weight, turned, rows,
        ),
        out_specs=(
            rows, rows, vector, weight, weight, weight, turned, vector, weight, weight, turned,
        ),
        check_vma=False,
    )
```
